256 devices in a mesh: segment: 4 (over x_hi, core), lat: 64 (over y, x_lo, z).
Axes of the slice: x: 4 (x_hi: 2, x_lo: 2; x = x_hi * 2 + x_lo), y: 4, z: 8, core: 2. Of those that a mesh axis runs over, the one named last changes fastest.
Arguments:
- pixels: bfloat16 [4, 4, 5, 512, 128], P(None, None, None, 'lat'), may hold values from -6 to 6
- embed_weight: bfloat16 [80, 512], replicated, may hold values from -0.625 to 0.625
- level_code: bfloat16 [4, 512], replicated, may hold values from -6 to 6
- depth_kernel: bfloat16 [4, 2, 25, 512], P('segment'), may hold values from -1.25 to 1.25
- norm_gain: bfloat16 [4, 2, 512], P('segment'), may hold values from 0.099609375 to 1.8984375
- up_weight: bfloat16 [4, 2, 512, 1024], P('segment'), may hold values from -0.25 to 0.25
- up_bias: bfloat16 [4, 2, 1024], P('segment'), may hold values from -3 to 3
- down_weight: bfloat16 [4, 2, 1024, 512], P('segment'), may hold values from -0.1875 to 0.1875
- down_bias: bfloat16 [4, 2, 512], P('segment'), may hold values from -3 to 3
- fold_gain: bfloat16 [512], replicated, may hold values from 0.099609375 to 1.8984375
- latents: bfloat16 [3, 512], replicated, may hold values from -6 to 6
- memory_weight: bfloat16 [512, 1024], replicated, may hold values from -0.25 to 0.25
- output_weight: bfloat16 [512, 512], replicated, may hold values from -0.25 to 0.25
Outputs:
- latents_out: bfloat16 [4, 128, 32, 3, 512], P('segment', 'lat')
The draws below stay inside these ranges and needn't reach their ends.
All inputs are finite; a program needn't handle non-finite values.
Results may differ from the reference program's by a relative error of at most 0.014.
Values may be sent and summed in bfloat16 or wider, within the bound.
A program may use at most 64 MiB of HBM per device.

```python
import jax
import jax.numpy as jnp
from jax import lax

D = 512
HID = 1024
HEADS = 16
HSZ = 32
VARS = 5
PATCH = 4
LV = 4
NLAT = 3
BLOCKS = 2
COLS = 32
SECTIONS = 4
MICRO = 4
NR = 128


def level_of(own_key, dims, split, low, largest):
    level = 1.0
    for dim, blocks in split:
        heights = jax.random.uniform(jax.random.fold_in(jax.random.fold_in(own_key, 6), dim), (blocks,), jnp.float32, low / len(split), largest / len(split))
        level = level * jnp.repeat(jnp.exp(heights), dims[dim] // blocks).reshape((-1,) + (1,) * (len(dims) - 1 - dim))
    return level


def scatter_about(key, dims, spread, bound, cuts=(), dtype=jnp.bfloat16):
    entries = spread * jax.random.normal(key, dims, jnp.float32)
    if cuts:
        entries = entries * level_of(key, dims, cuts, -0.22, 0.18)
    return jnp.clip(entries, -bound, bound).astype(dtype)


def setup_inputs(seed: int = 0) -> dict:
    splits = jax.random.split(jax.random.key(seed), 14)
    pixels = scatter_about(splits[0], (MICRO, LV, VARS, NR * PATCH, COLS * PATCH), 1.0, 6.0, ((3, 64),))
    embed_weight = scatter_about(splits[1], (VARS * PATCH * PATCH, D), (VARS * PATCH * PATCH) ** -0.5, 0.625)
    level_code = scatter_about(splits[2], (LV, D), 1.0, 6.0)
    depth_kernel = scatter_about(splits[3], (SECTIONS, BLOCKS, 25, D), 25 ** -0.5, 1.25, ((0, 4),))
    norm_gain = jnp.clip(1.0 + 0.18 * jax.random.normal(splits[4], (SECTIONS, BLOCKS, D), jnp.float32), 0.099609375, 1.8984375).astype(jnp.bfloat16)
    up_weight = scatter_about(splits[5], (SECTIONS, BLOCKS, D, HID), D ** -0.5, 0.25, ((0, 4),))
    up_bias = scatter_about(splits[6], (SECTIONS, BLOCKS, HID), 0.5, 3.0, ((0, 4),))
    down_weight = scatter_about(splits[7], (SECTIONS, BLOCKS, HID, D), HID ** -0.5, 0.1875, ((0, 4),))
    down_bias = scatter_about(splits[8], (SECTIONS, BLOCKS, D), 0.5, 3.0, ((0, 4),))
    fold_gain = jnp.clip(1.0 + 0.18 * jax.random.normal(splits[9], (D,), jnp.float32), 0.099609375, 1.8984375).astype(jnp.bfloat16)
    latents = scatter_about(splits[10], (NLAT, D), 1.0, 6.0)
    memory_weight = scatter_about(splits[11], (D, 2 * D), D ** -0.5, 0.25)
    output_weight = scatter_about(splits[12], (D, D), D ** -0.5, 0.25)
    return {"pixels": pixels, "embed_weight": embed_weight, "level_code": level_code, "depth_kernel": depth_kernel, "norm_gain": norm_gain, "up_weight": up_weight, "up_bias": up_bias, "down_weight": down_weight, "down_bias": down_bias, "fold_gain": fold_gain, "latents": latents, "memory_weight": memory_weight, "output_weight": output_weight}


EPSILON = 1e-06

def normalize(values_in, gain):
    average = lax.optimization_barrier(jnp.mean(values_in, axis=-1, keepdims=True))
    centred = values_in - average
    spread_sq = lax.optimization_barrier(jnp.mean(centred * centred, axis=-1, keepdims=True))
    return centred * lax.rsqrt(spread_sq + EPSILON) * gain.astype(jnp.float32)

def depthwise(padded, kernel, row_count, col_count):
    conv_out = jnp.zeros((padded.shape[0], row_count, col_count, padded.shape[3]), jnp.float32)
    for row_off in range(5):
        for col_off in range(5):
            window = padded[:, row_off:row_off + row_count, col_off:col_off + col_count, :].astype(jnp.float32)
            conv_out = conv_out + window * kernel[row_off * 5 + col_off].astype(jnp.float32)
    return conv_out

def conv_block(features, padded_rows, kernel, gain, up_mat, up_shift, down_mat, down_shift):
    padded = jnp.pad(padded_rows, ((0, 0), (0, 0), (2, 2), (0, 0)))
    row_count = features.shape[1]
    col_count = features.shape[2]
    width = features.shape[3]
    conv_out = depthwise(padded, kernel, row_count, col_count)
    normed = normalize(conv_out, gain).astype(jnp.bfloat16)
    flat_rows = normed.reshape(-1, width)
    hidden = jax.nn.gelu(jnp.dot(flat_rows, up_mat, preferred_element_type=jnp.float32) + up_shift.astype(jnp.float32), approximate=False).astype(jnp.bfloat16)
    branch = jnp.dot(hidden, down_mat, preferred_element_type=jnp.float32) + down_shift.astype(jnp.float32)
    return (features.astype(jnp.float32) + branch.reshape(features.shape)).astype(jnp.bfloat16)

def embed_patches(sample_pixels, embed_weight, level_code):
    levels = sample_pixels.shape[0]
    variables = sample_pixels.shape[1]
    row_count = sample_pixels.shape[2] // PATCH
    col_count = sample_pixels.shape[3] // PATCH
    patches = sample_pixels.reshape(levels, variables, row_count, PATCH, col_count, PATCH)
    patches = patches.transpose(0, 2, 4, 1, 3, 5).reshape(levels * row_count * col_count, variables * PATCH * PATCH)
    embedded = jnp.dot(patches, embed_weight, preferred_element_type=jnp.float32).reshape(levels, row_count, col_count, -1)
    embedded = embedded + level_code[:, None, None, :].astype(jnp.float32)
    return embedded.astype(jnp.bfloat16)

def fold_levels(features, fold_gain, latents, memory_weight, output_weight):
    levels, row_count, col_count, width = features.shape
    places = row_count * col_count
    normed = normalize(features.astype(jnp.float32), fold_gain).astype(jnp.bfloat16).reshape(levels * places, width)
    keyval = jnp.dot(normed, memory_weight, preferred_element_type=jnp.float32).astype(jnp.bfloat16)
    keyval = keyval.reshape(levels, places, 2, HEADS, HSZ)
    queries = latents.reshape(NLAT, HEADS, HSZ).astype(jnp.float32)
    scores = jnp.einsum('lphe,qhe->pqlh', keyval[:, :, 0].astype(jnp.float32), queries) * HSZ ** (-0.5)
    raised = jnp.exp(scores)
    share = (raised / lax.optimization_barrier(jnp.sum(raised, axis=2, keepdims=True))).astype(jnp.bfloat16)
    mixed = jnp.einsum('pqlh,lphe->pqhe', share.astype(jnp.float32), keyval[:, :, 1].astype(jnp.float32))
    mixed = mixed.astype(jnp.bfloat16).reshape(places * NLAT, width)
    folded = jnp.dot(mixed, output_weight, preferred_element_type=jnp.float32).reshape(places, NLAT, width)
    folded = folded + latents.astype(jnp.float32)[None, :, :]
    return folded.astype(jnp.bfloat16).reshape(row_count, col_count, NLAT, width)

def reference(pixels, embed_weight, level_code, depth_kernel, norm_gain, up_weight, up_bias, down_weight, down_bias, fold_gain, latents, memory_weight, output_weight):

    def per_sample(sample_pixels):
        features = embed_patches(sample_pixels, embed_weight, level_code)
        for section_id in range(SECTIONS):
            for block_id in range(BLOCKS):
                padded_rows = jnp.pad(features, ((0, 0), (2, 2), (0, 0), (0, 0)))
                features = conv_block(features, padded_rows, depth_kernel[section_id, block_id], norm_gain[section_id, block_id], up_weight[section_id, block_id], up_bias[section_id, block_id], down_weight[section_id, block_id], down_bias[section_id, block_id])
        return fold_levels(features, fold_gain, latents, memory_weight, output_weight)
    return lax.map(per_sample, pixels)
```

```python
import functools

import jax
import jax.numpy as jnp
from jax import lax
from jax.experimental import pallas as pl
from jax.experimental.pallas import tpu as pltpu
from jax.sharding import PartitionSpec as P

MESH = pl.DeviceIdType.MESH
F32 = jnp.float32
BF16 = jnp.bfloat16
EPSILON = 1e-06
ROWS = 8
COLS = 32
WIDTH = 512
HIDDEN = 1024
NBLOCKS = 8
PLACES = ROWS * COLS
HEADS = 16
HSZ = 32
NLAT = 3
LEFT = 8


def dev(xh, xl, y, z, core):
    return (xh * 2 + core, y * 16 + xl * 8 + z)


def remote(src, dst, send, recv, target):
    return pltpu.make_async_remote_copy(
        src_ref=src, dst_ref=dst, send_sem=send, recv_sem=recv, device_id=target, device_id_type=MESH
    )


def normed_rows(x, gain):
    average = jnp.mean(x, axis=-1, keepdims=True)
    centred = x - average
    spread = jnp.mean(centred * centred, axis=-1, keepdims=True)
    return centred * lax.rsqrt(spread + EPSILON) * gain


def gelu(x):
    return 0.5 * x * (1.0 + lax.erf(x * (2.0**-0.5)))


def kernel(
    pixels, embed_weight, level_code, depth, gain, up, up_bias, down, down_bias,
    fold_gain, latents, memory_weight, output_weight,
    out,
    pix, pack, pack_f, upw, downw, memw, outw, feat, top, bottom, xpad, conv, hsum, gath, fold_in,
    pix_send, pix_recv, small_send, small_recv, own_load, sib_send, sib_recv,
    bnd_send, bnd_recv, fwd_send, fwd_recv, sibf_send, sibf_recv,
    halo_send, halo_recv, fin_send, fin_recv, misc,
):
    seg = lax.axis_index("segment")
    lat = lax.axis_index("lat")
    xh, core = seg // 2, seg % 2
    y, xl, z = lat // 16, (lat // 8) % 2, lat % 8
    band = 2 * z + core
    has_up, has_down = band > 0, band < 15

    sibling = dev(xh, xl, y, z, 1 - core)
    partner = dev(1 - xh, 1 - xl, y, z, core)
    ring = [
        dev(xh, xl, (y + 1) % 4, z, core),
        dev(xh, xl, (y + 3) % 4, z, core),
        dev(xh, 1 - xl, y, z, core),
    ]
    others = [((seg + k) % 4, lat) for k in (1, 2, 3)]
    up_band = jnp.maximum(band - 1, 0)
    down_band = jnp.minimum(band + 1, 15)
    above = dev(xh, xl, y, up_band // 2, up_band % 2)
    below = dev(xh, xl, y, down_band // 2, down_band % 2)
    src_band = lat // 4
    goes = [dev(xh, core, l, src_band // 2, src_band % 2) for l in range(4)]
    comes = [dev(xh, z % 2, z // 2, 4 * core + k, xl) for k in range(4)]

    def is_me(target):
        return (target[0] == seg) & (target[1] == lat)

    def not_me(target):
        return (target[0] != seg) | (target[1] != lat)

    barrier = pltpu.get_barrier_semaphore()

    def greet(target):
        pl.semaphore_signal(barrier, inc=1, device_id=target, device_id_type=MESH)

    for target in ring + [partner] + others:
        greet(target)
    expected = jnp.int32(7)
    for target in goes + comes:
        pl.when(not_me(target))(functools.partial(greet, target))
        expected = expected + not_me(target).astype(jnp.int32)
    pl.when(has_up)(functools.partial(greet, above))
    pl.when(has_down)(functools.partial(greet, below))
    expected = expected + has_up.astype(jnp.int32) + has_down.astype(jnp.int32)
    pl.semaphore_wait(barrier, expected)

    my_slot = lat % 4

    def pix_copy(l):
        return remote(pixels.at[seg, l], pix.at[my_slot], pix_send.at[l], pix_recv.at[my_slot], goes[l])

    def pix_local(l):
        return pltpu.make_async_copy(pixels.at[seg, l], pix.at[my_slot], pix_recv.at[my_slot])

    for l in range(4):
        pl.when(not_me(goes[l]))(lambda l=l: pix_copy(l).start())
        pl.when(is_me(goes[l]))(lambda l=l: pix_local(l).start())

    def pix_wait(k):
        remote(pixels.at[seg, 0], pix.at[k], pix_send.at[0], pix_recv.at[k], comes[k]).wait_recv()

    quarter_to = (y + 2 * (1 - xl)) % 4
    quarter = (y + 2 * xl) % 4
    mine = 2 * seg
    far = 2 * ((1 - xh) * 2 + core)
    far_sib = 2 * ((1 - xh) * 2 + (1 - core))
    sib_first = 2 * (xh * 2 + (1 - core))

    def store(ud):
        return (upw, downw)[ud]

    def given(ud):
        return (up, down)[ud]

    def span(ud, q):
        rows = (128, 256)[ud]
        return pl.ds(pl.multiple_of(q * rows, rows), rows)

    def own_copy(i, ud):
        return pltpu.make_async_copy(given(ud).at[0, i], store(ud).at[mine + i], own_load.at[i, ud])

    def sib_copy(i, ud):
        return remote(given(ud).at[0, i], store(ud).at[mine + i], sib_send.at[i, ud], sib_recv.at[i, ud], sibling)

    def sib_arrives(i, ud):
        remote(given(ud).at[0, i], store(ud).at[sib_first + i], sib_send.at[i, ud], sib_recv.at[i, ud], sibling).wait_recv()

    def bnd_copy(i, ud):
        return remote(
            given(ud).at[0, i, span(ud, quarter_to)],
            store(ud).at[mine + i, span(ud, quarter_to)],
            bnd_send.at[i, ud], bnd_recv.at[i, ud], partner,
        )

    def far_part(i, ud, q):
        return store(ud).at[far + i, span(ud, q)]

    def bnd_arrives(i, ud):
        part = far_part(i, ud, quarter)
        remote(part, part, bnd_send.at[i, ud], bnd_recv.at[i, ud], partner).wait_recv()

    def fwd_copy(i, ud, r):
        part = far_part(i, ud, quarter)
        return remote(part, part, fwd_send.at[i, ud, r], fwd_recv.at[i, ud, r], ring[r])

    def fwd_arrives(i, ud, r):
        part = far_part(i, ud, (quarter + (3, 1, 2)[r]) % 4)
        remote(part, part, fwd_send.at[i, ud, r], fwd_recv.at[i, ud, r], ring[r]).wait_recv()

    def sibf_copy(i, ud):
        whole = store(ud).at[far + i]
        return remote(whole, whole, sibf_send.at[i, ud], sibf_recv.at[i, ud], sibling)

    def sibf_arrives(i, ud):
        whole = store(ud).at[far_sib + i]
        remote(whole, whole, sibf_send.at[i, ud], sibf_recv.at[i, ud], sibling).wait_recv()

    def forward(i, ud):
        bnd_arrives(i, ud)
        for r in range(3):
            fwd_copy(i, ud, r).start()

    def hand_over(i, ud):
        for r in range(3):
            fwd_arrives(i, ud, r)
        sibf_copy(i, ud).start()

    def by_role(a0, a1, b0, b1):
        first = jnp.where(core == 0, a0, a1)
        second = jnp.where(core == 0, b0, b1)
        return jnp.where(xh == 0, first, second)

    pt_bnd = {
        (0, 0): by_role(-1, 2, -1, -1), (0, 1): by_role(-1, 2, -1, -1),
        (1, 0): by_role(-1, 2, -1, -1), (1, 1): by_role(-1, 2, -1, -1),
    }
    pt_fwd = {
        (0, 0): by_role(2, 3, 0, 3), (0, 1): by_role(2, 3, 0, 3),
        (1, 0): by_role(4, 5, 1, 4), (1, 1): by_role(4, 5, 2, 5),
    }
    pt_hand = {
        (0, 0): by_role(4, 5, 1, 4), (0, 1): by_role(4, 5, 1, 5),
        (1, 0): by_role(6, 7, 3, 6), (1, 1): by_role(6, 7, 3, 7),
    }
    KINDS = [(0, 0), (0, 1), (1, 0), (1, 1)]

    def service(point):
        for i, ud in KINDS:
            pl.when(pt_bnd[i, ud] == point)(lambda i=i, ud=ud: bnd_copy(i, ud).start())
        for i, ud in KINDS:
            pl.when(pt_fwd[i, ud] == point)(functools.partial(forward, i, ud))
        for i, ud in KINDS:
            pl.when(pt_hand[i, ud] == point)(functools.partial(hand_over, i, ud))

    service(-1)
    for i, ud in KINDS:
        own_copy(i, ud).start()
    for i, ud in KINDS:
        sib_copy(i, ud).start()
    load_mem = pltpu.make_async_copy(memory_weight, memw, misc.at[0])
    load_out = pltpu.make_async_copy(output_weight, outw, misc.at[1])
    load_mem.start()
    load_out.start()

    for i in range(2):
        pack_f[0:25] = depth[0, :, i, :].astype(F32)
        pack_f[25:26] = gain[0, i : i + 1, :].astype(F32)
        pack_f[26:27] = up_bias[0, i : i + 1, :WIDTH].astype(F32)
        pack_f[27:28] = up_bias[0, i : i + 1, WIDTH:].astype(F32)
        pack_f[28:29] = down_bias[0, i : i + 1, :].astype(F32)
        pack_f[29:32] = jnp.zeros((3, WIDTH), F32)
        pack[mine + i] = pack_f[...].astype(BF16)

    def small_copy(k):
        part = pack.at[pl.ds(mine, 2)]
        return remote(part, part, small_send.at[k], small_recv.at[k], others[k])

    def small_arrives(k):
        source = (seg + 3 - k) % 4
        part = pack.at[pl.ds(2 * source, 2)]
        remote(part, part, small_send.at[k], small_recv.at[k], others[k]).wait_recv()

    for k in range(3):
        small_copy(k).start()

    xpad[:, 0:LEFT, :] = jnp.zeros((ROWS + 4, LEFT, WIDTH), F32)
    xpad[:, LEFT + COLS :, :] = jnp.zeros((ROWS + 4, LEFT, WIDTH), F32)

    def equal(a, b):
        return jnp.where(a == b, 1.0, 0.0).astype(BF16)

    rho = lax.broadcasted_iota(jnp.int32, (128, 128), 0)
    lon = lax.broadcasted_iota(jnp.int32, (128, 128), 1)
    pick = equal(lon, 4 * (rho % 32) + rho // 32)
    row = lax.broadcasted_iota(jnp.int32, (40, 80), 0)
    col = lax.broadcasted_iota(jnp.int32, (40, 80), 1)
    source_col = ((row // 8) * 4 + row % 4) * 4
    half = (row // 4) % 2
    for k in range(4):
        pix_wait(k)
    for k in range(4):
        cells = pix[k].astype(F32).reshape(40, 128).astype(BF16)
        picked = lax.dot_general(pick, cells, (((1,), (1,)), ((), ())), preferred_element_type=F32)
        for j in range(4):
            gath[j, k * 32 : (k + 1) * 32, :] = picked[j * 32 : (j + 1) * 32, :]
    code = level_code[pl.ds(y, 1), 0, :].astype(F32)
    for r2 in range(2):
        total = jnp.zeros((128, WIDTH), F32)
        for j in range(4):
            choose = equal(jnp.where(half == r2, source_col + j, -1), col)
            part = jnp.dot(choose, embed_weight[...], preferred_element_type=F32).astype(BF16)
            total = total + jnp.dot(gath[j].astype(BF16), part, preferred_element_type=F32)
        total = (total + code).astype(BF16)
        for k in range(4):
            piece = total[k * 32 : (k + 1) * 32, :]
            start = (2 * k + r2) * 32
            feat[0, start : start + 32, :] = piece
            xpad[2 + 2 * k + r2, LEFT : LEFT + COLS, :] = piece.astype(F32)

    def halo_up(h, slot):
        return remote(feat.at[slot, pl.ds(0, 64)], bottom.at[h], halo_send.at[0, h], halo_recv.at[0, h], above)

    def halo_down(h, slot):
        return remote(feat.at[slot, pl.ds(PLACES - 64, 64)], top.at[h], halo_send.at[1, h], halo_recv.at[1, h], below)

    def send_halos(h, slot):
        pl.when(has_up)(lambda: halo_up(h, slot).start())
        pl.when(has_down)(lambda: halo_down(h, slot).start())

    def halos_sent(h, slot):
        pl.when(has_up)(lambda: halo_up(h, slot).wait_send())
        pl.when(has_down)(lambda: halo_down(h, slot).wait_send())

    send_halos(0, 0)

    @pl.when(jnp.logical_not(has_up))
    def _():
        xpad[0:2, LEFT : LEFT + COLS, :] = jnp.zeros((2, COLS, WIDTH), F32)

    @pl.when(jnp.logical_not(has_down))
    def _():
        xpad[ROWS + 2 :, LEFT : LEFT + COLS, :] = jnp.zeros((2, COLS, WIDTH), F32)

    for k in range(3):
        small_arrives(k)

    def conv_rows(first, count):
        def lanes(t, _):
            at = pl.ds(pl.multiple_of(t * 128, 128), 128)
            acc = jnp.zeros((count, COLS, 128), F32)
            for j in range(5):
                window = xpad[first : first + count + 4, LEFT - 2 + j : LEFT - 2 + j + COLS, at]
                for i in range(5):
                    acc = acc + window[i : i + count] * pack_f[5 * i + j : 5 * i + j + 1, at][None]
            conv[first * COLS : (first + count) * COLS, at] = acc.reshape(count * COLS, 128)
            return 0

        lax.fori_loop(0, WIDTH // 128, lanes, 0)

    def block(b, _):
        slot = b % 2
        other = 1 - slot
        service(2 * b)
        pack_f[...] = pack[b].astype(F32)
        conv_rows(2, 4)

        @pl.when(has_up)
        def _():
            halo_down(b, slot).wait_recv()
            xpad[0:2, LEFT : LEFT + COLS, :] = top[b].astype(F32).reshape(2, COLS, WIDTH)

        @pl.when(has_down)
        def _():
            halo_up(b, slot).wait_recv()
            xpad[ROWS + 2 :, LEFT : LEFT + COLS, :] = bottom[b].astype(F32).reshape(2, COLS, WIDTH)

        conv_rows(0, 2)
        conv_rows(6, 2)
        service(2 * b + 1)
        section, i = b // 2, b % 2

        def settle(test, arrives):
            for n in range(2):
                for ud in range(2):
                    pl.when(test & (i == n))(functools.partial(arrives, n, ud))

        near = section // 2 == xh
        same = section % 2 == core
        settle(near & same, lambda n, ud: own_copy(n, ud).wait())
        settle(near & jnp.logical_not(same), sib_arrives)
        settle(jnp.logical_not(near) & jnp.logical_not(same), sibf_arrives)

        normed = normed_rows(conv[...], pack_f[25:26, :]).astype(BF16)
        for n in range(4):
            at = pl.ds(n * 256, 256)
            bias = pack_f[26 + n // 2 : 27 + n // 2, (n % 2) * 256 : (n % 2) * 256 + 256]
            hidden = gelu(jnp.dot(normed, upw[b, :, at], preferred_element_type=F32) + bias).astype(BF16)
            part = jnp.dot(hidden, downw[b, at, :], preferred_element_type=F32)
            if n == 0:
                hsum[...] = part
            else:
                hsum[...] += part

        @pl.when(b > 0)
        def _():
            halos_sent(b - 1, other)

        old = xpad[2 : 2 + ROWS, LEFT : LEFT + COLS, :].reshape(PLACES, WIDTH)
        new = (old + (hsum[...] + pack_f[28:29, :])).astype(BF16)
        feat[other] = new
        xpad[2 : 2 + ROWS, LEFT : LEFT + COLS, :] = new.astype(F32).reshape(ROWS, COLS, WIDTH)

        @pl.when(b < NBLOCKS - 1)
        def _():
            send_halos(b + 1, other)

        return 0

    lax.fori_loop(0, NBLOCKS, block, 0)

    def fin_copy(k):
        return remote(feat.at[0, pl.ds(64 * k, 64)], fold_in.at[y], fin_send.at[k], fin_recv.at[y], comes[k])

    def fin_local(k):
        return pltpu.make_async_copy(feat.at[0, pl.ds(64 * k, 64)], fold_in.at[y], fin_recv.at[y])

    for k in range(4):
        pl.when(not_me(comes[k]))(lambda k=k: fin_copy(k).start())
        pl.when(is_me(comes[k]))(lambda k=k: fin_local(k).start())

    for l in range(4):
        pl.when(not_me(goes[l]))(lambda l=l: pix_copy(l).wait_send())
    for k in range(3):
        small_copy(k).wait_send()
    for i, ud in KINDS:
        sib_copy(i, ud).wait_send()
        bnd_copy(i, ud).wait_send()
        sibf_copy(i, ud).wait_send()
        for r in range(3):
            fwd_copy(i, ud, r).wait_send()
    halos_sent(NBLOCKS - 1, 1)
    load_mem.wait()
    load_out.wait()

    lane = lax.broadcasted_iota(jnp.int32, (8, 128), 1)
    query = lax.broadcasted_iota(jnp.int32, (8, 128), 0)
    heads_of = equal(jnp.where(lane < HEADS * NLAT, lane // HEADS, -1), query)
    lat_f = jnp.concatenate([latents[...].astype(F32), jnp.zeros((5, WIDTH), F32)], axis=0)
    spread = jnp.dot(lat_f.T.astype(BF16), heads_of, preferred_element_type=F32)
    d_row = lax.broadcasted_iota(jnp.int32, (WIDTH, 128), 0)
    d_lane = lax.broadcasted_iota(jnp.int32, (WIDTH, 128), 1)
    queries = jnp.where(d_row // HSZ == d_lane % HEADS, spread, 0.0).astype(BF16)
    e_row = lax.broadcasted_iota(jnp.int32, (128, WIDTH), 0)
    e_lane = lax.broadcasted_iota(jnp.int32, (128, WIDTH), 1)

    for l in range(4):
        remote(feat.at[0, pl.ds(0, 64)], fold_in.at[l], fin_send.at[0], fin_recv.at[l], goes[l]).wait_recv()

    memory = normed_rows(
        fold_in[...].astype(F32).reshape(PLACES, WIDTH), fold_gain[...].astype(F32)
    ).astype(BF16)
    keys = jnp.dot(memory, memw[:, :WIDTH], preferred_element_type=F32).astype(BF16)
    values = jnp.dot(memory, memw[:, WIDTH:], preferred_element_type=F32).astype(BF16).astype(F32)
    raised = jnp.exp(jnp.dot(keys, queries, preferred_element_type=F32) * HSZ ** (-0.5))
    raised = raised.reshape(4, 64, 128)
    share = (raised / jnp.sum(raised, axis=0, keepdims=True)).astype(BF16).reshape(PLACES, 128)
    for q in range(NLAT):
        widen = equal(e_row, q * HEADS + e_lane // HSZ)
        wide = jnp.dot(share, widen, preferred_element_type=F32)
        mixed = jnp.sum((wide * values).reshape(4, 64, WIDTH), axis=0).astype(BF16)
        folded = jnp.dot(mixed, outw[...], preferred_element_type=F32) + lat_f[q : q + 1, :]
        folded = folded.astype(BF16)
        for r in range(2):
            out[0, r, q] = folded[r * 32 : (r + 1) * 32, :]

    for l in range(4):
        pass
    for k in range(4):
        pl.when(not_me(comes[k]))(lambda k=k: fin_copy(k).wait_send())


def on_device(
    pixels, embed_weight, level_code, depth_kernel, norm_gain, up_weight, up_bias,
    down_weight, down_bias, fold_gain, latents, memory_weight, output_weight,
):
    vmem = pl.BlockSpec(memory_space=pltpu.VMEM)
    hbm = pl.BlockSpec(memory_space=pl.ANY)
    dma = pltpu.SemaphoreType.DMA
    result = pl.pallas_call(
        kernel,
        out_shape=jax.ShapeDtypeStruct((1, 2, NLAT, COLS, WIDTH), BF16),
        in_specs=[hbm, vmem, vmem, vmem, vmem, hbm, vmem, hbm, vmem, vmem, vmem, hbm, hbm],
        out_specs=vmem,
        scratch_shapes=[
            pltpu.VMEM((4, 5, 8, 128), BF16),
            pltpu.VMEM((NBLOCKS, 32, WIDTH), BF16),
            pltpu.VMEM((32, WIDTH), F32),
            pltpu.VMEM((NBLOCKS, WIDTH, HIDDEN), BF16),
            pltpu.VMEM((NBLOCKS, HIDDEN, WIDTH), BF16),
            pltpu.VMEM((WIDTH, 2 * WIDTH), BF16),
            pltpu.VMEM((WIDTH, WIDTH), BF16),
            pltpu.VMEM((2, PLACES, WIDTH), BF16),
            pltpu.VMEM((NBLOCKS, 64, WIDTH), BF16),
            pltpu.VMEM((NBLOCKS, 64, WIDTH), BF16),
            pltpu.VMEM((ROWS + 4, COLS + 2 * LEFT, WIDTH), F32),
            pltpu.VMEM((PLACES, WIDTH), F32),
            pltpu.VMEM((PLACES, WIDTH), F32),
            pltpu.VMEM((4, 128, 40), F32),
            pltpu.VMEM((4, 64, WIDTH), BF16),
            dma((4,)), dma((4,)), dma((3,)), dma((3,)), dma((2, 2)), dma((2, 2)), dma((2, 2)),
            dma((2, 2)), dma((2, 2)), dma((2, 2, 3)), dma((2, 2, 3)), dma((2, 2)), dma((2, 2)),
            dma((2, NBLOCKS)), dma((2, NBLOCKS)), dma((4,)), dma((4,)), dma((2,)),
        ],
        compiler_params=pltpu.CompilerParams(
            collective_id=0, has_side_effects=True, vmem_limit_bytes=48 * 1024 * 1024
        ),
    )(
        pixels, embed_weight, level_code[:, None, :], jnp.transpose(depth_kernel, (0, 2, 1, 3)),
        norm_gain, up_weight, up_bias, down_weight, down_bias, fold_gain[None, :], latents,
        memory_weight, output_weight,
    )
    return jnp.transpose(result, (0, 1, 3, 2, 4))


def solution(mesh):
    return jax.shard_map(
        on_device,
        mesh=mesh,
        in_specs=(
            P(None, None, None, "lat", None),
            P(),
            P(),
            P("segment", None, None, None),
            P("segment", None, None),
            P("segment", None, None, None),
            P("segment", None, None),
            P("segment", None, None, None),
            P("segment", None, None),
            P(),
            P(),
            P(),
            P(),
        ),
        out_specs=P("segment", "lat", None, None, None),
        check_vma=False,
    )
```

```python
import functools

import jax
import jax.numpy as jnp
from jax import lax
from jax.experimental import pallas as pl
from jax.experimental.pallas import tpu as pltpu
from jax.sharding import PartitionSpec as P

MESH = pl.DeviceIdType.MESH
F32 = jnp.float32
BF16 = jnp.bfloat16
EPSILON = 1e-06
ROWS = 8
COLS = 32
WIDTH = 512
HIDDEN = 1024
NBLOCKS = 8
PLACES = ROWS * COLS
HEADS = 16
HSZ = 32
NLAT = 3
PIECE = (0, 128, 192, 64)
ROW_AT = (0, 32, 128, 160, 192, 224, 64, 96)
MIRROR = 11


def dev(xh, xl, y, z, core):
    return (xh * 2 + core, y * 16 + xl * 8 + z)


def remote(src, dst, send, recv, target):
    return pltpu.make_async_remote_copy(
        src_ref=src, dst_ref=dst, send_sem=send, recv_sem=recv, device_id=target, device_id_type=MESH
    )


def normed_rows(x, gain):
    average = jnp.mean(x, axis=-1, keepdims=True)
    centred = x - average
    spread = jnp.mean(centred * centred, axis=-1, keepdims=True)
    return centred * lax.rsqrt(spread + EPSILON) * gain


def gelu(x):
    return 0.5 * x * (1.0 + lax.erf(x * (2.0**-0.5)))


def kernel(
    pixels, embed_weight, level_code, depth, gain, up, up_bias, down, down_bias,
    fold_gain, latents, memory_weight, output_weight,
    out,
    embw, codes, taps, gains, up_shift, down_shift, fold_scale, lats,
    pix, pack, pack_f, upw, downw, memw, outw, feat, top, bottom, padded, taps8, conv8, conv, hsum, gath, fold_in,
    pix_send, pix_recv, small_send, small_recv, own_load, sib_send, sib_recv,
    bnd_send, bnd_recv, fwd_send, fwd_recv, sibf_send, sibf_recv,
    halo_send, halo_recv, fin_send, fin_recv, misc, load_sem,
):
    loads = [
        pltpu.make_async_copy(source, target, load_sem.at[n])
        for n, (source, target) in enumerate(
            (
                (depth, taps), (gain, gains), (up_bias, up_shift), (down_bias, down_shift),
                (embed_weight, embw), (level_code, codes), (fold_gain, fold_scale), (latents, lats),
            )
        )
    ]
    for load in loads:
        load.start()
    seg = lax.axis_index("segment")
    lat = lax.axis_index("lat")
    xh, core = seg // 2, seg % 2
    y, xl, z = lat // 16, (lat // 8) % 2, lat % 8
    level, chip = z % 4, 2 * y + xl
    band = 2 * chip + core
    has_up, has_down = band > 0, band < 15

    sibling = dev(xh, xl, y, z, 1 - core)
    partner = dev(1 - xh, 1 - xl, y, z, core)
    crossed = dev(1 - xh, 1 - xl, y, z, 1 - core)
    ring = [
        dev(xh, xl, y, (z + 1) % 8, core),
        dev(xh, xl, y, (z + 7) % 8, core),
        dev(xh, xl, y + 1 - 2 * (y % 2), z, core),
    ]
    others = [sibling, partner, crossed]
    up_band = jnp.maximum(band - 1, 0)
    down_band = jnp.minimum(band + 1, 15)
    above = dev(xh, (up_band // 2) % 2, up_band // 4, z, up_band % 2)
    below = dev(xh, (down_band // 2) % 2, down_band // 4, z, down_band % 2)
    goes = [dev(xh, xl, y, core * 4 + l, z // 4) for l in range(4)]
    comes = [dev(xh, xl, y, core * 4 + k, z // 4) for k in range(4)]

    def is_me(target):
        return (target[0] == seg) & (target[1] == lat)

    def not_me(target):
        return (target[0] != seg) | (target[1] != lat)

    barrier = pltpu.get_barrier_semaphore()

    def greet(target):
        pl.semaphore_signal(barrier, inc=1, device_id=target, device_id_type=MESH)

    for target in ring + others:
        greet(target)
    expected = jnp.int32(6)
    for target in goes + comes:
        pl.when(not_me(target))(functools.partial(greet, target))
        expected = expected + not_me(target).astype(jnp.int32)
    pl.when(has_up)(functools.partial(greet, above))
    pl.when(has_down)(functools.partial(greet, below))
    expected = expected + has_up.astype(jnp.int32) + has_down.astype(jnp.int32)
    pl.semaphore_wait(barrier, expected)

    my_slot = lat % 4

    def pix_copy(l):
        return remote(pixels.at[seg, l], pix.at[my_slot], pix_send.at[l], pix_recv.at[my_slot], goes[l])

    def pix_local(l):
        return pltpu.make_async_copy(pixels.at[seg, l], pix.at[my_slot], pix_recv.at[my_slot])

    for l in range(4):
        pl.when(not_me(goes[l]))(lambda l=l: pix_copy(l).start())
        pl.when(is_me(goes[l]))(lambda l=l: pix_local(l).start())

    def pix_wait(k):
        remote(pixels.at[seg, 0], pix.at[k], pix_send.at[0], pix_recv.at[k], comes[k]).wait_recv()

    quarter = (z + 2 * (y % 2)) % 4
    mine = 2 * seg
    far = 2 * ((1 - xh) * 2 + core)
    far_sib = 2 * ((1 - xh) * 2 + (1 - core))
    sib_first = 2 * (xh * 2 + (1 - core))

    def store(ud):
        return (upw, downw)[ud]

    def given(ud):
        return (up, down)[ud]

    def span(ud, q):
        rows = (128, 256)[ud]
        return pl.ds(pl.multiple_of(q * rows, rows), rows)

    def own_copy(i, ud):
        return pltpu.make_async_copy(given(ud).at[0, i], store(ud).at[mine + i], own_load.at[i, ud])

    def sib_copy(i, ud):
        return remote(given(ud).at[0, i], store(ud).at[mine + i], sib_send.at[i, ud], sib_recv.at[i, ud], sibling)

    def sib_arrives(i, ud):
        remote(given(ud).at[0, i], store(ud).at[sib_first + i], sib_send.at[i, ud], sib_recv.at[i, ud], sibling).wait_recv()

    def bnd_copy(i, ud):
        return remote(
            given(ud).at[0, i, span(ud, quarter)],
            store(ud).at[mine + i, span(ud, quarter)],
            bnd_send.at[i, ud], bnd_recv.at[i, ud], partner,
        )

    def far_part(i, ud, q):
        return store(ud).at[far + i, span(ud, q)]

    def bnd_arrives(i, ud):
        part = far_part(i, ud, quarter)
        remote(part, part, bnd_send.at[i, ud], bnd_recv.at[i, ud], partner).wait_recv()

    def fwd_copy(i, ud, r):
        part = far_part(i, ud, quarter)
        return remote(part, part, fwd_send.at[i, ud, r], fwd_recv.at[i, ud, r], ring[r])

    def fwd_arrives(i, ud, r):
        part = far_part(i, ud, (quarter + (3, 1, 2)[r]) % 4)
        remote(part, part, fwd_send.at[i, ud, r], fwd_recv.at[i, ud, r], ring[r]).wait_recv()

    def sibf_copy(i, ud):
        whole = store(ud).at[far + i]
        return remote(whole, whole, sibf_send.at[i, ud], sibf_recv.at[i, ud], sibling)

    def sibf_arrives(i, ud):
        whole = store(ud).at[far_sib + i]
        remote(whole, whole, sibf_send.at[i, ud], sibf_recv.at[i, ud], sibling).wait_recv()

    def forward(i, ud):
        bnd_arrives(i, ud)
        for r in range(3):
            fwd_copy(i, ud, r).start()

    def hand_over(i, ud):
        for r in range(3):
            fwd_arrives(i, ud, r)
        sibf_copy(i, ud).start()

    def by_role(a0, a1, b0, b1):
        first = jnp.where(core == 0, a0, a1)
        second = jnp.where(core == 0, b0, b1)
        return jnp.where(xh == 0, first, second)

    def when(block, step):
        return 3 * block + step

    pt_bnd = {}
    for n in range(2):
        for ud in range(2):
            pt_bnd[n, ud] = by_role(-1, when(1, 0), -1, when(1, 0))
    pt_fwd = {
        (0, 0): by_role(when(1, 0), when(4, 0), when(0, 0), when(0, 2)),
        (0, 1): by_role(when(1, 0), when(4, 0), when(0, 0), when(1, 0)),
        (1, 0): by_role(when(2, 0), when(5, 0), when(0, 1), when(1, 2)),
        (1, 1): by_role(when(2, 0), when(5, 0), when(0, 2), when(2, 0)),
    }
    pt_hand = {
        (0, 0): by_role(when(2, 0), when(5, 0), when(0, 1), when(1, 1)),
        (0, 1): by_role(when(2, 0), when(5, 0), when(0, 1), when(1, 2)),
        (1, 0): by_role(when(3, 0), when(6, 0), when(1, 1), when(2, 1)),
        (1, 1): by_role(when(3, 0), when(6, 0), when(1, 1), when(2, 2)),
    }
    pt_sib = {
        (0, 0): by_role(-1, -1, when(2, 2), when(2, 2)), (0, 1): by_role(-1, -1, when(2, 2), when(2, 2)),
        (1, 0): by_role(1, 1, when(3, 0), when(3, 0)), (1, 1): by_role(1, 1, when(3, 0), when(3, 0)),
    }
    KINDS = [(0, 0), (0, 1), (1, 0), (1, 1)]

    def service(point):
        for i, ud in KINDS:
            pl.when(pt_sib[i, ud] == point)(lambda i=i, ud=ud: sib_copy(i, ud).start())
        for i, ud in KINDS:
            pl.when(pt_bnd[i, ud] == point)(lambda i=i, ud=ud: bnd_copy(i, ud).start())
        for i, ud in KINDS:
            pl.when(pt_fwd[i, ud] == point)(functools.partial(forward, i, ud))
        for i, ud in KINDS:
            pl.when(pt_hand[i, ud] == point)(functools.partial(hand_over, i, ud))

    for i, ud in KINDS:
        own_copy(i, ud).start()
    load_mem = pltpu.make_async_copy(memory_weight, memw, misc.at[0])
    load_out = pltpu.make_async_copy(output_weight, outw, misc.at[1])
    load_mem.start()
    load_out.start()

    for load in loads:
        load.wait()
    for i in range(2):
        pack_f[0:25] = taps[0, :, i, :].astype(F32)
        pack_f[25:26] = gains[0, i : i + 1, :].astype(F32)
        pack_f[26:27] = up_shift[0, i : i + 1, :WIDTH].astype(F32)
        pack_f[27:28] = up_shift[0, i : i + 1, WIDTH:].astype(F32)
        pack_f[28:29] = down_shift[0, i : i + 1, :].astype(F32)
        pack_f[29:32] = jnp.zeros((3, WIDTH), F32)
        pack[mine + i] = pack_f[...].astype(BF16)

    def small_copy(k):
        part = pack.at[pl.ds(mine, 2)]
        return remote(part, part, small_send.at[k], small_recv.at[k], others[k])

    def small_from(k):
        return (xh * 2 + (1 - core), (1 - xh) * 2 + core, (1 - xh) * 2 + (1 - core))[k]

    def small_arrives(k):
        part = pack.at[pl.ds(2 * small_from(k), 2)]
        remote(part, part, small_send.at[k], small_recv.at[k], others[k]).wait_recv()

    for k in range(3):
        small_copy(k).start()
    service(-1)

    grid4 = padded.reshape(8, COLS + 4, 8, 128)
    grid4[:, 0:2] = jnp.zeros((8, 2, 8, 128), F32)
    grid4[:, COLS + 2 :] = jnp.zeros((8, 2, 8, 128), F32)

    def place(padded_row, values):
        for flip in range(2):
            p = MIRROR - padded_row if flip else padded_row
            if p < 8:
                for c in range(0, COLS, 8):
                    for g in range(4):
                        start = (p * (COLS + 4) + 2 + c) * 8 + flip * 4 + g
                        padded[pl.ds(start, 8, stride=8), :] = values[c : c + 8, g * 128 : g * 128 + 128]

    def equal(a, b):
        return jnp.where(a == b, 1.0, 0.0).astype(BF16)

    rho = lax.broadcasted_iota(jnp.int32, (128, 128), 0)
    lon = lax.broadcasted_iota(jnp.int32, (128, 128), 1)
    pick = equal(lon, 4 * (rho % 32) + rho // 32)
    row = lax.broadcasted_iota(jnp.int32, (40, 80), 0)
    col = lax.broadcasted_iota(jnp.int32, (40, 80), 1)
    source_col = ((row // 8) * 4 + row % 4) * 4
    half = (row // 4) % 2
    for k in range(4):
        pix_wait(k)
    for k in range(4):
        cells = pix[k].astype(F32).reshape(40, 128).astype(BF16)
        picked = lax.dot_general(pick, cells, (((1,), (1,)), ((), ())), preferred_element_type=F32)
        for j in range(4):
            gath[j, k * 32 : (k + 1) * 32, :] = picked[j * 32 : (j + 1) * 32, :]
    level_row = lax.broadcasted_iota(jnp.int32, (4, WIDTH), 0)
    code = jnp.sum(jnp.where(level_row == level, codes[...].astype(F32), 0.0), axis=0, keepdims=True)
    for r2 in range(2):
        total = jnp.zeros((128, WIDTH), F32)
        for j in range(4):
            choose = equal(jnp.where(half == r2, source_col + j, -1), col)
            part = jnp.dot(choose, embw[...], preferred_element_type=F32).astype(BF16)
            total = total + jnp.dot(gath[j].astype(BF16), part, preferred_element_type=F32)
        total = (total + code).astype(BF16)
        for k in range(4):
            piece = total[k * 32 : (k + 1) * 32, :]
            start = PIECE[k] + r2 * 32
            feat[0, start : start + 32, :] = piece
            place(2 + 2 * k + r2, piece.astype(F32))

    def halo_up(h, slot):
        return remote(feat.at[slot, pl.ds(0, 64)], bottom.at[h], halo_send.at[0, h], halo_recv.at[0, h], above)

    def halo_down(h, slot):
        return remote(feat.at[slot, pl.ds(64, 64)], top.at[h], halo_send.at[1, h], halo_recv.at[1, h], below)

    def send_halos(h, slot):
        pl.when(has_up)(lambda: halo_up(h, slot).start())
        pl.when(has_down)(lambda: halo_down(h, slot).start())

    def halos_sent(h, slot):
        pl.when(has_up)(lambda: halo_up(h, slot).wait_send())
        pl.when(has_down)(lambda: halo_down(h, slot).wait_send())

    send_halos(0, 0)

    @pl.when(jnp.logical_not(has_up))
    def _():
        for r in range(2):
            place(r, jnp.zeros((COLS, WIDTH), F32))

    @pl.when(jnp.logical_not(has_down))
    def _():
        for r in range(2):
            place(ROWS + 2 + r, jnp.zeros((COLS, WIDTH), F32))

    def conv_rows(first):
        def columns(step, _):
            base = step * 8
            sums = [[None] * 8 for _ in range(2)]
            for p in range(first, first + 6):
                for c in range(12):
                    value = padded[pl.ds(pl.multiple_of((p * (COLS + 4) + c) * 8 + base * 8, 8), 8), :]
                    for r in range(2):
                        i = p - first - r
                        for j in range(5):
                            if 0 <= i < 5 and 0 <= c - j < 8:
                                term = value * taps8[8 * (5 * i + j) : 8 * (5 * i + j) + 8, :]
                                old = sums[r][c - j]
                                sums[r][c - j] = term if old is None else old + term
            for r in range(2):
                for q in range(8):
                    at = pl.multiple_of(((first + r) * COLS + q) * 8 + base * 8, 8)
                    conv8[pl.ds(at, 8), :] = sums[r][q]
            return 0

        lax.fori_loop(0, COLS // 8, columns, 0)
        for r in (first, first + 1, 7 - first, 6 - first):
            flip = r > 3
            line = 7 - r if flip else r
            for c in range(0, COLS, 8):
                for g in range(4):
                    start = (line * COLS + c) * 8 + flip * 4 + g
                    at = ROW_AT[r] + c
                    conv[at : at + 8, g * 128 : g * 128 + 128] = conv8[pl.ds(start, 8, stride=8), :]

    def fin_copy(k):
        source = feat.at[0, pl.ds(PIECE[k], 64)]
        return remote(source, fold_in.at[level], fin_send.at[k], fin_recv.at[level], comes[k])

    def fin_local(k):
        source = feat.at[0, pl.ds(PIECE[k], 64)]
        return pltpu.make_async_copy(source, fold_in.at[level], fin_recv.at[level])

    def finish(k):
        pl.when(not_me(comes[k]))(lambda: fin_copy(k).start())
        pl.when(is_me(comes[k]))(lambda: fin_local(k).start())

    def block(b, _):
        slot = b % 2
        other = 1 - slot
        section, i = b // 2, b % 2
        service(3 * b)
        for k in range(3):
            pl.when((i == 0) & (section == small_from(k)))(functools.partial(small_arrives, k))
        pack_f[...] = pack[b].astype(F32)
        for n in range(5):
            for g in range(4):
                five = pack_f[5 * n : 5 * n + 5, g * 128 : g * 128 + 128]
                taps8[pl.ds(40 * n + g, 5, stride=8), :] = five
                taps8[pl.ds(40 * (4 - n) + 4 + g, 5, stride=8), :] = five
        conv_rows(2)

        @pl.when(has_up)
        def _():
            halo_down(b, slot).wait_recv()
            for r in range(2):
                place(r, top[b, r * 32 : r * 32 + 32, :].astype(F32))

        @pl.when(has_down)
        def _():
            halo_up(b, slot).wait_recv()
            for r in range(2):
                place(ROWS + 2 + r, bottom[b, r * 32 : r * 32 + 32, :].astype(F32))

        conv_rows(0)
        service(3 * b + 1)

        def settle(test, arrives):
            for n in range(2):
                for ud in range(2):
                    pl.when(test & (i == n))(functools.partial(arrives, n, ud))

        near = section // 2 == xh
        same = section % 2 == core
        settle(near & same, lambda n, ud: own_copy(n, ud).wait())
        settle(near & jnp.logical_not(same), sib_arrives)
        settle(jnp.logical_not(near) & jnp.logical_not(same), sibf_arrives)

        def pointwise(first, rows):
            part_rows = slice(first, first + 128)
            normed = normed_rows(conv[part_rows, :], pack_f[25:26, :]).astype(BF16)
            for n in range(4):
                at = pl.ds(n * 256, 256)
                bias = pack_f[26 + n // 2 : 27 + n // 2, (n % 2) * 256 : (n % 2) * 256 + 256]
                hidden = gelu(jnp.dot(normed, upw[b, :, at], preferred_element_type=F32) + bias).astype(BF16)
                part = jnp.dot(hidden, downw[b, at, :], preferred_element_type=F32)
                if n == 0:
                    hsum[...] = part
                else:
                    hsum[...] += part
            old = feat[slot, part_rows, :].astype(F32)
            new = (old + (hsum[...] + pack_f[28:29, :])).astype(BF16)
            feat[other, part_rows, :] = new
            wide = new.astype(F32)
            for n, r in enumerate(rows):
                place(2 + r, wide[32 * n : 32 * n + 32, :])

        @pl.when(b > 0)
        def _():
            halos_sent(b - 1, other)

        pointwise(0, (0, 1, 6, 7))

        @pl.when(b < NBLOCKS - 1)
        def _():
            send_halos(b + 1, other)

        @pl.when(b == NBLOCKS - 1)
        def _():
            finish(0)
            finish(3)

        service(3 * b + 2)
        pointwise(128, (2, 3, 4, 5))
        return 0

    lax.fori_loop(0, NBLOCKS, block, 0)

    finish(1)
    finish(2)

    for l in range(4):
        pl.when(not_me(goes[l]))(lambda l=l: pix_copy(l).wait_send())
    for k in range(3):
        small_copy(k).wait_send()
    for i, ud in KINDS:
        sib_copy(i, ud).wait_send()
        bnd_copy(i, ud).wait_send()
        sibf_copy(i, ud).wait_send()
        for r in range(3):
            fwd_copy(i, ud, r).wait_send()
    halos_sent(NBLOCKS - 1, 1)
    load_mem.wait()
    load_out.wait()

    lane = lax.broadcasted_iota(jnp.int32, (8, 128), 1)
    query = lax.broadcasted_iota(jnp.int32, (8, 128), 0)
    heads_of = equal(jnp.where(lane < HEADS * NLAT, lane // HEADS, -1), query)
    lat_f = jnp.concatenate([lats[...].astype(F32), jnp.zeros((5, WIDTH), F32)], axis=0)
    spread = jnp.dot(lat_f.T.astype(BF16), heads_of, preferred_element_type=F32)
    d_row = lax.broadcasted_iota(jnp.int32, (WIDTH, 128), 0)
    d_lane = lax.broadcasted_iota(jnp.int32, (WIDTH, 128), 1)
    queries = jnp.where(d_row // HSZ == d_lane % HEADS, spread, 0.0).astype(BF16)
    e_row = lax.broadcasted_iota(jnp.int32, (128, WIDTH), 0)
    e_lane = lax.broadcasted_iota(jnp.int32, (128, WIDTH), 1)

    for l in range(4):
        remote(feat.at[0, pl.ds(0, 64)], fold_in.at[l], fin_send.at[0], fin_recv.at[l], goes[l]).wait_recv()

    memory = normed_rows(
        fold_in[...].astype(F32).reshape(PLACES, WIDTH), fold_scale[...].astype(F32)
    ).astype(BF16)
    keys = jnp.dot(memory, memw[:, :WIDTH], preferred_element_type=F32).astype(BF16)
    values = jnp.dot(memory, memw[:, WIDTH:], preferred_element_type=F32).astype(BF16).astype(F32)
    raised = jnp.exp(jnp.dot(keys, queries, preferred_element_type=F32) * HSZ ** (-0.5))
    raised = raised.reshape(4, 64, 128)
    share = (raised / jnp.sum(raised, axis=0, keepdims=True)).astype(BF16).reshape(PLACES, 128)
    for q in range(NLAT):
        widen = equal(e_row, q * HEADS + e_lane // HSZ)
        wide = jnp.dot(share, widen, preferred_element_type=F32)
        mixed = jnp.sum((wide * values).reshape(4, 64, WIDTH), axis=0).astype(BF16)
        folded = jnp.dot(mixed, outw[...], preferred_element_type=F32) + lat_f[q : q + 1, :]
        folded = folded.astype(BF16)
        for r in range(2):
            out[0, r, q] = folded[r * 32 : (r + 1) * 32, :]

    for k in range(4):
        pl.when(not_me(comes[k]))(lambda k=k: fin_copy(k).wait_send())


def on_device(
    pixels, embed_weight, level_code, depth_kernel, norm_gain, up_weight, up_bias,
    down_weight, down_bias, fold_gain, latents, memory_weight, output_weight,
):
    vmem = pl.BlockSpec(memory_space=pltpu.VMEM)
    hbm = pl.BlockSpec(memory_space=pl.ANY)
    dma = pltpu.SemaphoreType.DMA
    result = pl.pallas_call(
        kernel,
        out_shape=jax.ShapeDtypeStruct((1, 2, NLAT, COLS, WIDTH), BF16),
        in_specs=[hbm] * 13,
        out_specs=vmem,
        scratch_shapes=[
            pltpu.VMEM((80, WIDTH), BF16),
            pltpu.VMEM((4, WIDTH), BF16),
            pltpu.VMEM((1, 25, 2, WIDTH), BF16),
            pltpu.VMEM((1, 2, WIDTH), BF16),
            pltpu.VMEM((1, 2, HIDDEN), BF16),
            pltpu.VMEM((1, 2, WIDTH), BF16),
            pltpu.VMEM((WIDTH,), BF16),
            pltpu.VMEM((NLAT, WIDTH), BF16),
            pltpu.VMEM((4, 5, 8, 128), BF16),
            pltpu.VMEM((NBLOCKS, 32, WIDTH), BF16),
            pltpu.VMEM((32, WIDTH), F32),
            pltpu.VMEM((NBLOCKS, WIDTH, HIDDEN), BF16),
            pltpu.VMEM((NBLOCKS, HIDDEN, WIDTH), BF16),
            pltpu.VMEM((WIDTH, 2 * WIDTH), BF16),
            pltpu.VMEM((WIDTH, WIDTH), BF16),
            pltpu.VMEM((2, PLACES, WIDTH), BF16),
            pltpu.VMEM((NBLOCKS, 64, WIDTH), BF16),
            pltpu.VMEM((NBLOCKS, 64, WIDTH), BF16),
            pltpu.VMEM((8 * (COLS + 4) * 8, 128), F32),
            pltpu.VMEM((200, 128), F32),
            pltpu.VMEM((4 * COLS * 8, 128), F32),
            pltpu.VMEM((PLACES, WIDTH), F32),
            pltpu.VMEM((128, WIDTH), F32),
            pltpu.VMEM((4, 128, 40), F32),
            pltpu.VMEM((4, 64, WIDTH), BF16),
            dma((4,)), dma((4,)), dma((3,)), dma((3,)), dma((2, 2)), dma((2, 2)), dma((2, 2)),
            dma((2, 2)), dma((2, 2)), dma((2, 2, 3)), dma((2, 2, 3)), dma((2, 2)), dma((2, 2)),
            dma((2, NBLOCKS)), dma((2, NBLOCKS)), dma((4,)), dma((4,)), dma((2,)), dma((8,)),
        ],
        compiler_params=pltpu.CompilerParams(
            collective_id=0, has_side_effects=True, vmem_limit_bytes=62 * 1024 * 1024
        ),
    )(
        pixels, embed_weight, level_code, jnp.transpose(depth_kernel, (0, 2, 1, 3)),
        norm_gain, up_weight, up_bias, down_weight, down_bias, fold_gain, latents,
        memory_weight, output_weight,
    )
    return jnp.transpose(result, (0, 1, 3, 2, 4))


def solution(mesh):
    return jax.shard_map(
        on_device,
        mesh=mesh,
        in_specs=(
            P(None, None, None, "lat", None),
            P(),
            P(),
            P("segment", None, None, None),
            P("segment", None, None),
            P("segment", None, None, None),
            P("segment", None, None),
            P("segment", None, None, None),
            P("segment", None, None),
            P(),
            P(),
            P(),
            P(),
        ),
        out_specs=P("segment", "lat", None, None, None),
        check_vma=False,
    )
```

```python
import functools

import jax
import jax.numpy as jnp
from jax import lax
from jax.experimental import pallas as pl
from jax.experimental.pallas import tpu as pltpu
from jax.sharding import PartitionSpec as P

MESH = pl.DeviceIdType.MESH
F32 = jnp.float32
BF16 = jnp.bfloat16
EPSILON = 1e-06
ROWS = 8
COLS = 32
WIDTH = 512
HIDDEN = 1024
NBLOCKS = 8
PLACES = ROWS * COLS
HEADS = 16
HSZ = 32
NLAT = 3
PIECE = (0, 128, 192, 64)
ROW_AT = (0, 32, 128, 160, 192, 224, 64, 96)
MIRROR = 11


def dev(xh, xl, y, z, core):
    return (xh * 2 + core, y * 16 + xl * 8 + z)


def remote(src, dst, send, recv, target):
    return pltpu.make_async_remote_copy(
        src_ref=src, dst_ref=dst, send_sem=send, recv_sem=recv, device_id=target, device_id_type=MESH
    )


def normed_rows(x, gain):
    average = jnp.mean(x, axis=-1, keepdims=True)
    centred = x - average
    spread = jnp.mean(centred * centred, axis=-1, keepdims=True)
    return centred * lax.rsqrt(spread + EPSILON) * gain


def gelu(x):
    return 0.5 * x * (1.0 + lax.erf(x * (2.0**-0.5)))


def kernel(
    pixels, embed_weight, level_code, depth, gain, up, up_bias, down, down_bias,
    fold_gain, latents, memory_weight, output_weight,
    out,
    embw, codes, taps, gains, up_shift, down_shift, fold_scale, lats,
    pix, pack, pack_f, upw, downw, memw, outw, feat, top, bottom, padded, taps8, conv8, conv, hsum, gath, fold_in,
    pix_send, pix_recv, small_send, small_recv, own_load, sib_send, sib_recv,
    bnd_send, bnd_recv, fwd_send, fwd_recv, sibf_send, sibf_recv,
    halo_send, halo_recv, fin_send, fin_recv, misc, load_sem, move_send, move_recv, turn,
):
    loads = [
        pltpu.make_async_copy(source, target, load_sem.at[n])
        for n, (source, target) in enumerate(
            (
                (depth, taps), (gain, gains), (up_bias, up_shift), (down_bias, down_shift),
                (embed_weight, embw), (level_code, codes), (fold_gain, fold_scale), (latents, lats),
            )
        )
    ]
    for load in loads:
        load.start()
    seg = lax.axis_index("segment")
    lat = lax.axis_index("lat")
    xh, core = seg // 2, seg % 2
    y, xl, z = lat // 16, (lat // 8) % 2, lat % 8
    early, late = xh == 0, xh == 1
    level, band = y, 2 * z + core
    has_up, has_down = band > 0, band < 15

    sibling = dev(xh, xl, y, z, 1 - core)
    partner = dev(1 - xh, 1 - xl, y, z, core)
    crossed = dev(1 - xh, 1 - xl, y, z, 1 - core)
    ring = [
        dev(xh, xl, (y + 1) % 4, z, core),
        dev(xh, xl, (y + 3) % 4, z, core),
        dev(xh, 1 - xl, y, z, core),
    ]
    others = [sibling, partner, crossed]
    up_band = jnp.maximum(band - 1, 0)
    down_band = jnp.minimum(band + 1, 15)
    above = dev(xh, xl, y, up_band // 2, up_band % 2)
    below = dev(xh, xl, y, down_band // 2, down_band % 2)
    src_band = lat // 4
    goes = [dev(xh, core, l, src_band // 2, src_band % 2) for l in range(4)]
    comes = [dev(xh, z % 2, z // 2, 4 * core + k, xl) for k in range(4)]

    def is_me(target):
        return (target[0] == seg) & (target[1] == lat)

    def not_me(target):
        return (target[0] != seg) | (target[1] != lat)

    barrier = pltpu.get_barrier_semaphore()

    def greet(target):
        pl.semaphore_signal(barrier, inc=1, device_id=target, device_id_type=MESH)

    for target in ring + others:
        greet(target)
    expected = jnp.int32(6)
    for target in goes + comes:
        pl.when(not_me(target))(functools.partial(greet, target))
        expected = expected + not_me(target).astype(jnp.int32)
    pl.when(has_up)(functools.partial(greet, above))
    pl.when(has_down)(functools.partial(greet, below))
    expected = expected + has_up.astype(jnp.int32) + has_down.astype(jnp.int32)
    pl.semaphore_wait(barrier, expected)

    my_slot = lat % 4

    def micro(image):
        return jnp.where(image == 0, core, 3 - core)

    def pix_copy(image, l):
        at = 4 * image + my_slot
        return remote(
            pixels.at[micro(image), l], pix.at[at], pix_send.at[4 * image + l], pix_recv.at[at], goes[l]
        )

    def pix_local(image, l):
        at = 4 * image + my_slot
        return pltpu.make_async_copy(pixels.at[micro(image), l], pix.at[at], pix_recv.at[at])

    def pix_wait(image, k):
        at = 4 * image + k
        remote(pixels.at[0, 0], pix.at[at], pix_send.at[0], pix_recv.at[at], comes[k]).wait_recv()

    @pl.when(early)
    def _():
        for image in (1, 0):
            for l in range(4):
                pl.when(not_me(goes[l]))(lambda: pix_copy(image, l).start())
                pl.when(is_me(goes[l]))(lambda: pix_local(image, l).start())

    quarter_to = (y + 2 * (1 - xl)) % 4
    quarter = (y + 2 * xl) % 4
    mine = 2 * seg
    far = 2 * ((1 - xh) * 2 + core)
    far_sib = 2 * ((1 - xh) * 2 + (1 - core))
    sib_first = 2 * (xh * 2 + (1 - core))

    def store(ud):
        return (upw, downw)[ud]

    def given(ud):
        return (up, down)[ud]

    def span(ud, q):
        rows = (128, 256)[ud]
        return pl.ds(pl.multiple_of(q * rows, rows), rows)

    def own_copy(i, ud):
        return pltpu.make_async_copy(given(ud).at[0, i], store(ud).at[mine + i], own_load.at[i, ud])

    def sib_copy(i, ud):
        return remote(given(ud).at[0, i], store(ud).at[mine + i], sib_send.at[i, ud], sib_recv.at[i, ud], sibling)

    def sib_arrives(i, ud):
        remote(given(ud).at[0, i], store(ud).at[sib_first + i], sib_send.at[i, ud], sib_recv.at[i, ud], sibling).wait_recv()

    def bnd_copy(i, ud):
        return remote(
            given(ud).at[0, i, span(ud, quarter_to)],
            store(ud).at[mine + i, span(ud, quarter_to)],
            bnd_send.at[i, ud], bnd_recv.at[i, ud], partner,
        )

    def far_part(i, ud, q):
        return store(ud).at[far + i, span(ud, q)]

    def bnd_arrives(i, ud):
        part = far_part(i, ud, quarter)
        remote(part, part, bnd_send.at[i, ud], bnd_recv.at[i, ud], partner).wait_recv()

    def fwd_copy(i, ud, r):
        part = far_part(i, ud, quarter)
        return remote(part, part, fwd_send.at[i, ud, r], fwd_recv.at[i, ud, r], ring[r])

    def fwd_arrives(i, ud, r):
        part = far_part(i, ud, (quarter + (3, 1, 2)[r]) % 4)
        remote(part, part, fwd_send.at[i, ud, r], fwd_recv.at[i, ud, r], ring[r]).wait_recv()

    def sibf_copy(i, ud):
        whole = store(ud).at[far + i]
        return remote(whole, whole, sibf_send.at[i, ud], sibf_recv.at[i, ud], sibling)

    def sibf_arrives(i, ud):
        whole = store(ud).at[far_sib + i]
        remote(whole, whole, sibf_send.at[i, ud], sibf_recv.at[i, ud], sibling).wait_recv()

    def forward(i, ud):
        bnd_arrives(i, ud)
        for r in range(3):
            fwd_copy(i, ud, r).start()

    def hand_over(i, ud):
        for r in range(3):
            fwd_arrives(i, ud, r)
        sibf_copy(i, ud).start()

    def by_core(first, second):
        return jnp.where(early, jnp.where(core == 0, first, second), -9)

    def when(step, part):
        return 3 * step + part

    pt_fwd = {
        (0, 0): by_core(when(1, 0), when(7, 0)), (0, 1): by_core(when(2, 1), when(8, 0)),
        (1, 0): by_core(when(4, 0), when(9, 0)), (1, 1): by_core(when(5, 0), when(9, 2)),
    }
    pt_hand = {
        (0, 0): by_core(when(3, 0), when(8, 2)), (0, 1): by_core(when(4, 1), when(9, 1)),
        (1, 0): by_core(when(6, 0), when(10, 1)), (1, 1): by_core(when(7, 0), when(11, 0)),
    }
    pt_sib = {
        (0, 0): by_core(-1, -1), (0, 1): by_core(-1, -1),
        (1, 0): by_core(when(0, 1), when(0, 1)), (1, 1): by_core(when(0, 1), when(0, 1)),
    }
    KINDS = [(0, 0), (0, 1), (1, 0), (1, 1)]

    def service(point):
        for i, ud in KINDS:
            pl.when(pt_sib[i, ud] == point)(lambda i=i, ud=ud: sib_copy(i, ud).start())
        for i, ud in KINDS:
            pl.when(pt_fwd[i, ud] == point)(functools.partial(forward, i, ud))
        for i, ud in KINDS:
            pl.when(pt_hand[i, ud] == point)(functools.partial(hand_over, i, ud))

    for i, ud in KINDS:
        own_copy(i, ud).start()
    load_mem = pltpu.make_async_copy(memory_weight, memw, misc.at[0])
    load_out = pltpu.make_async_copy(output_weight, outw, misc.at[1])
    load_mem.start()
    load_out.start()

    for load in loads:
        load.wait()
    for i in range(2):
        pack_f[0:25] = taps[0, :, i, :].astype(F32)
        pack_f[25:26] = gains[0, i : i + 1, :].astype(F32)
        pack_f[26:27] = up_shift[0, i : i + 1, :WIDTH].astype(F32)
        pack_f[27:28] = up_shift[0, i : i + 1, WIDTH:].astype(F32)
        pack_f[28:29] = down_shift[0, i : i + 1, :].astype(F32)
        pack_f[29:32] = jnp.zeros((3, WIDTH), F32)
        pack[mine + i] = pack_f[...].astype(BF16)

    def small_copy(k):
        part = pack.at[pl.ds(mine, 2)]
        return remote(part, part, small_send.at[k], small_recv.at[k], others[k])

    def small_from(k):
        return (xh * 2 + (1 - core), (1 - xh) * 2 + core, (1 - xh) * 2 + (1 - core))[k]

    def small_arrives(k):
        part = pack.at[pl.ds(2 * small_from(k), 2)]
        remote(part, part, small_send.at[k], small_recv.at[k], others[k]).wait_recv()

    small_copy(0).start()
    service(-1)

    grid5 = padded.reshape(2, 8, COLS + 4, 8, 128)
    for image in range(2):
        grid5[image, :, 0:2] = jnp.zeros((8, 2, 8, 128), F32)
        grid5[image, :, COLS + 2 :] = jnp.zeros((8, 2, 8, 128), F32)

    def place(image, padded_row, values):
        for flip in range(2):
            p = MIRROR - padded_row if flip else padded_row
            if p < 8:
                for c in range(0, COLS, 8):
                    for g in range(4):
                        start = (p * (COLS + 4) + 2 + c) * 8 + flip * 4 + g
                        padded[image, pl.ds(start, 8, stride=8), :] = values[c : c + 8, g * 128 : g * 128 + 128]

    def equal(a, b):
        return jnp.where(a == b, 1.0, 0.0).astype(BF16)

    rho = lax.broadcasted_iota(jnp.int32, (128, 128), 0)
    lon = lax.broadcasted_iota(jnp.int32, (128, 128), 1)
    pick = equal(lon, 4 * (rho % 32) + rho // 32)
    row = lax.broadcasted_iota(jnp.int32, (40, 80), 0)
    col = lax.broadcasted_iota(jnp.int32, (40, 80), 1)
    source_col = ((row // 8) * 4 + row % 4) * 4
    half = (row // 4) % 2
    def embed(image):
        for k in range(4):
            pix_wait(image, k)
        for k in range(4):
            cells = pix[4 * image + k].astype(F32).reshape(40, 128).astype(BF16)
            picked = lax.dot_general(pick, cells, (((1,), (1,)), ((), ())), preferred_element_type=F32)
            for j in range(4):
                gath[j, k * 32 : (k + 1) * 32, :] = picked[j * 32 : (j + 1) * 32, :]
        level_row = lax.broadcasted_iota(jnp.int32, (4, WIDTH), 0)
        code = jnp.sum(jnp.where(level_row == level, codes[...].astype(F32), 0.0), axis=0, keepdims=True)
        for r2 in range(2):
            total = jnp.zeros((128, WIDTH), F32)
            for j in range(4):
                choose = equal(jnp.where(half == r2, source_col + j, -1), col)
                part = jnp.dot(choose, embw[...], preferred_element_type=F32).astype(BF16)
                total = total + jnp.dot(gath[j].astype(BF16), part, preferred_element_type=F32)
            total = (total + code).astype(BF16)
            for k in range(4):
                piece = total[k * 32 : (k + 1) * 32, :]
                start = PIECE[k] + r2 * 32
                feat[2 * image, start : start + 32, :] = piece
                place(image, 2 + 2 * k + r2, piece.astype(F32))

    def halo_up(image, h, slot):
        at = NBLOCKS * image + h
        source = feat.at[2 * image + slot, pl.ds(0, 64)]
        return remote(source, bottom.at[at], halo_send.at[0, at], halo_recv.at[0, at], above)

    def halo_down(image, h, slot):
        at = NBLOCKS * image + h
        source = feat.at[2 * image + slot, pl.ds(64, 64)]
        return remote(source, top.at[at], halo_send.at[1, at], halo_recv.at[1, at], below)

    def send_halos(image, h, slot):
        pl.when(has_up)(lambda: halo_up(image, h, slot).start())
        pl.when(has_down)(lambda: halo_down(image, h, slot).start())

    def halos_sent(image, h, slot):
        pl.when(has_up)(lambda: halo_up(image, h, slot).wait_send())
        pl.when(has_down)(lambda: halo_down(image, h, slot).wait_send())

    for image in range(2):
        @pl.when(jnp.logical_not(has_up))
        def _():
            for r in range(2):
                place(image, r, jnp.zeros((COLS, WIDTH), F32))

        @pl.when(jnp.logical_not(has_down))
        def _():
            for r in range(2):
                place(image, ROWS + 2 + r, jnp.zeros((COLS, WIDTH), F32))

    def move_copy(part):
        rows = pl.ds(128 * part, 128)
        return remote(feat.at[2, rows], feat.at[0, rows], move_send.at[part], move_recv.at[part], partner)

    def move_arrives(part):
        move_copy(part).wait_recv()
        rows = (0, 1, 6, 7, 2, 3, 4, 5)[4 * part : 4 * part + 4]
        for n, r in enumerate(rows):
            start = ROW_AT[r]
            place(0, 2 + r, feat[0, start : start + 32, :].astype(F32))

    @pl.when(early)
    def _():
        for image in (1, 0):
            embed(image)
            send_halos(image, 0, 0)

    @pl.when(late)
    def _():
        @pl.when(core == 1)
        def _():
            pl.semaphore_wait(turn, 1)

        for i, ud in KINDS:
            bnd_copy(i, ud).start()
            bnd_copy(i, ud).wait_send()

        @pl.when(core == 0)
        def _():
            pl.semaphore_signal(turn, inc=1, device_id=sibling, device_id_type=MESH)

        for k in (1, 2):
            small_copy(k).start()
        for i, ud in KINDS:
            sib_copy(i, ud).start()
        move_arrives(0)
        send_halos(0, 4, 0)
        move_arrives(1)

    def conv_rows(image, first):
        def columns(step, _):
            base = step * 8
            sums = [[None] * 8 for _ in range(2)]
            for p in range(first, first + 6):
                for c in range(12):
                    value = padded[image, pl.ds(pl.multiple_of((p * (COLS + 4) + c) * 8 + base * 8, 8), 8), :]
                    for r in range(2):
                        i = p - first - r
                        for j in range(5):
                            if 0 <= i < 5 and 0 <= c - j < 8:
                                term = value * taps8[8 * (5 * i + j) : 8 * (5 * i + j) + 8, :]
                                old = sums[r][c - j]
                                sums[r][c - j] = term if old is None else old + term
            for r in range(2):
                for q in range(8):
                    at = pl.multiple_of(((first + r) * COLS + q) * 8 + base * 8, 8)
                    conv8[pl.ds(at, 8), :] = sums[r][q]
            return 0

        lax.fori_loop(0, COLS // 8, columns, 0)
        for r in (first, first + 1, 7 - first, 6 - first):
            flip = r > 3
            line = 7 - r if flip else r
            for c in range(0, COLS, 8):
                for g in range(4):
                    start = (line * COLS + c) * 8 + flip * 4 + g
                    at = ROW_AT[r] + c
                    conv[at : at + 8, g * 128 : g * 128 + 128] = conv8[pl.ds(start, 8, stride=8), :]

    def fin_copy(k):
        source = feat.at[0, pl.ds(PIECE[k], 64)]
        return remote(source, fold_in.at[level], fin_send.at[k], fin_recv.at[level], comes[k])

    def fin_local(k):
        source = feat.at[0, pl.ds(PIECE[k], 64)]
        return pltpu.make_async_copy(source, fold_in.at[level], fin_recv.at[level])

    def finish(k):
        pl.when(not_me(comes[k]))(lambda: fin_copy(k).start())
        pl.when(is_me(comes[k]))(lambda: fin_local(k).start())

    def block(step, _):
        both = early & (step < 8)
        image = jnp.where(both, 1 - step % 2, 0)
        b = jnp.where(both, step // 2, jnp.where(early, step - 4, step + 4))
        first_use = late | (image == 1) | (b >= 4)
        slot = b % 2
        other = 1 - slot
        section, i = b // 2, b % 2
        final = jnp.where(image == 1, 3, NBLOCKS - 1)
        service(3 * step)
        for k in range(3):
            pl.when(first_use & (i == 0) & (section == small_from(k)))(functools.partial(small_arrives, k))
        pack_f[...] = pack[b].astype(F32)
        for n in range(5):
            for g in range(4):
                five = pack_f[5 * n : 5 * n + 5, g * 128 : g * 128 + 128]
                taps8[pl.ds(40 * n + g, 5, stride=8), :] = five
                taps8[pl.ds(40 * (4 - n) + 4 + g, 5, stride=8), :] = five
        conv_rows(image, 2)

        @pl.when(has_up)
        def _():
            halo_down(image, b, slot).wait_recv()
            for r in range(2):
                place(image, r, top[NBLOCKS * image + b, r * 32 : r * 32 + 32, :].astype(F32))

        @pl.when(has_down)
        def _():
            halo_up(image, b, slot).wait_recv()
            for r in range(2):
                place(image, ROWS + 2 + r, bottom[NBLOCKS * image + b, r * 32 : r * 32 + 32, :].astype(F32))

        conv_rows(image, 0)
        service(3 * step + 1)

        def settle(test, arrives):
            for n in range(2):
                for ud in range(2):
                    pl.when(test & first_use & (i == n))(functools.partial(arrives, n, ud))

        near = section // 2 == xh
        same = section % 2 == core
        settle(near & same, lambda n, ud: own_copy(n, ud).wait())
        settle(near & jnp.logical_not(same), sib_arrives)
        settle(jnp.logical_not(near) & jnp.logical_not(same), sibf_arrives)

        def pointwise(first, rows):
            part_rows = slice(first, first + 128)
            normed = normed_rows(conv[part_rows, :], pack_f[25:26, :]).astype(BF16)
            for n in range(4):
                at = pl.ds(n * 256, 256)
                bias = pack_f[26 + n // 2 : 27 + n // 2, (n % 2) * 256 : (n % 2) * 256 + 256]
                hidden = gelu(jnp.dot(normed, upw[b, :, at], preferred_element_type=F32) + bias).astype(BF16)
                part = jnp.dot(hidden, downw[b, at, :], preferred_element_type=F32)
                if n == 0:
                    hsum[...] = part
                else:
                    hsum[...] += part
            old = feat[2 * image + slot, part_rows, :].astype(F32)
            new = (old + (hsum[...] + pack_f[28:29, :])).astype(BF16)
            feat[2 * image + other, part_rows, :] = new
            wide = new.astype(F32)
            for n, r in enumerate(rows):
                place(image, 2 + r, wide[32 * n : 32 * n + 32, :])

        @pl.when(b > jnp.where(late, 4, 0))
        def _():
            halos_sent(image, b - 1, other)

        pointwise(0, (0, 1, 6, 7))

        @pl.when(b < final)
        def _():
            send_halos(image, b + 1, other)

        @pl.when((b == final) & (image == 0))
        def _():
            finish(0)
            finish(3)

        pl.when((b == final) & (image == 1))(lambda: move_copy(0).start())
        service(3 * step + 2)
        pointwise(128, (2, 3, 4, 5))
        pl.when((b == final) & (image == 1))(lambda: move_copy(1).start())
        return 0

    lax.fori_loop(0, jnp.where(early, 12, 4), block, 0)

    finish(1)
    finish(2)

    small_copy(0).wait_send()
    for i, ud in KINDS:
        sib_copy(i, ud).wait_send()
    halos_sent(0, NBLOCKS - 1, 1)

    @pl.when(early)
    def _():
        for image in range(2):
            for l in range(4):
                pl.when(not_me(goes[l]))(lambda: pix_copy(image, l).wait_send())
        for i, ud in KINDS:
            sibf_copy(i, ud).wait_send()
            for r in range(3):
                fwd_copy(i, ud, r).wait_send()
        halos_sent(1, 3, 1)
        for part in range(2):
            move_copy(part).wait_send()

    @pl.when(late)
    def _():
        for k in (1, 2):
            small_copy(k).wait_send()

    load_mem.wait()
    load_out.wait()

    lane = lax.broadcasted_iota(jnp.int32, (8, 128), 1)
    query = lax.broadcasted_iota(jnp.int32, (8, 128), 0)
    heads_of = equal(jnp.where(lane < HEADS * NLAT, lane // HEADS, -1), query)
    lat_f = jnp.concatenate([lats[...].astype(F32), jnp.zeros((5, WIDTH), F32)], axis=0)
    spread = jnp.dot(lat_f.T.astype(BF16), heads_of, preferred_element_type=F32)
    d_row = lax.broadcasted_iota(jnp.int32, (WIDTH, 128), 0)
    d_lane = lax.broadcasted_iota(jnp.int32, (WIDTH, 128), 1)
    queries = jnp.where(d_row // HSZ == d_lane % HEADS, spread, 0.0).astype(BF16)
    e_row = lax.broadcasted_iota(jnp.int32, (128, WIDTH), 0)
    e_lane = lax.broadcasted_iota(jnp.int32, (128, WIDTH), 1)

    for l in range(4):
        remote(feat.at[0, pl.ds(0, 64)], fold_in.at[l], fin_send.at[0], fin_recv.at[l], goes[l]).wait_recv()

    memory = normed_rows(
        fold_in[...].astype(F32).reshape(PLACES, WIDTH), fold_scale[...].astype(F32)
    ).astype(BF16)
    keys = jnp.dot(memory, memw[:, :WIDTH], preferred_element_type=F32).astype(BF16)
    values = jnp.dot(memory, memw[:, WIDTH:], preferred_element_type=F32).astype(BF16).astype(F32)
    raised = jnp.exp(jnp.dot(keys, queries, preferred_element_type=F32) * HSZ ** (-0.5))
    raised = raised.reshape(4, 64, 128)
    share = (raised / jnp.sum(raised, axis=0, keepdims=True)).astype(BF16).reshape(PLACES, 128)
    for q in range(NLAT):
        widen = equal(e_row, q * HEADS + e_lane // HSZ)
        wide = jnp.dot(share, widen, preferred_element_type=F32)
        mixed = jnp.sum((wide * values).reshape(4, 64, WIDTH), axis=0).astype(BF16)
        folded = jnp.dot(mixed, outw[...], preferred_element_type=F32) + lat_f[q : q + 1, :]
        folded = folded.astype(BF16)
        for r in range(2):
            out[0, r, q] = folded[r * 32 : (r + 1) * 32, :]

    for k in range(4):
        pl.when(not_me(comes[k]))(lambda k=k: fin_copy(k).wait_send())


def on_device(
    pixels, embed_weight, level_code, depth_kernel, norm_gain, up_weight, up_bias,
    down_weight, down_bias, fold_gain, latents, memory_weight, output_weight,
):
    vmem = pl.BlockSpec(memory_space=pltpu.VMEM)
    hbm = pl.BlockSpec(memory_space=pl.ANY)
    dma = pltpu.SemaphoreType.DMA
    result = pl.pallas_call(
        kernel,
        out_shape=jax.ShapeDtypeStruct((1, 2, NLAT, COLS, WIDTH), BF16),
        in_specs=[hbm] * 13,
        out_specs=vmem,
        scratch_shapes=[
            pltpu.VMEM((80, WIDTH), BF16),
            pltpu.VMEM((4, WIDTH), BF16),
            pltpu.VMEM((1, 25, 2, WIDTH), BF16),
            pltpu.VMEM((1, 2, WIDTH), BF16),
            pltpu.VMEM((1, 2, HIDDEN), BF16),
            pltpu.VMEM((1, 2, WIDTH), BF16),
            pltpu.VMEM((WIDTH,), BF16),
            pltpu.VMEM((NLAT, WIDTH), BF16),
            pltpu.VMEM((8, 5, 8, 128), BF16),
            pltpu.VMEM((NBLOCKS, 32, WIDTH), BF16),
            pltpu.VMEM((32, WIDTH), F32),
            pltpu.VMEM((NBLOCKS, WIDTH, HIDDEN), BF16),
            pltpu.VMEM((NBLOCKS, HIDDEN, WIDTH), BF16),
            pltpu.VMEM((WIDTH, 2 * WIDTH), BF16),
            pltpu.VMEM((WIDTH, WIDTH), BF16),
            pltpu.VMEM((4, PLACES, WIDTH), BF16),
            pltpu.VMEM((2 * NBLOCKS, 64, WIDTH), BF16),
            pltpu.VMEM((2 * NBLOCKS, 64, WIDTH), BF16),
            pltpu.VMEM((2, 8 * (COLS + 4) * 8, 128), F32),
            pltpu.VMEM((200, 128), F32),
            pltpu.VMEM((4 * COLS * 8, 128), F32),
            pltpu.VMEM((PLACES, WIDTH), F32),
            pltpu.VMEM((128, WIDTH), F32),
            pltpu.VMEM((4, 128, 40), F32),
            pltpu.VMEM((4, 64, WIDTH), BF16),
            dma((8,)), dma((8,)), dma((3,)), dma((3,)), dma((2, 2)), dma((2, 2)), dma((2, 2)),
            dma((2, 2)), dma((2, 2)), dma((2, 2, 3)), dma((2, 2, 3)), dma((2, 2)), dma((2, 2)),
            dma((2, 2 * NBLOCKS)), dma((2, 2 * NBLOCKS)), dma((4,)), dma((4,)), dma((2,)), dma((8,)),
            dma((2,)), dma((2,)), pltpu.SemaphoreType.REGULAR,
        ],
        compiler_params=pltpu.CompilerParams(
            collective_id=0, has_side_effects=True, vmem_limit_bytes=62 * 1024 * 1024
        ),
    )(
        pixels, embed_weight, level_code, jnp.transpose(depth_kernel, (0, 2, 1, 3)),
        norm_gain, up_weight, up_bias, down_weight, down_bias, fold_gain, latents,
        memory_weight, output_weight,
    )
    return jnp.transpose(result, (0, 1, 3, 2, 4))


def solution(mesh):
    return jax.shard_map(
        on_device,
        mesh=mesh,
        in_specs=(
            P(None, None, None, "lat", None),
            P(),
            P(),
            P("segment", None, None, None),
            P("segment", None, None),
            P("segment", None, None, None),
            P("segment", None, None),
            P("segment", None, None, None),
            P("segment", None, None),
            P(),
            P(),
            P(),
            P(),
        ),
        out_specs=P("segment", "lat", None, None, None),
        check_vma=False,
    )
```

```python
import functools

import jax
import jax.numpy as jnp
from jax import lax
from jax.experimental import pallas as pl
from jax.experimental.pallas import tpu as pltpu
from jax.sharding import PartitionSpec as P

MESH = pl.DeviceIdType.MESH
F32 = jnp.float32
BF16 = jnp.bfloat16
EPSILON = 1e-06
ROWS = 8
COLS = 32
WIDTH = 512
HIDDEN = 1024
NBLOCKS = 8
PLACES = ROWS * COLS
HEADS = 16
HSZ = 32
NLAT = 3
PIECE = (0, 128, 192, 64)
ROW_AT = (0, 32, 128, 160, 192, 224, 64, 96)
MIRROR = 11


def dev(xh, xl, y, z, core):
    return (xh * 2 + core, y * 16 + xl * 8 + z)


def remote(src, dst, send, recv, target):
    return pltpu.make_async_remote_copy(
        src_ref=src, dst_ref=dst, send_sem=send, recv_sem=recv, device_id=target, device_id_type=MESH
    )


def normed_rows(x, gain):
    average = jnp.mean(x, axis=-1, keepdims=True)
    centred = x - average
    spread = jnp.mean(centred * centred, axis=-1, keepdims=True)
    return centred * lax.rsqrt(spread + EPSILON) * gain


def gelu(x):
    return 0.5 * x * (1.0 + lax.erf(x * (2.0**-0.5)))


def kernel(
    pixels, embed_weight, level_code, depth, gain, up, up_bias, down, down_bias,
    fold_gain, latents, memory_weight, output_weight,
    out,
    embw, codes, taps, gains, up_shift, down_shift, fold_scale, lats,
    pix, pack, pack_f, upw, downw, memw, outw, feat, top, bottom, padded, taps8, conv8, conv, hsum, gath, cellw, fold_in,
    pix_send, pix_recv, small_send, small_recv, own_load, sib_send, sib_recv,
    bnd_send, bnd_recv, fwd_send, fwd_recv, sibf_send, sibf_recv,
    halo_send, halo_recv, fin_send, fin_recv, misc, load_sem, move_send, move_recv,
):
    loads = [
        pltpu.make_async_copy(source, target, load_sem.at[n])
        for n, (source, target) in enumerate(
            (
                (depth, taps), (gain, gains), (up_bias, up_shift), (down_bias, down_shift),
                (embed_weight, embw), (level_code, codes), (fold_gain, fold_scale), (latents, lats),
            )
        )
    ]
    for load in loads:
        load.start()
    seg = lax.axis_index("segment")
    lat = lax.axis_index("lat")
    xh, core = seg // 2, seg % 2
    y, xl, z = lat // 16, (lat // 8) % 2, lat % 8
    early, late = xh == 0, xh == 1
    level, bend = z % 4, (y + xh) % 2
    chip = 2 * y + (xl + bend) % 2
    band = 2 * chip + core
    has_up, has_down = band > 0, band < 15

    def of_band(n):
        return dev(xh, (n // 2 + n // 4 + xh) % 2, n // 4, z, n % 2)

    sibling = dev(xh, xl, y, z, 1 - core)
    partner = dev(1 - xh, 1 - xl, y, z, core)
    crossed = dev(1 - xh, 1 - xl, y, z, 1 - core)
    odd = 2 * (y % 2)
    flipped = jnp.where((xl + xh) % 2 == 0, y + 1 - odd, (y + 3 + odd) % 4)
    ring = [
        dev(xh, xl, y, (z + 1) % 8, core),
        dev(xh, xl, y, (z + 7) % 8, core),
        dev(xh, xl, flipped, z, core),
    ]
    others = [sibling, partner, crossed]
    above = of_band(jnp.maximum(band - 1, 0))
    below = of_band(jnp.minimum(band + 1, 15))
    goes = [dev(xh, (xl + bend) % 2, y, core * 4 + l, z // 4) for l in range(4)]
    comes = [dev(xh, chip % 2, y, core * 4 + k, z // 4) for k in range(4)]

    def is_me(target):
        return (target[0] == seg) & (target[1] == lat)

    def not_me(target):
        return (target[0] != seg) | (target[1] != lat)

    barrier = pltpu.get_barrier_semaphore()

    def greet(target):
        pl.semaphore_signal(barrier, inc=1, device_id=target, device_id_type=MESH)

    for target in ring + others:
        greet(target)
    expected = jnp.int32(6)
    for target in goes + comes:
        pl.when(not_me(target))(functools.partial(greet, target))
        expected = expected + not_me(target).astype(jnp.int32)
    pl.when(has_up)(functools.partial(greet, above))
    pl.when(has_down)(functools.partial(greet, below))
    expected = expected + has_up.astype(jnp.int32) + has_down.astype(jnp.int32)

    my_slot = lat % 4

    def micro(image):
        return core + 2 * image

    def pix_copy(image, l):
        at = 4 * image + my_slot
        return remote(
            pixels.at[micro(image), l], pix.at[at], pix_send.at[4 * image + l], pix_recv.at[at], goes[l]
        )

    def pix_local(image, l):
        at = 4 * image + my_slot
        return pltpu.make_async_copy(pixels.at[micro(image), l], pix.at[at], pix_recv.at[at])

    def pix_wait(image, k):
        at = 4 * image + k
        remote(pixels.at[0, 0], pix.at[at], pix_send.at[0], pix_recv.at[at], comes[k]).wait_recv()

    quarter = (z + 2 * (y % 2)) % 4
    mine = 2 * seg
    far = 2 * ((1 - xh) * 2 + core)
    far_sib = 2 * ((1 - xh) * 2 + (1 - core))
    sib_first = 2 * (xh * 2 + (1 - core))

    def store(ud):
        return (upw, downw)[ud]

    def given(ud):
        return (up, down)[ud]

    def span(ud, q):
        rows = (128, 256)[ud]
        return pl.ds(pl.multiple_of(q * rows, rows), rows)

    def own_copy(i, ud):
        return pltpu.make_async_copy(given(ud).at[0, i], store(ud).at[mine + i], own_load.at[i, ud])

    def sib_copy(i, ud):
        return remote(given(ud).at[0, i], store(ud).at[mine + i], sib_send.at[i, ud], sib_recv.at[i, ud], sibling)

    def sib_arrives(i, ud):
        remote(given(ud).at[0, i], store(ud).at[sib_first + i], sib_send.at[i, ud], sib_recv.at[i, ud], sibling).wait_recv()

    def bnd_copy(i, ud):
        return remote(
            given(ud).at[0, i, span(ud, quarter)],
            store(ud).at[mine + i, span(ud, quarter)],
            bnd_send.at[i, ud], bnd_recv.at[i, ud], partner,
        )

    def far_part(i, ud, q):
        return store(ud).at[far + i, span(ud, q)]

    def bnd_arrives(i, ud):
        part = far_part(i, ud, quarter)
        remote(part, part, bnd_send.at[i, ud], bnd_recv.at[i, ud], partner).wait_recv()

    def fwd_copy(i, ud, r):
        part = far_part(i, ud, quarter)
        return remote(part, part, fwd_send.at[i, ud, r], fwd_recv.at[i, ud, r], ring[r])

    def fwd_arrives(i, ud, r):
        part = far_part(i, ud, (quarter + (3, 1, 2)[r]) % 4)
        remote(part, part, fwd_send.at[i, ud, r], fwd_recv.at[i, ud, r], ring[r]).wait_recv()

    def sibf_copy(i, ud):
        whole = store(ud).at[far + i]
        return remote(whole, whole, sibf_send.at[i, ud], sibf_recv.at[i, ud], sibling)

    def sibf_arrives(i, ud):
        whole = store(ud).at[far_sib + i]
        remote(whole, whole, sibf_send.at[i, ud], sibf_recv.at[i, ud], sibling).wait_recv()

    def forward(i, ud):
        bnd_arrives(i, ud)
        for r in range(3):
            fwd_copy(i, ud, r).start()

    def hand_over(i, ud):
        for r in range(3):
            fwd_arrives(i, ud, r)
        sibf_copy(i, ud).start()

    def by_core(first, second):
        return jnp.where(early, jnp.where(core == 0, first, second), -9)

    def when(step, part):
        return 3 * step + part

    pt_fwd = {
        (0, 0): by_core(when(1, 0), when(1, 0)), (0, 1): by_core(when(3, 0), when(3, 0)),
        (1, 0): by_core(when(5, 0), when(5, 0)), (1, 1): by_core(when(6, 2), when(7, 0)),
    }
    pt_hand = {
        (0, 0): by_core(when(4, 0), when(4, 0)), (0, 1): by_core(when(6, 0), when(6, 0)),
        (1, 0): by_core(when(8, 0), when(8, 2)), (1, 1): by_core(when(9, 0), when(9, 2)),
    }
    pt_sib = {
        (0, 0): by_core(-1, -1), (0, 1): by_core(-1, -1),
        (1, 0): by_core(when(0, 1), when(0, 1)), (1, 1): by_core(when(0, 1), when(0, 1)),
    }
    KINDS = [(0, 0), (0, 1), (1, 0), (1, 1)]

    def service(point):
        for i, ud in KINDS:
            pl.when(pt_sib[i, ud] == point)(lambda i=i, ud=ud: sib_copy(i, ud).start())
        for i, ud in KINDS:
            pl.when(pt_fwd[i, ud] == point)(functools.partial(forward, i, ud))
        for i, ud in KINDS:
            pl.when(pt_hand[i, ud] == point)(functools.partial(hand_over, i, ud))

    for i, ud in KINDS:
        own_copy(i, ud).start()
    load_mem = pltpu.make_async_copy(memory_weight, memw, misc.at[0])
    load_out = pltpu.make_async_copy(output_weight, outw, misc.at[1])
    load_mem.start()
    load_out.start()

    for load in loads:
        load.wait()
    for i in range(2):
        pack_f[0:25] = taps[0, :, i, :].astype(F32)
        pack_f[25:26] = gains[0, i : i + 1, :].astype(F32)
        pack_f[26:27] = up_shift[0, i : i + 1, :WIDTH].astype(F32)
        pack_f[27:28] = up_shift[0, i : i + 1, WIDTH:].astype(F32)
        pack_f[28:29] = down_shift[0, i : i + 1, :].astype(F32)
        pack_f[29:32] = jnp.zeros((3, WIDTH), F32)
        pack[mine + i] = pack_f[...].astype(BF16)

    def small_copy(k):
        part = pack.at[pl.ds(mine, 2)]
        return remote(part, part, small_send.at[k], small_recv.at[k], others[k])

    def small_from(k):
        return (xh * 2 + (1 - core), (1 - xh) * 2 + core, (1 - xh) * 2 + (1 - core))[k]

    def small_arrives(k):
        part = pack.at[pl.ds(2 * small_from(k), 2)]
        remote(part, part, small_send.at[k], small_recv.at[k], others[k]).wait_recv()

    grid5 = padded.reshape(2, 8, COLS + 4, 8, 128)
    for image in range(2):
        grid5[image, :, 0:2] = jnp.zeros((8, 2, 8, 128), F32)
        grid5[image, :, COLS + 2 :] = jnp.zeros((8, 2, 8, 128), F32)

    def place(image, padded_row, values):
        for flip in range(2):
            p = MIRROR - padded_row if flip else padded_row
            if p < 8:
                for c in range(0, COLS, 8):
                    for g in range(4):
                        start = (p * (COLS + 4) + 2 + c) * 8 + flip * 4 + g
                        padded[image, pl.ds(start, 8, stride=8), :] = values[c : c + 8, g * 128 : g * 128 + 128]

    def equal(a, b):
        return jnp.where(a == b, 1.0, 0.0).astype(BF16)

    rho = lax.broadcasted_iota(jnp.int32, (128, 128), 0)
    lon = lax.broadcasted_iota(jnp.int32, (128, 128), 1)
    pick = equal(lon, 4 * (rho % 32) + rho // 32)
    row = lax.broadcasted_iota(jnp.int32, (40, 80), 0)
    col = lax.broadcasted_iota(jnp.int32, (40, 80), 1)
    source_col = ((row // 8) * 4 + row % 4) * 4
    half = (row // 4) % 2
    @pl.when(early)
    def _():
        for r2 in range(2):
            for j in range(4):
                choose = equal(jnp.where(half == r2, source_col + j, -1), col)
                part = jnp.dot(choose, embw[...], preferred_element_type=F32)
                cellw[4 * r2 + j] = part.astype(BF16)

    for image in range(2):
        @pl.when(jnp.logical_not(has_up))
        def _():
            for r in range(2):
                place(image, r, jnp.zeros((COLS, WIDTH), F32))

        @pl.when(jnp.logical_not(has_down))
        def _():
            for r in range(2):
                place(image, ROWS + 2 + r, jnp.zeros((COLS, WIDTH), F32))

    pl.semaphore_wait(barrier, expected)

    @pl.when(early)
    def _():
        for image in (1, 0):
            for l in range(4):
                pl.when(not_me(goes[l]))(lambda: pix_copy(image, l).start())
                pl.when(is_me(goes[l]))(lambda: pix_local(image, l).start())

    small_copy(0).start()
    service(-1)

    def embed(image):
        for k in range(4):
            pix_wait(image, k)
        for k in range(4):
            cells = pix[4 * image + k].astype(F32).reshape(40, 128).astype(BF16)
            picked = lax.dot_general(pick, cells, (((1,), (1,)), ((), ())), preferred_element_type=F32)
            for j in range(4):
                gath[j, k * 32 : (k + 1) * 32, :] = picked[j * 32 : (j + 1) * 32, :]
        level_row = lax.broadcasted_iota(jnp.int32, (4, WIDTH), 0)
        code = jnp.sum(jnp.where(level_row == level, codes[...].astype(F32), 0.0), axis=0, keepdims=True)
        for r2 in range(2):
            total = jnp.zeros((128, WIDTH), F32)
            for j in range(4):
                total = total + jnp.dot(gath[j].astype(BF16), cellw[4 * r2 + j], preferred_element_type=F32)
            total = (total + code).astype(BF16)
            for k in range(4):
                piece = total[k * 32 : (k + 1) * 32, :]
                start = PIECE[k] + r2 * 32
                feat[2 * image, start : start + 32, :] = piece
                place(image, 2 + 2 * k + r2, piece.astype(F32))

    def halo_up(image, h, slot):
        at = NBLOCKS * image + h
        source = feat.at[2 * image + slot, pl.ds(0, 64)]
        return remote(source, bottom.at[at], halo_send.at[0, at], halo_recv.at[0, at], above)

    def halo_down(image, h, slot):
        at = NBLOCKS * image + h
        source = feat.at[2 * image + slot, pl.ds(64, 64)]
        return remote(source, top.at[at], halo_send.at[1, at], halo_recv.at[1, at], below)

    def send_halos(image, h, slot):
        pl.when(has_up)(lambda: halo_up(image, h, slot).start())
        pl.when(has_down)(lambda: halo_down(image, h, slot).start())

    def halos_sent(image, h, slot):
        pl.when(has_up)(lambda: halo_up(image, h, slot).wait_send())
        pl.when(has_down)(lambda: halo_down(image, h, slot).wait_send())

    def move_copy(part):
        rows = pl.ds(128 * part, 128)
        return remote(feat.at[2, rows], feat.at[0, rows], move_send.at[part], move_recv.at[part], partner)

    def move_arrives(part):
        move_copy(part).wait_recv()
        rows = (0, 1, 6, 7, 2, 3, 4, 5)[4 * part : 4 * part + 4]
        for n, r in enumerate(rows):
            start = ROW_AT[r]
            place(0, 2 + r, feat[0, start : start + 32, :].astype(F32))

    @pl.when(early)
    def _():
        for image in (1, 0):
            embed(image)
            send_halos(image, 0, 0)

    @pl.when(late)
    def _():
        for i, ud in KINDS:
            sib_copy(i, ud).start()
        for i, ud in KINDS:
            bnd_copy(i, ud).start()
            bnd_copy(i, ud).wait_send()
            if (i, ud) == (0, 1):
                for k in (1, 2):
                    small_copy(k).start()
        move_arrives(0)
        send_halos(0, 4, 0)
        move_arrives(1)

    def conv_rows(image, first, lines, drain):
        def columns(step, _):
            base = step * 8
            sums = [[None] * 8 for _ in range(2)]
            at = [[pl.ds(pl.multiple_of(((first + r) * COLS + q) * 8 + base * 8, 8), 8) for q in range(8)] for r in range(2)]
            if lines[0] < 2:
                sums = [[conv8[at[r][q], :] for q in range(8)] for r in range(2)]
            for p in lines:
                for c in range(12):
                    value = padded[image, pl.ds(pl.multiple_of((p * (COLS + 4) + c) * 8 + base * 8, 8), 8), :]
                    for r in range(2):
                        i = p - first - r
                        for j in range(5):
                            if 0 <= i < 5 and 0 <= c - j < 8:
                                term = value * taps8[8 * (5 * i + j) : 8 * (5 * i + j) + 8, :]
                                old = sums[r][c - j]
                                sums[r][c - j] = term if old is None else old + term
            for r in range(2):
                for q in range(8):
                    conv8[at[r][q], :] = sums[r][q]
            return 0

        lax.fori_loop(0, COLS // 8, columns, 0)
        for r in (first, first + 1, 7 - first, 6 - first) if drain else ():
            flip = r > 3
            line = 7 - r if flip else r
            for c in range(0, COLS, 8):
                for g in range(4):
                    start = (line * COLS + c) * 8 + flip * 4 + g
                    at = ROW_AT[r] + c
                    conv[at : at + 8, g * 128 : g * 128 + 128] = conv8[pl.ds(start, 8, stride=8), :]

    def fin_copy(k):
        source = feat.at[0, pl.ds(PIECE[k], 64)]
        return remote(source, fold_in.at[level], fin_send.at[k], fin_recv.at[level], comes[k])

    def fin_local(k):
        source = feat.at[0, pl.ds(PIECE[k], 64)]
        return pltpu.make_async_copy(source, fold_in.at[level], fin_recv.at[level])

    def finish(k):
        pl.when(not_me(comes[k]))(lambda: fin_copy(k).start())
        pl.when(is_me(comes[k]))(lambda: fin_local(k).start())

    def block(step, _):
        both = early & (step < 8)
        image = jnp.where(both, 1 - step % 2, 0)
        b = jnp.where(both, step // 2, jnp.where(early, step - 4, step + 4))
        first_use = late | (image == 1) | (b >= 4)
        slot = b % 2
        other = 1 - slot
        section, i = b // 2, b % 2
        final = jnp.where(image == 1, 3, NBLOCKS - 1)
        service(3 * step)
        for k in range(3):
            pl.when(first_use & (i == 0) & (section == small_from(k)))(functools.partial(small_arrives, k))
        pack_f[...] = pack[b].astype(F32)
        for n in range(5):
            for g in range(4):
                five = pack_f[5 * n : 5 * n + 5, g * 128 : g * 128 + 128]
                taps8[pl.ds(40 * n + g, 5, stride=8), :] = five
                taps8[pl.ds(40 * (4 - n) + 4 + g, 5, stride=8), :] = five
        conv_rows(image, 2, range(2, 8), True)
        conv_rows(image, 0, range(2, 6), False)

        @pl.when(has_up)
        def _():
            halo_down(image, b, slot).wait_recv()
            for r in range(2):
                place(image, r, top[NBLOCKS * image + b, r * 32 : r * 32 + 32, :].astype(F32))

        @pl.when(has_down)
        def _():
            halo_up(image, b, slot).wait_recv()
            for r in range(2):
                place(image, ROWS + 2 + r, bottom[NBLOCKS * image + b, r * 32 : r * 32 + 32, :].astype(F32))

        conv_rows(image, 0, range(2), True)
        service(3 * step + 1)

        def settle(test, arrives):
            for n in range(2):
                for ud in range(2):
                    pl.when(test & first_use & (i == n))(functools.partial(arrives, n, ud))

        near = section // 2 == xh
        same = section % 2 == core
        settle(near & same, lambda n, ud: own_copy(n, ud).wait())
        settle(near & jnp.logical_not(same), sib_arrives)
        settle(jnp.logical_not(near) & jnp.logical_not(same), sibf_arrives)

        def pointwise(first, rows):
            part_rows = slice(first, first + 128)
            normed = normed_rows(conv[part_rows, :], pack_f[25:26, :]).astype(BF16)
            for n in range(4):
                at = pl.ds(n * 256, 256)
                bias = pack_f[26 + n // 2 : 27 + n // 2, (n % 2) * 256 : (n % 2) * 256 + 256]
                hidden = gelu(jnp.dot(normed, upw[b, :, at], preferred_element_type=F32) + bias).astype(BF16)
                part = jnp.dot(hidden, downw[b, at, :], preferred_element_type=F32)
                if n == 0:
                    hsum[...] = part
                else:
                    hsum[...] += part
            old = feat[2 * image + slot, part_rows, :].astype(F32)
            new = (old + (hsum[...] + pack_f[28:29, :])).astype(BF16)
            feat[2 * image + other, part_rows, :] = new
            wide = new.astype(F32)
            for n, r in enumerate(rows):
                place(image, 2 + r, wide[32 * n : 32 * n + 32, :])

        @pl.when(b > jnp.where(late, 4, 0))
        def _():
            halos_sent(image, b - 1, other)

        pointwise(0, (0, 1, 6, 7))

        @pl.when(b < final)
        def _():
            send_halos(image, b + 1, other)

        @pl.when((b == final) & (image == 0))
        def _():
            finish(0)
            finish(3)

        pl.when((b == final) & (image == 1))(lambda: move_copy(0).start())
        service(3 * step + 2)
        pointwise(128, (2, 3, 4, 5))
        pl.when((b == final) & (image == 1))(lambda: move_copy(1).start())
        return 0

    lax.fori_loop(0, jnp.where(early, 12, 4), block, 0)

    finish(1)
    finish(2)

    small_copy(0).wait_send()
    for i, ud in KINDS:
        sib_copy(i, ud).wait_send()
    halos_sent(0, NBLOCKS - 1, 1)

    @pl.when(early)
    def _():
        for image in range(2):
            for l in range(4):
                pl.when(not_me(goes[l]))(lambda: pix_copy(image, l).wait_send())
        for i, ud in KINDS:
            sibf_copy(i, ud).wait_send()
            for r in range(3):
                fwd_copy(i, ud, r).wait_send()
        halos_sent(1, 3, 1)
        for part in range(2):
            move_copy(part).wait_send()

    @pl.when(late)
    def _():
        for k in (1, 2):
            small_copy(k).wait_send()

    load_mem.wait()
    load_out.wait()

    lane = lax.broadcasted_iota(jnp.int32, (8, 128), 1)
    query = lax.broadcasted_iota(jnp.int32, (8, 128), 0)
    heads_of = equal(jnp.where(lane < HEADS * NLAT, lane // HEADS, -1), query)
    lat_f = jnp.concatenate([lats[...].astype(F32), jnp.zeros((5, WIDTH), F32)], axis=0)
    spread = jnp.dot(lat_f.T.astype(BF16), heads_of, preferred_element_type=F32)
    d_row = lax.broadcasted_iota(jnp.int32, (WIDTH, 128), 0)
    d_lane = lax.broadcasted_iota(jnp.int32, (WIDTH, 128), 1)
    queries = jnp.where(d_row // HSZ == d_lane % HEADS, spread, 0.0).astype(BF16)
    e_row = lax.broadcasted_iota(jnp.int32, (128, WIDTH), 0)
    e_lane = lax.broadcasted_iota(jnp.int32, (128, WIDTH), 1)

    for l in range(4):
        remote(feat.at[0, pl.ds(0, 64)], fold_in.at[l], fin_send.at[0], fin_recv.at[l], goes[l]).wait_recv()

    memory = normed_rows(
        fold_in[...].astype(F32).reshape(PLACES, WIDTH), fold_scale[...].astype(F32)
    ).astype(BF16)
    keys = jnp.dot(memory, memw[:, :WIDTH], preferred_element_type=F32).astype(BF16)
    values = jnp.dot(memory, memw[:, WIDTH:], preferred_element_type=F32).astype(BF16).astype(F32)
    raised = jnp.exp(jnp.dot(keys, queries, preferred_element_type=F32) * HSZ ** (-0.5))
    raised = raised.reshape(4, 64, 128)
    share = (raised / jnp.sum(raised, axis=0, keepdims=True)).astype(BF16).reshape(PLACES, 128)
    for q in range(NLAT):
        widen = equal(e_row, q * HEADS + e_lane // HSZ)
        wide = jnp.dot(share, widen, preferred_element_type=F32)
        mixed = jnp.sum((wide * values).reshape(4, 64, WIDTH), axis=0).astype(BF16)
        folded = jnp.dot(mixed, outw[...], preferred_element_type=F32) + lat_f[q : q + 1, :]
        folded = folded.astype(BF16)
        for r in range(2):
            out[0, r, q] = folded[r * 32 : (r + 1) * 32, :]

    for k in range(4):
        pl.when(not_me(comes[k]))(lambda k=k: fin_copy(k).wait_send())


def on_device(
    pixels, embed_weight, level_code, depth_kernel, norm_gain, up_weight, up_bias,
    down_weight, down_bias, fold_gain, latents, memory_weight, output_weight,
):
    vmem = pl.BlockSpec(memory_space=pltpu.VMEM)
    hbm = pl.BlockSpec(memory_space=pl.ANY)
    dma = pltpu.SemaphoreType.DMA
    result = pl.pallas_call(
        kernel,
        out_shape=jax.ShapeDtypeStruct((1, 2, NLAT, COLS, WIDTH), BF16),
        in_specs=[hbm] * 13,
        out_specs=vmem,
        scratch_shapes=[
            pltpu.VMEM((80, WIDTH), BF16),
            pltpu.VMEM((4, WIDTH), BF16),
            pltpu.VMEM((1, 25, 2, WIDTH), BF16),
            pltpu.VMEM((1, 2, WIDTH), BF16),
            pltpu.VMEM((1, 2, HIDDEN), BF16),
            pltpu.VMEM((1, 2, WIDTH), BF16),
            pltpu.VMEM((WIDTH,), BF16),
            pltpu.VMEM((NLAT, WIDTH), BF16),
            pltpu.VMEM((8, 5, 8, 128), BF16),
            pltpu.VMEM((NBLOCKS, 32, WIDTH), BF16),
            pltpu.VMEM((32, WIDTH), F32),
            pltpu.VMEM((NBLOCKS, WIDTH, HIDDEN), BF16),
            pltpu.VMEM((NBLOCKS, HIDDEN, WIDTH), BF16),
            pltpu.VMEM((WIDTH, 2 * WIDTH), BF16),
            pltpu.VMEM((WIDTH, WIDTH), BF16),
            pltpu.VMEM((4, PLACES, WIDTH), BF16),
            pltpu.VMEM((2 * NBLOCKS, 64, WIDTH), BF16),
            pltpu.VMEM((2 * NBLOCKS, 64, WIDTH), BF16),
            pltpu.VMEM((2, 8 * (COLS + 4) * 8, 128), F32),
            pltpu.VMEM((200, 128), F32),
            pltpu.VMEM((4 * COLS * 8, 128), F32),
            pltpu.VMEM((PLACES, WIDTH), F32),
            pltpu.VMEM((128, WIDTH), F32),
            pltpu.VMEM((4, 128, 40), F32),
            pltpu.VMEM((8, 40, WIDTH), BF16),
            pltpu.VMEM((4, 64, WIDTH), BF16),
            dma((8,)), dma((8,)), dma((3,)), dma((3,)), dma((2, 2)), dma((2, 2)), dma((2, 2)),
            dma((2, 2)), dma((2, 2)), dma((2, 2, 3)), dma((2, 2, 3)), dma((2, 2)), dma((2, 2)),
            dma((2, 2 * NBLOCKS)), dma((2, 2 * NBLOCKS)), dma((4,)), dma((4,)), dma((2,)), dma((8,)),
            dma((2,)), dma((2,)),
        ],
        compiler_params=pltpu.CompilerParams(
            collective_id=0, has_side_effects=True, vmem_limit_bytes=62 * 1024 * 1024
        ),
    )(
        pixels, embed_weight, level_code, jnp.transpose(depth_kernel, (0, 2, 1, 3)),
        norm_gain, up_weight, up_bias, down_weight, down_bias, fold_gain, latents,
        memory_weight, output_weight,
    )
    return jnp.transpose(result, (0, 1, 3, 2, 4))


def solution(mesh):
    return jax.shard_map(
        on_device,
        mesh=mesh,
        in_specs=(
            P(None, None, None, "lat", None),
            P(),
            P(),
            P("segment", None, None, None),
            P("segment", None, None),
            P("segment", None, None, None),
            P("segment", None, None),
            P("segment", None, None, None),
            P("segment", None, None),
            P(),
            P(),
            P(),
            P(),
        ),
        out_specs=P("segment", "lat", None, None, None),
        check_vma=False,
    )
```

```python
import functools

import jax
import jax.numpy as jnp
from jax import lax
from jax.experimental import pallas as pl
from jax.experimental.pallas import tpu as pltpu
from jax.sharding import PartitionSpec as P

MESH = pl.DeviceIdType.MESH
F32 = jnp.float32
BF16 = jnp.bfloat16
EPSILON = 1e-06
ROWS = 8
COLS = 32
WIDTH = 512
HIDDEN = 1024
NBLOCKS = 8
PLACES = ROWS * COLS
HEADS = 16
HSZ = 32
NLAT = 3
PIECE = (0, 128, 192, 64)
ROW_AT = (0, 32, 128, 160, 192, 224, 64, 96)
MIRROR = 11


def dev(xh, xl, y, z, core):
    return (xh * 2 + core, y * 16 + xl * 8 + z)


def remote(src, dst, send, recv, target):
    return pltpu.make_async_remote_copy(
        src_ref=src, dst_ref=dst, send_sem=send, recv_sem=recv, device_id=target, device_id_type=MESH
    )


def normed_rows(x, gain):
    average = jnp.mean(x, axis=-1, keepdims=True)
    centred = x - average
    spread = jnp.mean(centred * centred, axis=-1, keepdims=True)
    return centred * lax.rsqrt(spread + EPSILON) * gain


def gelu(x):
    return 0.5 * x * (1.0 + lax.erf(x * (2.0**-0.5)))


def kernel(
    pixels, embed_weight, level_code, depth, gain, up, up_bias, down, down_bias,
    fold_gain, latents, memory_weight, output_weight,
    out,
    embw, codes, taps, gains, up_shift, down_shift, fold_scale, lats,
    pix, pack, pack_f, upw, downw, memw, outw, feat, top, bottom, padded, taps8, conv8, conv, hidden, gath, cellw, fold_in,
    pix_send, pix_recv, small_send, small_recv, own_load, sib_send, sib_recv,
    bnd_send, bnd_recv, fwd_send, fwd_recv, sibf_send, sibf_recv,
    halo_send, halo_recv, fin_send, fin_recv, misc, load_sem, move_send, move_recv,
):
    loads = [
        pltpu.make_async_copy(source, target, load_sem.at[n])
        for n, (source, target) in enumerate(
            (
                (depth, taps), (gain, gains), (up_bias, up_shift), (down_bias, down_shift),
                (embed_weight, embw), (level_code, codes), (fold_gain, fold_scale), (latents, lats),
            )
        )
    ]
    for load in loads:
        load.start()
    seg = lax.axis_index("segment")
    lat = lax.axis_index("lat")
    xh, core = seg // 2, seg % 2
    y, xl, z = lat // 16, (lat // 8) % 2, lat % 8
    early, late = xh == 0, xh == 1
    level, bend = z % 4, (y + xh) % 2
    chip = 2 * y + (xl + bend) % 2
    band = 2 * chip + core
    has_up, has_down = band > 0, band < 15

    def of_band(n):
        return dev(xh, (n // 2 + n // 4 + xh) % 2, n // 4, z, n % 2)

    sibling = dev(xh, xl, y, z, 1 - core)
    partner = dev(1 - xh, 1 - xl, y, z, core)
    crossed = dev(1 - xh, 1 - xl, y, z, 1 - core)
    odd = 2 * (y % 2)
    flipped = jnp.where((xl + xh) % 2 == 0, y + 1 - odd, (y + 3 + odd) % 4)
    ring = [
        dev(xh, xl, y, (z + 1) % 8, core),
        dev(xh, xl, y, (z + 7) % 8, core),
        dev(xh, xl, flipped, z, core),
    ]
    others = [sibling, partner, crossed]
    above = of_band(jnp.maximum(band - 1, 0))
    below = of_band(jnp.minimum(band + 1, 15))
    goes = [dev(xh, (xl + bend) % 2, y, core * 4 + l, z // 4) for l in range(4)]
    comes = [dev(xh, chip % 2, y, core * 4 + k, z // 4) for k in range(4)]

    def is_me(target):
        return (target[0] == seg) & (target[1] == lat)

    def not_me(target):
        return (target[0] != seg) | (target[1] != lat)

    barrier = pltpu.get_barrier_semaphore()

    def greet(target):
        pl.semaphore_signal(barrier, inc=1, device_id=target, device_id_type=MESH)

    for target in ring + others:
        greet(target)
    expected = jnp.int32(6)
    for target in goes + comes:
        pl.when(not_me(target))(functools.partial(greet, target))
        expected = expected + not_me(target).astype(jnp.int32)
    pl.when(has_up)(functools.partial(greet, above))
    pl.when(has_down)(functools.partial(greet, below))
    expected = expected + has_up.astype(jnp.int32) + has_down.astype(jnp.int32)

    my_slot = lat % 4

    def micro(image):
        return core + 2 * image

    def pix_copy(image, l):
        at = 4 * image + my_slot
        return remote(
            pixels.at[micro(image), l], pix.at[at], pix_send.at[4 * image + l], pix_recv.at[at], goes[l]
        )

    def pix_local(image, l):
        at = 4 * image + my_slot
        return pltpu.make_async_copy(pixels.at[micro(image), l], pix.at[at], pix_recv.at[at])

    def pix_wait(image, k):
        at = 4 * image + k
        remote(pixels.at[0, 0], pix.at[at], pix_send.at[0], pix_recv.at[at], comes[k]).wait_recv()

    quarter = (z + 2 * (y % 2)) % 4
    mine = 2 * seg
    far = 2 * ((1 - xh) * 2 + core)
    far_sib = 2 * ((1 - xh) * 2 + (1 - core))
    sib_first = 2 * (xh * 2 + (1 - core))

    def store(ud):
        return (upw, downw)[ud]

    def given(ud):
        return (up, down)[ud]

    def span(ud, q):
        rows = (128, 256)[ud]
        return pl.ds(pl.multiple_of(q * rows, rows), rows)

    def own_copy(i, ud):
        return pltpu.make_async_copy(given(ud).at[0, i], store(ud).at[mine + i], own_load.at[i, ud])

    def sib_copy(i, ud):
        return remote(given(ud).at[0, i], store(ud).at[mine + i], sib_send.at[i, ud], sib_recv.at[i, ud], sibling)

    def sib_arrives(i, ud):
        remote(given(ud).at[0, i], store(ud).at[sib_first + i], sib_send.at[i, ud], sib_recv.at[i, ud], sibling).wait_recv()

    def bnd_copy(i, ud):
        return remote(
            given(ud).at[0, i, span(ud, quarter)],
            store(ud).at[mine + i, span(ud, quarter)],
            bnd_send.at[i, ud], bnd_recv.at[i, ud], partner,
        )

    def far_part(i, ud, q):
        return store(ud).at[far + i, span(ud, q)]

    def bnd_arrives(i, ud):
        part = far_part(i, ud, quarter)
        remote(part, part, bnd_send.at[i, ud], bnd_recv.at[i, ud], partner).wait_recv()

    def fwd_copy(i, ud, r):
        part = far_part(i, ud, quarter)
        return remote(part, part, fwd_send.at[i, ud, r], fwd_recv.at[i, ud, r], ring[r])

    def fwd_arrives(i, ud, r):
        part = far_part(i, ud, (quarter + (3, 1, 2)[r]) % 4)
        remote(part, part, fwd_send.at[i, ud, r], fwd_recv.at[i, ud, r], ring[r]).wait_recv()

    def sibf_copy(i, ud):
        whole = store(ud).at[far + i]
        return remote(whole, whole, sibf_send.at[i, ud], sibf_recv.at[i, ud], sibling)

    def sibf_arrives(i, ud):
        whole = store(ud).at[far_sib + i]
        remote(whole, whole, sibf_send.at[i, ud], sibf_recv.at[i, ud], sibling).wait_recv()

    def forward(i, ud):
        bnd_arrives(i, ud)
        for r in range(3):
            fwd_copy(i, ud, r).start()

    def hand_over(i, ud):
        for r in range(3):
            fwd_arrives(i, ud, r)
        sibf_copy(i, ud).start()

    def by_core(first, second):
        return jnp.where(early, jnp.where(core == 0, first, second), -9)

    def when(step, part):
        return 3 * step + part

    pt_fwd = {
        (0, 0): by_core(when(1, 0), when(1, 0)), (0, 1): by_core(when(3, 0), when(3, 0)),
        (1, 0): by_core(when(5, 0), when(5, 0)), (1, 1): by_core(when(6, 2), when(7, 0)),
    }
    pt_hand = {
        (0, 0): by_core(when(4, 0), when(4, 0)), (0, 1): by_core(when(6, 0), when(6, 0)),
        (1, 0): by_core(when(8, 0), when(8, 2)), (1, 1): by_core(when(9, 0), when(9, 2)),
    }
    pt_sib = {
        (0, 0): by_core(-1, -1), (0, 1): by_core(-1, -1),
        (1, 0): by_core(when(0, 1), when(0, 1)), (1, 1): by_core(when(0, 1), when(0, 1)),
    }
    KINDS = [(0, 0), (0, 1), (1, 0), (1, 1)]

    def service(point):
        for i, ud in KINDS:
            pl.when(pt_sib[i, ud] == point)(lambda i=i, ud=ud: sib_copy(i, ud).start())
        for i, ud in KINDS:
            pl.when(pt_fwd[i, ud] == point)(functools.partial(forward, i, ud))
        for i, ud in KINDS:
            pl.when(pt_hand[i, ud] == point)(functools.partial(hand_over, i, ud))

    for i, ud in KINDS:
        own_copy(i, ud).start()
    load_mem = pltpu.make_async_copy(memory_weight, memw, misc.at[0])
    load_out = pltpu.make_async_copy(output_weight, outw, misc.at[1])
    load_mem.start()
    load_out.start()

    for load in loads:
        load.wait()
    for i in range(2):
        pack_f[0:25] = taps[0, :, i, :].astype(F32)
        pack_f[25:26] = gains[0, i : i + 1, :].astype(F32)
        pack_f[26:27] = up_shift[0, i : i + 1, :WIDTH].astype(F32)
        pack_f[27:28] = up_shift[0, i : i + 1, WIDTH:].astype(F32)
        pack_f[28:29] = down_shift[0, i : i + 1, :].astype(F32)
        pack_f[29:32] = jnp.zeros((3, WIDTH), F32)
        pack[mine + i] = pack_f[...].astype(BF16)

    def small_copy(k):
        part = pack.at[pl.ds(mine, 2)]
        return remote(part, part, small_send.at[k], small_recv.at[k], others[k])

    def small_from(k):
        return (xh * 2 + (1 - core), (1 - xh) * 2 + core, (1 - xh) * 2 + (1 - core))[k]

    def small_arrives(k):
        part = pack.at[pl.ds(2 * small_from(k), 2)]
        remote(part, part, small_send.at[k], small_recv.at[k], others[k]).wait_recv()

    grid5 = padded.reshape(2, 8, COLS + 4, 8, 128)
    for image in range(2):
        grid5[image, :, 0:2] = jnp.zeros((8, 2, 8, 128), F32)
        grid5[image, :, COLS + 2 :] = jnp.zeros((8, 2, 8, 128), F32)

    def place(image, padded_row, values):
        for flip in range(2):
            p = MIRROR - padded_row if flip else padded_row
            if p < 8:
                for c in range(0, COLS, 8):
                    for g in range(4):
                        start = (p * (COLS + 4) + 2 + c) * 8 + flip * 4 + g
                        padded[image, pl.ds(start, 8, stride=8), :] = values[c : c + 8, g * 128 : g * 128 + 128]

    def equal(a, b):
        return jnp.where(a == b, 1.0, 0.0).astype(BF16)

    rho = lax.broadcasted_iota(jnp.int32, (128, 128), 0)
    lon = lax.broadcasted_iota(jnp.int32, (128, 128), 1)
    pick = equal(lon, 4 * (rho % 32) + rho // 32)
    row = lax.broadcasted_iota(jnp.int32, (40, 80), 0)
    col = lax.broadcasted_iota(jnp.int32, (40, 80), 1)
    source_col = ((row // 8) * 4 + row % 4) * 4
    half = (row // 4) % 2
    @pl.when(early)
    def _():
        for r2 in range(2):
            for j in range(4):
                choose = equal(jnp.where(half == r2, source_col + j, -1), col)
                part = jnp.dot(choose, embw[...], preferred_element_type=F32)
                cellw[4 * r2 + j] = part.astype(BF16)

    for image in range(2):
        @pl.when(jnp.logical_not(has_up))
        def _():
            for r in range(2):
                place(image, r, jnp.zeros((COLS, WIDTH), F32))

        @pl.when(jnp.logical_not(has_down))
        def _():
            for r in range(2):
                place(image, ROWS + 2 + r, jnp.zeros((COLS, WIDTH), F32))

    pl.semaphore_wait(barrier, expected)

    @pl.when(early)
    def _():
        for image in (1, 0):
            for l in range(4):
                pl.when(not_me(goes[l]))(lambda: pix_copy(image, l).start())
                pl.when(is_me(goes[l]))(lambda: pix_local(image, l).start())

    small_copy(0).start()
    service(-1)

    def embed(image):
        for k in range(4):
            pix_wait(image, k)
        for k in range(4):
            cells = pix[4 * image + k].astype(F32).reshape(40, 128).astype(BF16)
            picked = lax.dot_general(pick, cells, (((1,), (1,)), ((), ())), preferred_element_type=F32)
            for j in range(4):
                gath[j, k * 32 : (k + 1) * 32, :] = picked[j * 32 : (j + 1) * 32, :]
        level_row = lax.broadcasted_iota(jnp.int32, (4, WIDTH), 0)
        code = jnp.sum(jnp.where(level_row == level, codes[...].astype(F32), 0.0), axis=0, keepdims=True)
        for r2 in range(2):
            total = jnp.zeros((128, WIDTH), F32)
            for j in range(4):
                total = total + jnp.dot(gath[j].astype(BF16), cellw[4 * r2 + j], preferred_element_type=F32)
            total = (total + code).astype(BF16)
            for k in range(4):
                piece = total[k * 32 : (k + 1) * 32, :]
                start = PIECE[k] + r2 * 32
                feat[2 * image, start : start + 32, :] = piece
                place(image, 2 + 2 * k + r2, piece.astype(F32))

    def halo_up(image, h, slot):
        at = NBLOCKS * image + h
        source = feat.at[2 * image + slot, pl.ds(0, 64)]
        return remote(source, bottom.at[at], halo_send.at[0, at], halo_recv.at[0, at], above)

    def halo_down(image, h, slot):
        at = NBLOCKS * image + h
        source = feat.at[2 * image + slot, pl.ds(64, 64)]
        return remote(source, top.at[at], halo_send.at[1, at], halo_recv.at[1, at], below)

    def send_halos(image, h, slot):
        pl.when(has_up)(lambda: halo_up(image, h, slot).start())
        pl.when(has_down)(lambda: halo_down(image, h, slot).start())

    def halos_sent(image, h, slot):
        pl.when(has_up)(lambda: halo_up(image, h, slot).wait_send())
        pl.when(has_down)(lambda: halo_down(image, h, slot).wait_send())

    def move_copy(part):
        rows = pl.ds(128 * part, 128)
        return remote(feat.at[2, rows], feat.at[0, rows], move_send.at[part], move_recv.at[part], partner)

    def move_arrives(part):
        move_copy(part).wait_recv()
        rows = (0, 1, 6, 7, 2, 3, 4, 5)[4 * part : 4 * part + 4]
        for n, r in enumerate(rows):
            start = ROW_AT[r]
            place(0, 2 + r, feat[0, start : start + 32, :].astype(F32))

    @pl.when(early)
    def _():
        for image in (1, 0):
            embed(image)
            send_halos(image, 0, 0)

    @pl.when(late)
    def _():
        for i, ud in KINDS:
            sib_copy(i, ud).start()
        for i, ud in KINDS:
            bnd_copy(i, ud).start()
            bnd_copy(i, ud).wait_send()
            if (i, ud) == (0, 1):
                for k in (1, 2):
                    small_copy(k).start()
        move_arrives(0)
        send_halos(0, 4, 0)
        move_arrives(1)

    def conv_rows(image, first, lines, drain):
        def columns(step, _):
            base = step * 8
            sums = [[None] * 8 for _ in range(2)]
            at = [[pl.ds(pl.multiple_of(((first + r) * COLS + q) * 8 + base * 8, 8), 8) for q in range(8)] for r in range(2)]
            if lines[0] < 2:
                sums = [[conv8[at[r][q], :] for q in range(8)] for r in range(2)]
            for p in lines:
                for c in range(12):
                    value = padded[image, pl.ds(pl.multiple_of((p * (COLS + 4) + c) * 8 + base * 8, 8), 8), :]
                    for r in range(2):
                        i = p - first - r
                        for j in range(5):
                            if 0 <= i < 5 and 0 <= c - j < 8:
                                term = value * taps8[8 * (5 * i + j) : 8 * (5 * i + j) + 8, :]
                                old = sums[r][c - j]
                                sums[r][c - j] = term if old is None else old + term
            for r in range(2):
                for q in range(8):
                    conv8[at[r][q], :] = sums[r][q]
            return 0

        lax.fori_loop(0, COLS // 8, columns, 0)
        for r in (first, first + 1, 7 - first, 6 - first) if drain else ():
            flip = r > 3
            line = 7 - r if flip else r
            for c in range(0, COLS, 8):
                for g in range(4):
                    start = (line * COLS + c) * 8 + flip * 4 + g
                    at = ROW_AT[r] + c
                    conv[at : at + 8, g * 128 : g * 128 + 128] = conv8[pl.ds(start, 8, stride=8), :]

    def fin_copy(k):
        source = feat.at[0, pl.ds(PIECE[k], 64)]
        return remote(source, fold_in.at[level], fin_send.at[k], fin_recv.at[level], comes[k])

    def fin_local(k):
        source = feat.at[0, pl.ds(PIECE[k], 64)]
        return pltpu.make_async_copy(source, fold_in.at[level], fin_recv.at[level])

    def finish(k):
        pl.when(not_me(comes[k]))(lambda: fin_copy(k).start())
        pl.when(is_me(comes[k]))(lambda: fin_local(k).start())

    def block(step, _):
        both = early & (step < 8)
        image = jnp.where(both, 1 - step % 2, 0)
        b = jnp.where(both, step // 2, jnp.where(early, step - 4, step + 4))
        first_use = late | (image == 1) | (b >= 4)
        slot = b % 2
        other = 1 - slot
        section, i = b // 2, b % 2
        final = jnp.where(image == 1, 3, NBLOCKS - 1)
        service(3 * step)
        for k in range(3):
            pl.when(first_use & (i == 0) & (section == small_from(k)))(functools.partial(small_arrives, k))
        pack_f[...] = pack[b].astype(F32)
        for n in range(5):
            for g in range(4):
                five = pack_f[5 * n : 5 * n + 5, g * 128 : g * 128 + 128]
                taps8[pl.ds(40 * n + g, 5, stride=8), :] = five
                taps8[pl.ds(40 * (4 - n) + 4 + g, 5, stride=8), :] = five
        conv_rows(image, 2, range(2, 8), True)
        conv_rows(image, 0, range(2, 6), False)
        service(3 * step + 1)

        def settle(test, arrives):
            for n in range(2):
                for ud in range(2):
                    pl.when(test & first_use & (i == n))(functools.partial(arrives, n, ud))

        near = section // 2 == xh
        same = section % 2 == core
        settle(near & same, lambda n, ud: own_copy(n, ud).wait())
        settle(near & jnp.logical_not(same), sib_arrives)
        settle(jnp.logical_not(near) & jnp.logical_not(same), sibf_arrives)

        @pl.when(has_up)
        def _():
            halo_down(image, b, slot).wait_recv()
            for r in range(2):
                place(image, r, top[NBLOCKS * image + b, r * 32 : r * 32 + 32, :].astype(F32))

        @pl.when(has_down)
        def _():
            halo_up(image, b, slot).wait_recv()
            for r in range(2):
                place(image, ROWS + 2 + r, bottom[NBLOCKS * image + b, r * 32 : r * 32 + 32, :].astype(F32))

        conv_rows(image, 0, range(2), True)

        def pointwise(first, count):
            part_rows = slice(first, first + count)
            normed = normed_rows(conv[part_rows, :], pack_f[25:26, :]).astype(BF16)
            for n in range(2):
                at = pl.ds(n * WIDTH, WIDTH)
                raised = jnp.dot(normed, upw[b, :, at], preferred_element_type=F32)
                hidden[0:count, at] = gelu(raised + pack_f[26 + n : 27 + n, :]).astype(BF16)
            branch = jnp.dot(hidden[0:count, :], downw[b], preferred_element_type=F32)
            old = feat[2 * image + slot, part_rows, :].astype(F32)
            new = (old + (branch + pack_f[28:29, :])).astype(BF16)
            feat[2 * image + other, part_rows, :] = new
            wide = new.astype(F32)
            for r in range(ROWS):
                if first <= ROW_AT[r] < first + count:
                    place(image, 2 + r, wide[ROW_AT[r] - first : ROW_AT[r] - first + 32, :])

        @pl.when(b > jnp.where(late, 4, 0))
        def _():
            halos_sent(image, b - 1, other)

        whole = early & (step < 6)
        pl.when(whole)(lambda: pointwise(0, PLACES))
        pl.when(jnp.logical_not(whole))(lambda: pointwise(0, PLACES // 2))

        @pl.when(b < final)
        def _():
            send_halos(image, b + 1, other)

        @pl.when((b == final) & (image == 0))
        def _():
            finish(0)
            finish(3)

        pl.when((b == final) & (image == 1))(lambda: move_copy(0).start())
        service(3 * step + 2)
        pl.when(jnp.logical_not(whole))(lambda: pointwise(PLACES // 2, PLACES // 2))
        pl.when((b == final) & (image == 1))(lambda: move_copy(1).start())
        return 0

    lax.fori_loop(0, jnp.where(early, 12, 4), block, 0)

    finish(1)
    finish(2)

    small_copy(0).wait_send()
    for i, ud in KINDS:
        sib_copy(i, ud).wait_send()
    halos_sent(0, NBLOCKS - 1, 1)

    @pl.when(early)
    def _():
        for image in range(2):
            for l in range(4):
                pl.when(not_me(goes[l]))(lambda: pix_copy(image, l).wait_send())
        for i, ud in KINDS:
            sibf_copy(i, ud).wait_send()
            for r in range(3):
                fwd_copy(i, ud, r).wait_send()
        halos_sent(1, 3, 1)
        for part in range(2):
            move_copy(part).wait_send()

    @pl.when(late)
    def _():
        for k in (1, 2):
            small_copy(k).wait_send()

    load_mem.wait()
    load_out.wait()

    lane = lax.broadcasted_iota(jnp.int32, (8, 128), 1)
    query = lax.broadcasted_iota(jnp.int32, (8, 128), 0)
    heads_of = equal(jnp.where(lane < HEADS * NLAT, lane // HEADS, -1), query)
    lat_f = jnp.concatenate([lats[...].astype(F32), jnp.zeros((5, WIDTH), F32)], axis=0)
    spread = jnp.dot(lat_f.T.astype(BF16), heads_of, preferred_element_type=F32)
    d_row = lax.broadcasted_iota(jnp.int32, (WIDTH, 128), 0)
    d_lane = lax.broadcasted_iota(jnp.int32, (WIDTH, 128), 1)
    queries = jnp.where(d_row // HSZ == d_lane % HEADS, spread, 0.0).astype(BF16)
    e_row = lax.broadcasted_iota(jnp.int32, (128, WIDTH), 0)
    e_lane = lax.broadcasted_iota(jnp.int32, (128, WIDTH), 1)

    for l in range(4):
        remote(feat.at[0, pl.ds(0, 64)], fold_in.at[l], fin_send.at[0], fin_recv.at[l], goes[l]).wait_recv()

    memory = normed_rows(
        fold_in[...].astype(F32).reshape(PLACES, WIDTH), fold_scale[...].astype(F32)
    ).astype(BF16)
    keys = jnp.dot(memory, memw[:, :WIDTH], preferred_element_type=F32).astype(BF16)
    values = jnp.dot(memory, memw[:, WIDTH:], preferred_element_type=F32).astype(BF16).astype(F32)
    raised = jnp.exp(jnp.dot(keys, queries, preferred_element_type=F32) * HSZ ** (-0.5))
    raised = raised.reshape(4, 64, 128)
    share = (raised / jnp.sum(raised, axis=0, keepdims=True)).astype(BF16).reshape(PLACES, 128)
    for q in range(NLAT):
        widen = equal(e_row, q * HEADS + e_lane // HSZ)
        wide = jnp.dot(share, widen, preferred_element_type=F32)
        mixed = jnp.sum((wide * values).reshape(4, 64, WIDTH), axis=0).astype(BF16)
        folded = jnp.dot(mixed, outw[...], preferred_element_type=F32) + lat_f[q : q + 1, :]
        folded = folded.astype(BF16)
        for r in range(2):
            out[0, r, q] = folded[r * 32 : (r + 1) * 32, :]

    for k in range(4):
        pl.when(not_me(comes[k]))(lambda k=k: fin_copy(k).wait_send())


def on_device(
    pixels, embed_weight, level_code, depth_kernel, norm_gain, up_weight, up_bias,
    down_weight, down_bias, fold_gain, latents, memory_weight, output_weight,
):
    vmem = pl.BlockSpec(memory_space=pltpu.VMEM)
    hbm = pl.BlockSpec(memory_space=pl.ANY)
    dma = pltpu.SemaphoreType.DMA
    result = pl.pallas_call(
        kernel,
        out_shape=jax.ShapeDtypeStruct((1, 2, NLAT, COLS, WIDTH), BF16),
        in_specs=[hbm] * 13,
        out_specs=vmem,
        scratch_shapes=[
            pltpu.VMEM((80, WIDTH), BF16),
            pltpu.VMEM((4, WIDTH), BF16),
            pltpu.VMEM((1, 25, 2, WIDTH), BF16),
            pltpu.VMEM((1, 2, WIDTH), BF16),
            pltpu.VMEM((1, 2, HIDDEN), BF16),
            pltpu.VMEM((1, 2, WIDTH), BF16),
            pltpu.VMEM((WIDTH,), BF16),
            pltpu.VMEM((NLAT, WIDTH), BF16),
            pltpu.VMEM((8, 5, 8, 128), BF16),
            pltpu.VMEM((NBLOCKS, 32, WIDTH), BF16),
            pltpu.VMEM((32, WIDTH), F32),
            pltpu.VMEM((NBLOCKS, WIDTH, HIDDEN), BF16),
            pltpu.VMEM((NBLOCKS, HIDDEN, WIDTH), BF16),
            pltpu.VMEM((WIDTH, 2 * WIDTH), BF16),
            pltpu.VMEM((WIDTH, WIDTH), BF16),
            pltpu.VMEM((4, PLACES, WIDTH), BF16),
            pltpu.VMEM((2 * NBLOCKS, 64, WIDTH), BF16),
            pltpu.VMEM((2 * NBLOCKS, 64, WIDTH), BF16),
            pltpu.VMEM((2, 8 * (COLS + 4) * 8, 128), F32),
            pltpu.VMEM((200, 128), F32),
            pltpu.VMEM((4 * COLS * 8, 128), F32),
            pltpu.VMEM((PLACES, WIDTH), F32),
            pltpu.VMEM((PLACES, HIDDEN), BF16),
            pltpu.VMEM((4, 128, 40), F32),
            pltpu.VMEM((8, 40, WIDTH), BF16),
            pltpu.VMEM((4, 64, WIDTH), BF16),
            dma((8,)), dma((8,)), dma((3,)), dma((3,)), dma((2, 2)), dma((2, 2)), dma((2, 2)),
            dma((2, 2)), dma((2, 2)), dma((2, 2, 3)), dma((2, 2, 3)), dma((2, 2)), dma((2, 2)),
            dma((2, 2 * NBLOCKS)), dma((2, 2 * NBLOCKS)), dma((4,)), dma((4,)), dma((2,)), dma((8,)),
            dma((2,)), dma((2,)),
        ],
        compiler_params=pltpu.CompilerParams(
            collective_id=0, has_side_effects=True, vmem_limit_bytes=62 * 1024 * 1024
        ),
    )(
        pixels, embed_weight, level_code, jnp.transpose(depth_kernel, (0, 2, 1, 3)),
        norm_gain, up_weight, up_bias, down_weight, down_bias, fold_gain, latents,
        memory_weight, output_weight,
    )
    return jnp.transpose(result, (0, 1, 3, 2, 4))


def solution(mesh):
    return jax.shard_map(
        on_device,
        mesh=mesh,
        in_specs=(
            P(None, None, None, "lat", None),
            P(),
            P(),
            P("segment", None, None, None),
            P("segment", None, None),
            P("segment", None, None, None),
            P("segment", None, None),
            P("segment", None, None, None),
            P("segment", None, None),
            P(),
            P(),
            P(),
            P(),
        ),
        out_specs=P("segment", "lat", None, None, None),
        check_vma=False,
    )
```

```python
import functools

import jax
import jax.numpy as jnp
from jax import lax
from jax.experimental import pallas as pl
from jax.experimental.pallas import tpu as pltpu
from jax.sharding import PartitionSpec as P

MESH = pl.DeviceIdType.MESH
F32 = jnp.float32
BF16 = jnp.bfloat16
EPSILON = 1e-06
ROWS = 8
COLS = 32
WIDTH = 512
HIDDEN = 1024
NBLOCKS = 8
PLACES = ROWS * COLS
HEADS = 16
HSZ = 32
NLAT = 3
PIECE = (0, 128, 192, 64)
ROW_AT = (0, 32, 128, 160, 192, 224, 64, 96)
MIRROR = 11


def dev(xh, xl, y, z, core):
    return (xh * 2 + core, y * 16 + xl * 8 + z)


def remote(src, dst, send, recv, target):
    return pltpu.make_async_remote_copy(
        src_ref=src, dst_ref=dst, send_sem=send, recv_sem=recv, device_id=target, device_id_type=MESH
    )


def normed_rows(x, gain):
    average = jnp.mean(x, axis=-1, keepdims=True)
    centred = x - average
    spread = jnp.mean(centred * centred, axis=-1, keepdims=True)
    return centred * lax.rsqrt(spread + EPSILON) * gain


def gelu(x):
    return 0.5 * x * (1.0 + lax.erf(x * (2.0**-0.5)))


def kernel(
    pixels, embed_weight, level_code, depth, gain, up, up_bias, down, down_bias,
    fold_gain, latents, memory_weight, output_weight,
    out,
    embw, codes, taps, gains, up_shift, down_shift, fold_scale, lats,
    pix, pack, pack_f, upw, downw, memw, outw, feat, top, bottom, padded, taps8, conv8, conv, hidden, gath, cellw, fold_in,
    pix_send, pix_recv, small_send, small_recv, own_load, sib_send, sib_recv,
    halo_send, halo_recv, fin_send, fin_recv, misc, load_sem, move_send, move_recv,
):
    loads = [
        pltpu.make_async_copy(source, target, load_sem.at[n])
        for n, (source, target) in enumerate(
            (
                (depth, taps), (gain, gains), (up_bias, up_shift), (down_bias, down_shift),
                (embed_weight, embw), (level_code, codes), (fold_gain, fold_scale), (latents, lats),
            )
        )
    ]
    for load in loads:
        load.start()
    seg = lax.axis_index("segment")
    lat = lax.axis_index("lat")
    xh, core = seg // 2, seg % 2
    y, xl, z = lat // 16, (lat // 8) % 2, lat % 8
    early, late = xh == 0, xh == 1
    level, bend = z % 4, (y + xh) % 2
    chip = 2 * y + (xl + bend) % 2
    band = 2 * chip + core
    has_up, has_down = band > 0, band < 15

    def of_band(n):
        return dev(xh, (n // 2 + n // 4 + xh) % 2, n // 4, z, n % 2)

    sibling = dev(xh, xl, y, z, 1 - core)
    partner = dev(1 - xh, 1 - xl, y, z, core)
    others = [sibling, partner]
    above = of_band(jnp.maximum(band - 1, 0))
    below = of_band(jnp.minimum(band + 1, 15))
    goes = [dev(xh, (xl + bend) % 2, y, core * 4 + l, z // 4) for l in range(4)]
    comes = [dev(xh, chip % 2, y, core * 4 + k, z // 4) for k in range(4)]
    folds = [[dev(image, chip % 2, y, core * 4 + k, z // 4) for k in range(4)] for image in range(2)]
    ends = [dev(1, (xl + y + 1) % 2, y, core * 4 + l, z // 4) for l in range(4)]

    def is_me(target):
        return (target[0] == seg) & (target[1] == lat)

    def not_me(target):
        return (target[0] != seg) | (target[1] != lat)

    barrier = pltpu.get_barrier_semaphore()

    def greet(target):
        pl.semaphore_signal(barrier, inc=1, device_id=target, device_id_type=MESH)

    for target in others:
        greet(target)
    expected = jnp.int32(6)
    for target in goes + comes:
        pl.when(not_me(target))(functools.partial(greet, target))
        expected = expected + not_me(target).astype(jnp.int32)
    for n in range(4):
        pl.when(early)(functools.partial(greet, ends[n]))
        pl.when(late)(functools.partial(greet, folds[0][n]))
    pl.when(has_up)(functools.partial(greet, above))
    pl.when(has_down)(functools.partial(greet, below))
    expected = expected + has_up.astype(jnp.int32) + has_down.astype(jnp.int32)

    my_slot = lat % 4

    def micro(image):
        return core + 2 * image

    def pix_copy(image, l):
        at = 4 * image + my_slot
        return remote(
            pixels.at[micro(image), l], pix.at[at], pix_send.at[4 * image + l], pix_recv.at[at], goes[l]
        )

    def pix_local(image, l):
        at = 4 * image + my_slot
        return pltpu.make_async_copy(pixels.at[micro(image), l], pix.at[at], pix_recv.at[at])

    def pix_wait(image, k):
        at = 4 * image + k
        remote(pixels.at[0, 0], pix.at[at], pix_send.at[0], pix_recv.at[at], comes[k]).wait_recv()

    mine = 2 * seg
    sib_first = 2 * (xh * 2 + (1 - core))

    def store(ud):
        return (upw, downw)[ud]

    def given(ud):
        return (up, down)[ud]

    def own_copy(i, ud):
        return pltpu.make_async_copy(given(ud).at[0, i], store(ud).at[mine + i], own_load.at[i, ud])

    def sib_copy(i, ud):
        return remote(given(ud).at[0, i], store(ud).at[mine + i], sib_send.at[i, ud], sib_recv.at[i, ud], sibling)

    def sib_arrives(i, ud):
        remote(given(ud).at[0, i], store(ud).at[sib_first + i], sib_send.at[i, ud], sib_recv.at[i, ud], sibling).wait_recv()

    KINDS = [(0, 0), (0, 1), (1, 0), (1, 1)]

    for i, ud in KINDS:
        own_copy(i, ud).start()
    load_mem = pltpu.make_async_copy(memory_weight, memw, misc.at[0])
    load_out = pltpu.make_async_copy(output_weight, outw, misc.at[1])
    load_mem.start()
    load_out.start()

    for load in loads:
        load.wait()
    for i in range(2):
        pack_f[0:25] = taps[0, :, i, :].astype(F32)
        pack_f[25:26] = gains[0, i : i + 1, :].astype(F32)
        pack_f[26:27] = up_shift[0, i : i + 1, :WIDTH].astype(F32)
        pack_f[27:28] = up_shift[0, i : i + 1, WIDTH:].astype(F32)
        pack_f[28:29] = down_shift[0, i : i + 1, :].astype(F32)
        pack_f[29:32] = jnp.zeros((3, WIDTH), F32)
        pack[mine + i] = pack_f[...].astype(BF16)

    def small_copy():
        part = pack.at[pl.ds(mine, 2)]
        return remote(part, part, small_send.at[0], small_recv.at[0], sibling)

    def small_arrives():
        part = pack.at[pl.ds(sib_first, 2)]
        remote(part, part, small_send.at[0], small_recv.at[0], sibling).wait_recv()

    grid5 = padded.reshape(2, 8, COLS + 4, 8, 128)
    for image in range(2):
        grid5[image, :, 0:2] = jnp.zeros((8, 2, 8, 128), F32)
        grid5[image, :, COLS + 2 :] = jnp.zeros((8, 2, 8, 128), F32)

    def place(image, padded_row, values):
        for flip in range(2):
            p = MIRROR - padded_row if flip else padded_row
            if p < 8:
                for c in range(0, COLS, 8):
                    for g in range(4):
                        start = (p * (COLS + 4) + 2 + c) * 8 + flip * 4 + g
                        padded[image, pl.ds(start, 8, stride=8), :] = values[c : c + 8, g * 128 : g * 128 + 128]

    def equal(a, b):
        return jnp.where(a == b, 1.0, 0.0).astype(BF16)

    rho = lax.broadcasted_iota(jnp.int32, (128, 128), 0)
    lon = lax.broadcasted_iota(jnp.int32, (128, 128), 1)
    pick = equal(lon, 4 * (rho % 32) + rho // 32)
    row = lax.broadcasted_iota(jnp.int32, (40, 80), 0)
    col = lax.broadcasted_iota(jnp.int32, (40, 80), 1)
    source_col = ((row // 8) * 4 + row % 4) * 4
    half = (row // 4) % 2
    @pl.when(early)
    def _():
        for r2 in range(2):
            for j in range(4):
                choose = equal(jnp.where(half == r2, source_col + j, -1), col)
                part = jnp.dot(choose, embw[...], preferred_element_type=F32)
                cellw[4 * r2 + j] = part.astype(BF16)

    for image in range(2):
        @pl.when(jnp.logical_not(has_up))
        def _():
            for r in range(2):
                place(image, r, jnp.zeros((COLS, WIDTH), F32))

        @pl.when(jnp.logical_not(has_down))
        def _():
            for r in range(2):
                place(image, ROWS + 2 + r, jnp.zeros((COLS, WIDTH), F32))

    pl.semaphore_wait(barrier, expected)

    @pl.when(early)
    def _():
        for image in (1, 0):
            for l in range(4):
                pl.when(not_me(goes[l]))(lambda: pix_copy(image, l).start())
                pl.when(is_me(goes[l]))(lambda: pix_local(image, l).start())

    small_copy().start()
    for ud in range(2):
        sib_copy(0, ud).start()

    def embed(image):
        for k in range(4):
            pix_wait(image, k)
        for k in range(4):
            cells = pix[4 * image + k].astype(F32).reshape(40, 128).astype(BF16)
            picked = lax.dot_general(pick, cells, (((1,), (1,)), ((), ())), preferred_element_type=F32)
            for j in range(4):
                gath[j, k * 32 : (k + 1) * 32, :] = picked[j * 32 : (j + 1) * 32, :]
        level_row = lax.broadcasted_iota(jnp.int32, (4, WIDTH), 0)
        code = jnp.sum(jnp.where(level_row == level, codes[...].astype(F32), 0.0), axis=0, keepdims=True)
        for r2 in range(2):
            total = jnp.zeros((128, WIDTH), F32)
            for j in range(4):
                total = total + jnp.dot(gath[j].astype(BF16), cellw[4 * r2 + j], preferred_element_type=F32)
            total = (total + code).astype(BF16)
            for k in range(4):
                piece = total[k * 32 : (k + 1) * 32, :]
                start = PIECE[k] + r2 * 32
                feat[2 * image, start : start + 32, :] = piece
                place(image, 2 + 2 * k + r2, piece.astype(F32))

    def halo_up(image, h, slot):
        at = NBLOCKS * image + h
        source = feat.at[2 * image + slot, pl.ds(0, 64)]
        return remote(source, bottom.at[at], halo_send.at[0, at], halo_recv.at[0, at], above)

    def halo_down(image, h, slot):
        at = NBLOCKS * image + h
        source = feat.at[2 * image + slot, pl.ds(64, 64)]
        return remote(source, top.at[at], halo_send.at[1, at], halo_recv.at[1, at], below)

    def send_halos(image, h, slot):
        pl.when(has_up)(lambda: halo_up(image, h, slot).start())
        pl.when(has_down)(lambda: halo_down(image, h, slot).start())

    def halos_sent(image, h, slot):
        pl.when(has_up)(lambda: halo_up(image, h, slot).wait_send())
        pl.when(has_down)(lambda: halo_down(image, h, slot).wait_send())

    def move_copy(image, part):
        rows = feat.at[2 * image, pl.ds(128 * part, 128)]
        return remote(rows, rows, move_send.at[image, part], move_recv.at[image, part], partner)

    def move_arrives(image, part):
        move_copy(image, part).wait_recv()
        for r in range(ROWS):
            if ROW_AT[r] // 128 == part:
                place(image, 2 + r, feat[2 * image, ROW_AT[r] : ROW_AT[r] + 32, :].astype(F32))

    @pl.when(early)
    def _():
        for image in (1, 0):
            embed(image)
            send_halos(image, 0, 0)

    @pl.when(late)
    def _():
        move_arrives(1, 0)
        send_halos(1, 4, 0)
        move_arrives(1, 1)

    def conv_rows(image, first, lines, drain):
        def columns(step, _):
            base = step * 8
            sums = [[None] * 8 for _ in range(2)]
            at = [[pl.ds(pl.multiple_of(((first + r) * COLS + q) * 8 + base * 8, 8), 8) for q in range(8)] for r in range(2)]
            if lines[0] < 2:
                sums = [[conv8[at[r][q], :] for q in range(8)] for r in range(2)]
            for p in lines:
                for c in range(12):
                    value = padded[image, pl.ds(pl.multiple_of((p * (COLS + 4) + c) * 8 + base * 8, 8), 8), :]
                    for r in range(2):
                        i = p - first - r
                        for j in range(5):
                            if 0 <= i < 5 and 0 <= c - j < 8:
                                term = value * taps8[8 * (5 * i + j) : 8 * (5 * i + j) + 8, :]
                                old = sums[r][c - j]
                                sums[r][c - j] = term if old is None else old + term
            for r in range(2):
                for q in range(8):
                    conv8[at[r][q], :] = sums[r][q]
            return 0

        lax.fori_loop(0, COLS // 8, columns, 0)
        for r in (first, first + 1, 7 - first, 6 - first) if drain else ():
            flip = r > 3
            line = 7 - r if flip else r
            for c in range(0, COLS, 8):
                for g in range(4):
                    start = (line * COLS + c) * 8 + flip * 4 + g
                    at = ROW_AT[r] + c
                    conv[at : at + 8, g * 128 : g * 128 + 128] = conv8[pl.ds(start, 8, stride=8), :]

    def fin_copy(image, k):
        source = feat.at[2 * image, pl.ds(PIECE[k], 64)]
        return remote(source, fold_in.at[level], fin_send.at[image, k], fin_recv.at[level], folds[image][k])

    def fin_local(image, k):
        source = feat.at[2 * image, pl.ds(PIECE[k], 64)]
        return pltpu.make_async_copy(source, fold_in.at[level], fin_recv.at[level])

    def finish(image, k):
        pl.when(not_me(folds[image][k]))(lambda: fin_copy(image, k).start())
        pl.when(is_me(folds[image][k]))(lambda: fin_local(image, k).start())

    def leave(part, b_is_final, image_is):
        for n in range(2):
            @pl.when((b_is_final) & (image_is == n))
            def _():
                pl.when(early)(lambda: move_copy(n, part).start())

                @pl.when(late)
                def _():
                    for k in ((0, 3), (1, 2))[part]:
                        finish(n, k)

    def block(step, _):
        image = 1 - step % 2
        b = 4 * xh + step // 2
        slot = b % 2
        other = 1 - slot
        i = b % 2
        near = b // 2 == seg
        last = step >= 6
        pl.when((image == 1) & (i == 0) & jnp.logical_not(near))(small_arrives)
        pack_f[...] = pack[b].astype(F32)
        for n in range(5):
            for g in range(4):
                five = pack_f[5 * n : 5 * n + 5, g * 128 : g * 128 + 128]
                taps8[pl.ds(40 * n + g, 5, stride=8), :] = five
                taps8[pl.ds(40 * (4 - n) + 4 + g, 5, stride=8), :] = five
        conv_rows(image, 2, range(2, 8), True)
        conv_rows(image, 0, range(2, 6), False)

        @pl.when(step == 0)
        def _():
            for ud in range(2):
                sib_copy(1, ud).start()

            @pl.when(late)
            def _():
                move_arrives(0, 0)
                send_halos(0, 4, 0)

        def settle(test, arrives):
            for n in range(2):
                for ud in range(2):
                    pl.when(test & (image == 1) & (i == n))(functools.partial(arrives, n, ud))

        settle(near, lambda n, ud: own_copy(n, ud).wait())
        settle(jnp.logical_not(near), sib_arrives)

        @pl.when(has_up)
        def _():
            halo_down(image, b, slot).wait_recv()
            for r in range(2):
                place(image, r, top[NBLOCKS * image + b, r * 32 : r * 32 + 32, :].astype(F32))

        @pl.when(has_down)
        def _():
            halo_up(image, b, slot).wait_recv()
            for r in range(2):
                place(image, ROWS + 2 + r, bottom[NBLOCKS * image + b, r * 32 : r * 32 + 32, :].astype(F32))

        conv_rows(image, 0, range(2), True)

        def pointwise(first, count):
            part_rows = slice(first, first + count)
            normed = normed_rows(conv[part_rows, :], pack_f[25:26, :]).astype(BF16)
            for n in range(2):
                at = pl.ds(n * WIDTH, WIDTH)
                raised = jnp.dot(normed, upw[b, :, at], preferred_element_type=F32)
                hidden[0:count, at] = gelu(raised + pack_f[26 + n : 27 + n, :]).astype(BF16)
            branch = jnp.dot(hidden[0:count, :], downw[b], preferred_element_type=F32)
            old = feat[2 * image + slot, part_rows, :].astype(F32)
            new = (old + (branch + pack_f[28:29, :])).astype(BF16)
            feat[2 * image + other, part_rows, :] = new
            wide = new.astype(F32)
            for r in range(ROWS):
                if first <= ROW_AT[r] < first + count:
                    place(image, 2 + r, wide[ROW_AT[r] - first : ROW_AT[r] - first + 32, :])

        @pl.when(step > 1)
        def _():
            halos_sent(image, b - 1, other)

        whole = step < 6
        pl.when(whole)(lambda: pointwise(0, PLACES))
        pl.when(jnp.logical_not(whole))(lambda: pointwise(0, PLACES // 2))

        @pl.when(jnp.logical_not(last))
        def _():
            send_halos(image, b + 1, other)

        leave(0, last, image)
        pl.when(jnp.logical_not(whole))(lambda: pointwise(PLACES // 2, PLACES // 2))
        leave(1, last, image)
        pl.when(late & (step == 0))(lambda: move_arrives(0, 1))
        return 0

    lax.fori_loop(0, 8, block, 0)

    small_copy().wait_send()
    for i, ud in KINDS:
        sib_copy(i, ud).wait_send()
    for image in range(2):
        halos_sent(image, 4 * xh + 3, 1)

    @pl.when(early)
    def _():
        for image in range(2):
            for l in range(4):
                pl.when(not_me(goes[l]))(lambda: pix_copy(image, l).wait_send())
            for part in range(2):
                move_copy(image, part).wait_send()

    load_mem.wait()
    load_out.wait()

    lane = lax.broadcasted_iota(jnp.int32, (8, 128), 1)
    query = lax.broadcasted_iota(jnp.int32, (8, 128), 0)
    heads_of = equal(jnp.where(lane < HEADS * NLAT, lane // HEADS, -1), query)
    lat_f = jnp.concatenate([lats[...].astype(F32), jnp.zeros((5, WIDTH), F32)], axis=0)
    spread = jnp.dot(lat_f.T.astype(BF16), heads_of, preferred_element_type=F32)
    d_row = lax.broadcasted_iota(jnp.int32, (WIDTH, 128), 0)
    d_lane = lax.broadcasted_iota(jnp.int32, (WIDTH, 128), 1)
    queries = jnp.where(d_row // HSZ == d_lane % HEADS, spread, 0.0).astype(BF16)
    e_row = lax.broadcasted_iota(jnp.int32, (128, WIDTH), 0)
    e_lane = lax.broadcasted_iota(jnp.int32, (128, WIDTH), 1)

    for l in range(4):
        remote(feat.at[0, pl.ds(0, 64)], fold_in.at[l], fin_send.at[0, 0], fin_recv.at[l], ends[l]).wait_recv()

    memory = normed_rows(
        fold_in[...].astype(F32).reshape(PLACES, WIDTH), fold_scale[...].astype(F32)
    ).astype(BF16)
    keys = jnp.dot(memory, memw[:, :WIDTH], preferred_element_type=F32).astype(BF16)
    values = jnp.dot(memory, memw[:, WIDTH:], preferred_element_type=F32).astype(BF16).astype(F32)
    raised = jnp.exp(jnp.dot(keys, queries, preferred_element_type=F32) * HSZ ** (-0.5))
    raised = raised.reshape(4, 64, 128)
    share = (raised / jnp.sum(raised, axis=0, keepdims=True)).astype(BF16).reshape(PLACES, 128)
    for q in range(NLAT):
        widen = equal(e_row, q * HEADS + e_lane // HSZ)
        wide = jnp.dot(share, widen, preferred_element_type=F32)
        mixed = jnp.sum((wide * values).reshape(4, 64, WIDTH), axis=0).astype(BF16)
        folded = jnp.dot(mixed, outw[...], preferred_element_type=F32) + lat_f[q : q + 1, :]
        folded = folded.astype(BF16)
        for r in range(2):
            out[0, r, q] = folded[r * 32 : (r + 1) * 32, :]

    @pl.when(late)
    def _():
        for image in range(2):
            for k in range(4):
                pl.when(not_me(folds[image][k]))(lambda: fin_copy(image, k).wait_send())


def on_device(
    pixels, embed_weight, level_code, depth_kernel, norm_gain, up_weight, up_bias,
    down_weight, down_bias, fold_gain, latents, memory_weight, output_weight,
):
    vmem = pl.BlockSpec(memory_space=pltpu.VMEM)
    hbm = pl.BlockSpec(memory_space=pl.ANY)
    dma = pltpu.SemaphoreType.DMA
    result = pl.pallas_call(
        kernel,
        out_shape=jax.ShapeDtypeStruct((1, 2, NLAT, COLS, WIDTH), BF16),
        in_specs=[hbm] * 13,
        out_specs=vmem,
        scratch_shapes=[
            pltpu.VMEM((80, WIDTH), BF16),
            pltpu.VMEM((4, WIDTH), BF16),
            pltpu.VMEM((1, 25, 2, WIDTH), BF16),
            pltpu.VMEM((1, 2, WIDTH), BF16),
            pltpu.VMEM((1, 2, HIDDEN), BF16),
            pltpu.VMEM((1, 2, WIDTH), BF16),
            pltpu.VMEM((WIDTH,), BF16),
            pltpu.VMEM((NLAT, WIDTH), BF16),
            pltpu.VMEM((8, 5, 8, 128), BF16),
            pltpu.VMEM((NBLOCKS, 32, WIDTH), BF16),
            pltpu.VMEM((32, WIDTH), F32),
            pltpu.VMEM((NBLOCKS, WIDTH, HIDDEN), BF16),
            pltpu.VMEM((NBLOCKS, HIDDEN, WIDTH), BF16),
            pltpu.VMEM((WIDTH, 2 * WIDTH), BF16),
            pltpu.VMEM((WIDTH, WIDTH), BF16),
            pltpu.VMEM((4, PLACES, WIDTH), BF16),
            pltpu.VMEM((2 * NBLOCKS, 64, WIDTH), BF16),
            pltpu.VMEM((2 * NBLOCKS, 64, WIDTH), BF16),
            pltpu.VMEM((2, 8 * (COLS + 4) * 8, 128), F32),
            pltpu.VMEM((200, 128), F32),
            pltpu.VMEM((4 * COLS * 8, 128), F32),
            pltpu.VMEM((PLACES, WIDTH), F32),
            pltpu.VMEM((PLACES, HIDDEN), BF16),
            pltpu.VMEM((4, 128, 40), F32),
            pltpu.VMEM((8, 40, WIDTH), BF16),
            pltpu.VMEM((4, 64, WIDTH), BF16),
            dma((8,)), dma((8,)), dma((1,)), dma((1,)), dma((2, 2)), dma((2, 2)), dma((2, 2)),
            dma((2, 2 * NBLOCKS)), dma((2, 2 * NBLOCKS)), dma((2, 4)), dma((4,)), dma((2,)), dma((8,)),
            dma((2, 2)), dma((2, 2)),
        ],
        compiler_params=pltpu.CompilerParams(
            collective_id=0, has_side_effects=True, vmem_limit_bytes=62 * 1024 * 1024
        ),
    )(
        pixels, embed_weight, level_code, jnp.transpose(depth_kernel, (0, 2, 1, 3)),
        norm_gain, up_weight, up_bias, down_weight, down_bias, fold_gain, latents,
        memory_weight, output_weight,
    )
    return jnp.transpose(result, (0, 1, 3, 2, 4))


def solution(mesh):
    return jax.shard_map(
        on_device,
        mesh=mesh,
        in_specs=(
            P(None, None, None, "lat", None),
            P(),
            P(),
            P("segment", None, None, None),
            P("segment", None, None),
            P("segment", None, None, None),
            P("segment", None, None),
            P("segment", None, None, None),
            P("segment", None, None),
            P(),
            P(),
            P(),
            P(),
        ),
        out_specs=P("segment", "lat", None, None, None),
        check_vma=False,
    )
```

```python
import functools

import jax
import jax.numpy as jnp
from jax import lax
from jax.experimental import pallas as pl
from jax.experimental.pallas import tpu as pltpu
from jax.sharding import PartitionSpec as P

MESH = pl.DeviceIdType.MESH
F32 = jnp.float32
BF16 = jnp.bfloat16
EPSILON = 1e-06
ROWS = 8
COLS = 32
WIDTH = 512
HIDDEN = 1024
NBLOCKS = 8
PLACES = ROWS * COLS
HEADS = 16
HSZ = 32
NLAT = 3
PIECE = (0, 128, 192, 64)
ROW_AT = (0, 32, 128, 160, 192, 224, 64, 96)
MIRROR = 11


def dev(xh, xl, y, z, core):
    return (xh * 2 + core, y * 16 + xl * 8 + z)


def remote(src, dst, send, recv, target):
    return pltpu.make_async_remote_copy(
        src_ref=src, dst_ref=dst, send_sem=send, recv_sem=recv, device_id=target, device_id_type=MESH
    )


def normed_rows(x, gain):
    average = jnp.mean(x, axis=-1, keepdims=True)
    centred = x - average
    spread = jnp.mean(centred * centred, axis=-1, keepdims=True)
    return centred * lax.rsqrt(spread + EPSILON) * gain


def gelu(x):
    return 0.5 * x * (1.0 + lax.erf(x * (2.0**-0.5)))


def kernel(
    pixels, embed_weight, level_code, depth, gain, up, up_bias, down, down_bias,
    fold_gain, latents, memory_weight, output_weight,
    out,
    embw, codes, taps, gains, up_shift, down_shift, fold_scale, lats,
    pix, pack, pack_f, upw, downw, memw, outw, feat, top, bottom, padded, taps8, conv8, conv, hidden, gath, cellw, fold_in,
    pix_send, pix_recv, small_send, small_recv, own_load, sib_send, sib_recv,
    bnd_send, bnd_recv, fwd_send, fwd_recv, sibf_send, sibf_recv,
    halo_send, halo_recv, fin_send, fin_recv, misc, load_sem, move_send, move_recv,
):
    loads = [
        pltpu.make_async_copy(source, target, load_sem.at[n])
        for n, (source, target) in enumerate(
            (
                (depth, taps), (gain, gains), (up_bias, up_shift), (down_bias, down_shift),
                (embed_weight, embw), (level_code, codes), (fold_gain, fold_scale), (latents, lats),
            )
        )
    ]
    for load in loads:
        load.start()
    seg = lax.axis_index("segment")
    lat = lax.axis_index("lat")
    xh, core = seg // 2, seg % 2
    y, xl, z = lat // 16, (lat // 8) % 2, lat % 8
    early, late = xh == 0, xh == 1
    level, bend = z % 4, (y + xh) % 2
    chip = 2 * y + (xl + bend) % 2
    band = 2 * chip + core
    has_up, has_down = band > 0, band < 15

    def of_band(n):
        return dev(xh, (n // 2 + n // 4 + xh) % 2, n // 4, z, n % 2)

    sibling = dev(xh, xl, y, z, 1 - core)
    partner = dev(1 - xh, 1 - xl, y, z, core)
    crossed = dev(1 - xh, 1 - xl, y, z, 1 - core)
    odd = 2 * (y % 2)
    flipped = jnp.where((xl + xh) % 2 == 0, y + 1 - odd, (y + 3 + odd) % 4)
    ring = [
        dev(xh, xl, y, (z + 1) % 8, core),
        dev(xh, xl, y, (z + 7) % 8, core),
        dev(xh, xl, flipped, z, core),
    ]
    others = [sibling, partner, crossed]
    above = of_band(jnp.maximum(band - 1, 0))
    below = of_band(jnp.minimum(band + 1, 15))
    goes = [dev(xh, (xl + bend) % 2, y, core * 4 + l, z // 4) for l in range(4)]
    comes = [dev(xh, chip % 2, y, core * 4 + k, z // 4) for k in range(4)]

    def is_me(target):
        return (target[0] == seg) & (target[1] == lat)

    def not_me(target):
        return (target[0] != seg) | (target[1] != lat)

    barrier = pltpu.get_barrier_semaphore()

    def greet(target):
        pl.semaphore_signal(barrier, inc=1, device_id=target, device_id_type=MESH)

    for target in ring + others:
        greet(target)
    expected = jnp.int32(6)
    for target in goes + comes:
        pl.when(not_me(target))(functools.partial(greet, target))
        expected = expected + not_me(target).astype(jnp.int32)
    pl.when(has_up)(functools.partial(greet, above))
    pl.when(has_down)(functools.partial(greet, below))
    expected = expected + has_up.astype(jnp.int32) + has_down.astype(jnp.int32)

    my_slot = lat % 4

    def micro(image):
        return core + 2 * image

    def pix_copy(image, l):
        at = 4 * image + my_slot
        return remote(
            pixels.at[micro(image), l], pix.at[at], pix_send.at[4 * image + l], pix_recv.at[at], goes[l]
        )

    def pix_local(image, l):
        at = 4 * image + my_slot
        return pltpu.make_async_copy(pixels.at[micro(image), l], pix.at[at], pix_recv.at[at])

    def pix_wait(image, k):
        at = 4 * image + k
        remote(pixels.at[0, 0], pix.at[at], pix_send.at[0], pix_recv.at[at], comes[k]).wait_recv()

    quarter = (z + 2 * (y % 2)) % 4
    mine = 2 * seg
    far, far_sib = 4 + core, 5 - core
    sib_first = 2 * (xh * 2 + (1 - core))

    def store(ud):
        return (upw, downw)[ud]

    def given(ud):
        return (up, down)[ud]

    def span(ud, q):
        rows = (128, 256)[ud]
        return pl.ds(pl.multiple_of(q * rows, rows), rows)

    def own_copy(i, ud):
        return pltpu.make_async_copy(given(ud).at[0, i], store(ud).at[mine + i], own_load.at[i, ud])

    def sib_copy(i, ud):
        return remote(given(ud).at[0, i], store(ud).at[mine + i], sib_send.at[i, ud], sib_recv.at[i, ud], sibling)

    def sib_arrives(i, ud):
        remote(given(ud).at[0, i], store(ud).at[sib_first + i], sib_send.at[i, ud], sib_recv.at[i, ud], sibling).wait_recv()

    def bnd_copy(i, ud):
        whole = store(ud).at[far + 2 * i]
        part = whole if i else store(ud).at[far, span(ud, quarter)]
        return remote(part, part, bnd_send.at[i, ud], bnd_recv.at[i, ud], partner)

    def far_part(i, ud, q):
        return store(ud).at[far + 2 * i, span(ud, q)]

    def bnd_arrives(i, ud):
        bnd_copy(i, ud).wait_recv()

    def fwd_copy(i, ud, r):
        part = far_part(i, ud, quarter)
        return remote(part, part, fwd_send.at[i, ud, r], fwd_recv.at[i, ud, r], ring[r])

    def fwd_arrives(i, ud, r):
        part = far_part(i, ud, (quarter + (3, 1, 2)[r]) % 4)
        remote(part, part, fwd_send.at[i, ud, r], fwd_recv.at[i, ud, r], ring[r]).wait_recv()

    def sibf_copy(i, ud):
        whole = store(ud).at[far + 2 * i]
        return remote(whole, whole, sibf_send.at[i, ud], sibf_recv.at[i, ud], sibling)

    def sibf_arrives(i, ud):
        whole = store(ud).at[far_sib + 2 * i]
        remote(whole, whole, sibf_send.at[i, ud], sibf_recv.at[i, ud], sibling).wait_recv()

    def forward(i, ud):
        bnd_arrives(i, ud)
        for r in range(3):
            fwd_copy(i, ud, r).start()

    def hand_over(i, ud):
        if i:
            bnd_arrives(i, ud)
        else:
            for r in range(3):
                fwd_arrives(i, ud, r)
        sibf_copy(i, ud).start()

    def by_core(first, second):
        return jnp.where(early, jnp.where(core == 0, first, second), -9)

    def when(step, part):
        return 3 * step + part

    pt_fwd = {
        (0, 0): by_core(when(1, 2), when(1, 2)), (0, 1): by_core(when(3, 2), when(3, 2)),
    }
    pt_hand = {
        (0, 0): by_core(when(4, 2), when(4, 2)), (0, 1): by_core(when(6, 2), when(6, 2)),
        (1, 0): by_core(when(9, 2), when(9, 2)), (1, 1): by_core(when(9, 2), when(10, 2)),
    }
    pt_sib = {
        (0, 0): by_core(-1, -1), (0, 1): by_core(-1, -1),
        (1, 0): by_core(when(0, 1), when(0, 1)), (1, 1): by_core(when(0, 1), when(0, 1)),
    }
    KINDS = [(0, 0), (0, 1), (1, 0), (1, 1)]

    def service(point):
        for i, ud in KINDS:
            pl.when(pt_sib[i, ud] == point)(lambda i=i, ud=ud: sib_copy(i, ud).start())
        for i, ud in KINDS[:2]:
            pl.when(pt_fwd[i, ud] == point)(functools.partial(forward, i, ud))
        for i, ud in KINDS:
            pl.when(pt_hand[i, ud] == point)(functools.partial(hand_over, i, ud))

    for i, ud in KINDS:
        own_copy(i, ud).start()
    load_mem = pltpu.make_async_copy(memory_weight, memw, misc.at[0])
    load_out = pltpu.make_async_copy(output_weight, outw, misc.at[1])
    load_mem.start()
    load_out.start()

    for load in loads:
        load.wait()
    for i in range(2):
        pack_f[0:25] = taps[0, :, i, :].astype(F32)
        pack_f[25:26] = gains[0, i : i + 1, :].astype(F32)
        pack_f[26:27] = up_shift[0, i : i + 1, :WIDTH].astype(F32)
        pack_f[27:28] = up_shift[0, i : i + 1, WIDTH:].astype(F32)
        pack_f[28:29] = down_shift[0, i : i + 1, :].astype(F32)
        pack_f[29:32] = jnp.zeros((3, WIDTH), F32)
        pack[mine + i] = pack_f[...].astype(BF16)

    def small_copy(k):
        part = pack.at[pl.ds(mine, 2)]
        return remote(part, part, small_send.at[k], small_recv.at[k], others[k])

    def small_from(k):
        return (xh * 2 + (1 - core), (1 - xh) * 2 + core, (1 - xh) * 2 + (1 - core))[k]

    def small_arrives(k):
        part = pack.at[pl.ds(2 * small_from(k), 2)]
        remote(part, part, small_send.at[k], small_recv.at[k], others[k]).wait_recv()

    grid5 = padded.reshape(2, 8, COLS + 4, 8, 128)
    for image in range(2):
        grid5[image, :, 0:2] = jnp.zeros((8, 2, 8, 128), F32)
        grid5[image, :, COLS + 2 :] = jnp.zeros((8, 2, 8, 128), F32)

    def place(image, padded_row, values):
        for flip in range(2):
            p = MIRROR - padded_row if flip else padded_row
            if p < 8:
                for c in range(0, COLS, 8):
                    for g in range(4):
                        start = (p * (COLS + 4) + 2 + c) * 8 + flip * 4 + g
                        padded[image, pl.ds(start, 8, stride=8), :] = values[c : c + 8, g * 128 : g * 128 + 128]

    def equal(a, b):
        return jnp.where(a == b, 1.0, 0.0).astype(BF16)

    rho = lax.broadcasted_iota(jnp.int32, (128, 128), 0)
    lon = lax.broadcasted_iota(jnp.int32, (128, 128), 1)
    pick = equal(lon, 4 * (rho % 32) + rho // 32)
    row = lax.broadcasted_iota(jnp.int32, (40, 80), 0)
    col = lax.broadcasted_iota(jnp.int32, (40, 80), 1)
    source_col = ((row // 8) * 4 + row % 4) * 4
    half = (row // 4) % 2
    @pl.when(early)
    def _():
        for r2 in range(2):
            for j in range(4):
                choose = equal(jnp.where(half == r2, source_col + j, -1), col)
                part = jnp.dot(choose, embw[...], preferred_element_type=F32)
                cellw[4 * r2 + j] = part.astype(BF16)

    for image in range(2):
        @pl.when(jnp.logical_not(has_up))
        def _():
            for r in range(2):
                place(image, r, jnp.zeros((COLS, WIDTH), F32))

        @pl.when(jnp.logical_not(has_down))
        def _():
            for r in range(2):
                place(image, ROWS + 2 + r, jnp.zeros((COLS, WIDTH), F32))

    pl.semaphore_wait(barrier, expected)

    @pl.when(early)
    def _():
        for image in (1, 0):
            for l in range(4):
                pl.when(not_me(goes[l]))(lambda: pix_copy(image, l).start())
                pl.when(is_me(goes[l]))(lambda: pix_local(image, l).start())

    small_copy(0).start()
    service(-1)

    def embed(image):
        for k in range(4):
            pix_wait(image, k)
        for k in range(4):
            cells = pix[4 * image + k].astype(F32).reshape(40, 128).astype(BF16)
            picked = lax.dot_general(pick, cells, (((1,), (1,)), ((), ())), preferred_element_type=F32)
            for j in range(4):
                gath[j, k * 32 : (k + 1) * 32, :] = picked[j * 32 : (j + 1) * 32, :]
        level_row = lax.broadcasted_iota(jnp.int32, (4, WIDTH), 0)
        code = jnp.sum(jnp.where(level_row == level, codes[...].astype(F32), 0.0), axis=0, keepdims=True)
        for r2 in range(2):
            total = jnp.zeros((128, WIDTH), F32)
            for j in range(4):
                total = total + jnp.dot(gath[j].astype(BF16), cellw[4 * r2 + j], preferred_element_type=F32)
            total = (total + code).astype(BF16)
            for k in range(4):
                piece = total[k * 32 : (k + 1) * 32, :]
                start = PIECE[k] + r2 * 32
                feat[2 * image, start : start + 32, :] = piece
                place(image, 2 + 2 * k + r2, piece.astype(F32))

    def halo_up(image, h, slot):
        at = NBLOCKS * image + h
        source = feat.at[2 * image + slot, pl.ds(0, 64)]
        return remote(source, bottom.at[at], halo_send.at[0, at], halo_recv.at[0, at], above)

    def halo_down(image, h, slot):
        at = NBLOCKS * image + h
        source = feat.at[2 * image + slot, pl.ds(64, 64)]
        return remote(source, top.at[at], halo_send.at[1, at], halo_recv.at[1, at], below)

    def send_halos(image, h, slot):
        pl.when(has_up)(lambda: halo_up(image, h, slot).start())
        pl.when(has_down)(lambda: halo_down(image, h, slot).start())

    def halos_sent(image, h, slot):
        pl.when(has_up)(lambda: halo_up(image, h, slot).wait_send())
        pl.when(has_down)(lambda: halo_down(image, h, slot).wait_send())

    def move_copy(part):
        rows = pl.ds(128 * part, 128)
        return remote(feat.at[2, rows], feat.at[0, rows], move_send.at[part], move_recv.at[part], partner)

    def move_arrives(part):
        move_copy(part).wait_recv()
        rows = (0, 1, 6, 7, 2, 3, 4, 5)[4 * part : 4 * part + 4]
        for n, r in enumerate(rows):
            start = ROW_AT[r]
            place(0, 2 + r, feat[0, start : start + 32, :].astype(F32))

    @pl.when(early)
    def _():
        for image in (1, 0):
            embed(image)
            send_halos(image, 0, 0)

    @pl.when(late)
    def _():
        for i, ud in KINDS[2:] + KINDS[:2]:
            sib_copy(i, ud).start()
        for i, ud in KINDS:
            own_copy(i, ud).wait()
        for ud in range(2):
            pl.when(core == 1)(functools.partial(sib_arrives, 1, ud))
            bnd_copy(0, ud).start()
            bnd_copy(0, ud).wait_send()
        for k in (1, 2):
            small_copy(k).start()
        for ud in range(2):
            sib_arrives(0, ud)
            pl.when(core == 0)(functools.partial(sib_arrives, 1, ud))
        bnd_copy(1, 0).start()
        pl.when(core == 0)(lambda: bnd_copy(1, 1).start())
        move_arrives(0)
        send_halos(0, 4, 0)
        move_arrives(1)

    def conv_rows(image, first, lines, drain):
        def columns(step, _):
            base = step * 8
            sums = [[None] * 8 for _ in range(2)]
            at = [[pl.ds(pl.multiple_of(((first + r) * COLS + q) * 8 + base * 8, 8), 8) for q in range(8)] for r in range(2)]
            if lines[0] < 2:
                sums = [[conv8[at[r][q], :] for q in range(8)] for r in range(2)]
            for p in lines:
                for c in range(12):
                    value = padded[image, pl.ds(pl.multiple_of((p * (COLS + 4) + c) * 8 + base * 8, 8), 8), :]
                    for r in range(2):
                        i = p - first - r
                        for j in range(5):
                            if 0 <= i < 5 and 0 <= c - j < 8:
                                term = value * taps8[8 * (5 * i + j) : 8 * (5 * i + j) + 8, :]
                                old = sums[r][c - j]
                                sums[r][c - j] = term if old is None else old + term
            for r in range(2):
                for q in range(8):
                    conv8[at[r][q], :] = sums[r][q]
            return 0

        lax.fori_loop(0, COLS // 8, columns, 0)
        for r in (first, first + 1, 7 - first, 6 - first) if drain else ():
            flip = r > 3
            line = 7 - r if flip else r
            for c in range(0, COLS, 8):
                for g in range(4):
                    start = (line * COLS + c) * 8 + flip * 4 + g
                    at = ROW_AT[r] + c
                    conv[at : at + 8, g * 128 : g * 128 + 128] = conv8[pl.ds(start, 8, stride=8), :]

    def fin_copy(k):
        source = feat.at[0, pl.ds(PIECE[k], 64)]
        return remote(source, fold_in.at[level], fin_send.at[k], fin_recv.at[level], comes[k])

    def fin_local(k):
        source = feat.at[0, pl.ds(PIECE[k], 64)]
        return pltpu.make_async_copy(source, fold_in.at[level], fin_recv.at[level])

    def finish(k):
        pl.when(not_me(comes[k]))(lambda: fin_copy(k).start())
        pl.when(is_me(comes[k]))(lambda: fin_local(k).start())

    def block(step, _):
        both = early & (step < 8)
        image = jnp.where(both, 1 - step % 2, 0)
        b = jnp.where(both, step // 2, jnp.where(early, step - 4, step + 4))
        first_use = late | (image == 1) | (b >= 4)
        slot = b % 2
        other = 1 - slot
        section, i = b // 2, b % 2
        final = jnp.where(image == 1, 3, NBLOCKS - 1)
        service(3 * step)
        for k in range(3):
            pl.when(first_use & (i == 0) & (section == small_from(k)))(functools.partial(small_arrives, k))
        pack_f[...] = pack[b].astype(F32)
        for n in range(5):
            for g in range(4):
                five = pack_f[5 * n : 5 * n + 5, g * 128 : g * 128 + 128]
                taps8[pl.ds(40 * n + g, 5, stride=8), :] = five
                taps8[pl.ds(40 * (4 - n) + 4 + g, 5, stride=8), :] = five
        conv_rows(image, 2, range(2, 8), True)
        conv_rows(image, 0, range(2, 6), False)
        service(3 * step + 1)

        def settle(test, arrives):
            for n in range(2):
                for ud in range(2):
                    pl.when(test & first_use & (i == n))(functools.partial(arrives, n, ud))

        @pl.when(late & (step == 0) & (core == 1))
        def _():
            bnd_copy(1, 1).start()

        near = early & (b < 4)
        same = section % 2 == core
        settle(near & same, lambda n, ud: own_copy(n, ud).wait())
        settle(near & jnp.logical_not(same), sib_arrives)
        for n in range(2):
            for ud in range(2):
                pl.when(early & (b == far_sib + 2 * n))(functools.partial(sibf_arrives, n, ud))

        @pl.when(has_up)
        def _():
            halo_down(image, b, slot).wait_recv()
            for r in range(2):
                place(image, r, top[NBLOCKS * image + b, r * 32 : r * 32 + 32, :].astype(F32))

        @pl.when(has_down)
        def _():
            halo_up(image, b, slot).wait_recv()
            for r in range(2):
                place(image, ROWS + 2 + r, bottom[NBLOCKS * image + b, r * 32 : r * 32 + 32, :].astype(F32))

        conv_rows(image, 0, range(2), True)

        def pointwise(first, count):
            part_rows = slice(first, first + count)
            normed = normed_rows(conv[part_rows, :], pack_f[25:26, :]).astype(BF16)
            for n in range(2):
                at = pl.ds(n * WIDTH, WIDTH)
                raised = jnp.dot(normed, upw[b, :, at], preferred_element_type=F32)
                hidden[0:count, at] = gelu(raised + pack_f[26 + n : 27 + n, :]).astype(BF16)
            branch = jnp.dot(hidden[0:count, :], downw[b], preferred_element_type=F32)
            old = feat[2 * image + slot, part_rows, :].astype(F32)
            new = (old + (branch + pack_f[28:29, :])).astype(BF16)
            feat[2 * image + other, part_rows, :] = new
            wide = new.astype(F32)
            for r in range(ROWS):
                if first <= ROW_AT[r] < first + count:
                    place(image, 2 + r, wide[ROW_AT[r] - first : ROW_AT[r] - first + 32, :])

        @pl.when(b > jnp.where(late, 4, 0))
        def _():
            halos_sent(image, b - 1, other)

        whole = early & (step < 6)
        pl.when(whole)(lambda: pointwise(0, PLACES))
        pl.when(jnp.logical_not(whole))(lambda: pointwise(0, PLACES // 2))

        @pl.when(b < final)
        def _():
            send_halos(image, b + 1, other)

        @pl.when((b == final) & (image == 0))
        def _():
            finish(0)
            finish(3)

        pl.when((b == final) & (image == 1))(lambda: move_copy(0).start())
        service(3 * step + 2)
        pl.when(jnp.logical_not(whole))(lambda: pointwise(PLACES // 2, PLACES // 2))
        pl.when((b == final) & (image == 1))(lambda: move_copy(1).start())
        return 0

    lax.fori_loop(0, jnp.where(early, 12, 4), block, 0)

    finish(1)
    finish(2)

    small_copy(0).wait_send()
    for i, ud in KINDS:
        sib_copy(i, ud).wait_send()
    halos_sent(0, NBLOCKS - 1, 1)

    @pl.when(early)
    def _():
        for image in range(2):
            for l in range(4):
                pl.when(not_me(goes[l]))(lambda: pix_copy(image, l).wait_send())
        for i, ud in KINDS:
            sibf_copy(i, ud).wait_send()
            for r in range(0 if i else 3):
                fwd_copy(i, ud, r).wait_send()
        halos_sent(1, 3, 1)
        for part in range(2):
            move_copy(part).wait_send()

    @pl.when(late)
    def _():
        for ud in range(2):
            bnd_copy(1, ud).wait_send()
        for k in (1, 2):
            small_copy(k).wait_send()

    load_mem.wait()
    load_out.wait()

    lane = lax.broadcasted_iota(jnp.int32, (8, 128), 1)
    query = lax.broadcasted_iota(jnp.int32, (8, 128), 0)
    heads_of = equal(jnp.where(lane < HEADS * NLAT, lane // HEADS, -1), query)
    lat_f = jnp.concatenate([lats[...].astype(F32), jnp.zeros((5, WIDTH), F32)], axis=0)
    spread = jnp.dot(lat_f.T.astype(BF16), heads_of, preferred_element_type=F32)
    d_row = lax.broadcasted_iota(jnp.int32, (WIDTH, 128), 0)
    d_lane = lax.broadcasted_iota(jnp.int32, (WIDTH, 128), 1)
    queries = jnp.where(d_row // HSZ == d_lane % HEADS, spread, 0.0).astype(BF16)
    e_row = lax.broadcasted_iota(jnp.int32, (128, WIDTH), 0)
    e_lane = lax.broadcasted_iota(jnp.int32, (128, WIDTH), 1)

    for l in range(4):
        remote(feat.at[0, pl.ds(0, 64)], fold_in.at[l], fin_send.at[0], fin_recv.at[l], goes[l]).wait_recv()

    memory = normed_rows(
        fold_in[...].astype(F32).reshape(PLACES, WIDTH), fold_scale[...].astype(F32)
    ).astype(BF16)
    keys = jnp.dot(memory, memw[:, :WIDTH], preferred_element_type=F32).astype(BF16)
    values = jnp.dot(memory, memw[:, WIDTH:], preferred_element_type=F32).astype(BF16).astype(F32)
    raised = jnp.exp(jnp.dot(keys, queries, preferred_element_type=F32) * HSZ ** (-0.5))
    raised = raised.reshape(4, 64, 128)
    share = (raised / jnp.sum(raised, axis=0, keepdims=True)).astype(BF16).reshape(PLACES, 128)
    for q in range(NLAT):
        widen = equal(e_row, q * HEADS + e_lane // HSZ)
        wide = jnp.dot(share, widen, preferred_element_type=F32)
        mixed = jnp.sum((wide * values).reshape(4, 64, WIDTH), axis=0).astype(BF16)
        folded = jnp.dot(mixed, outw[...], preferred_element_type=F32) + lat_f[q : q + 1, :]
        folded = folded.astype(BF16)
        for r in range(2):
            out[0, r, q] = folded[r * 32 : (r + 1) * 32, :]

    for k in range(4):
        pl.when(not_me(comes[k]))(lambda k=k: fin_copy(k).wait_send())


def on_device(
    pixels, embed_weight, level_code, depth_kernel, norm_gain, up_weight, up_bias,
    down_weight, down_bias, fold_gain, latents, memory_weight, output_weight,
):
    vmem = pl.BlockSpec(memory_space=pltpu.VMEM)
    hbm = pl.BlockSpec(memory_space=pl.ANY)
    dma = pltpu.SemaphoreType.DMA
    result = pl.pallas_call(
        kernel,
        out_shape=jax.ShapeDtypeStruct((1, 2, NLAT, COLS, WIDTH), BF16),
        in_specs=[hbm] * 13,
        out_specs=vmem,
        scratch_shapes=[
            pltpu.VMEM((80, WIDTH), BF16),
            pltpu.VMEM((4, WIDTH), BF16),
            pltpu.VMEM((1, 25, 2, WIDTH), BF16),
            pltpu.VMEM((1, 2, WIDTH), BF16),
            pltpu.VMEM((1, 2, HIDDEN), BF16),
            pltpu.VMEM((1, 2, WIDTH), BF16),
            pltpu.VMEM((WIDTH,), BF16),
            pltpu.VMEM((NLAT, WIDTH), BF16),
            pltpu.VMEM((8, 5, 8, 128), BF16),
            pltpu.VMEM((NBLOCKS, 32, WIDTH), BF16),
            pltpu.VMEM((32, WIDTH), F32),
            pltpu.VMEM((NBLOCKS, WIDTH, HIDDEN), BF16),
            pltpu.VMEM((NBLOCKS, HIDDEN, WIDTH), BF16),
            pltpu.VMEM((WIDTH, 2 * WIDTH), BF16),
            pltpu.VMEM((WIDTH, WIDTH), BF16),
            pltpu.VMEM((4, PLACES, WIDTH), BF16),
            pltpu.VMEM((2 * NBLOCKS, 64, WIDTH), BF16),
            pltpu.VMEM((2 * NBLOCKS, 64, WIDTH), BF16),
            pltpu.VMEM((2, 8 * (COLS + 4) * 8, 128), F32),
            pltpu.VMEM((200, 128), F32),
            pltpu.VMEM((4 * COLS * 8, 128), F32),
            pltpu.VMEM((PLACES, WIDTH), F32),
            pltpu.VMEM((PLACES, HIDDEN), BF16),
            pltpu.VMEM((4, 128, 40), F32),
            pltpu.VMEM((8, 40, WIDTH), BF16),
            pltpu.VMEM((4, 64, WIDTH), BF16),
            dma((8,)), dma((8,)), dma((3,)), dma((3,)), dma((2, 2)), dma((2, 2)), dma((2, 2)),
            dma((2, 2)), dma((2, 2)), dma((2, 2, 3)), dma((2, 2, 3)), dma((2, 2)), dma((2, 2)),
            dma((2, 2 * NBLOCKS)), dma((2, 2 * NBLOCKS)), dma((4,)), dma((4,)), dma((2,)), dma((8,)),
            dma((2,)), dma((2,)),
        ],
        compiler_params=pltpu.CompilerParams(
            collective_id=0, has_side_effects=True, vmem_limit_bytes=62 * 1024 * 1024
        ),
    )(
        pixels, embed_weight, level_code, jnp.transpose(depth_kernel, (0, 2, 1, 3)),
        norm_gain, up_weight, up_bias, down_weight, down_bias, fold_gain, latents,
        memory_weight, output_weight,
    )
    return jnp.transpose(result, (0, 1, 3, 2, 4))


def solution(mesh):
    return jax.shard_map(
        on_device,
        mesh=mesh,
        in_specs=(
            P(None, None, None, "lat", None),
            P(),
            P(),
            P("segment", None, None, None),
            P("segment", None, None),
            P("segment", None, None, None),
            P("segment", None, None),
            P("segment", None, None, None),
            P("segment", None, None),
            P(),
            P(),
            P(),
            P(),
        ),
        out_specs=P("segment", "lat", None, None, None),
        check_vma=False,
    )
```

```python
import functools

import jax
import jax.numpy as jnp
from jax import lax
from jax.experimental import pallas as pl
from jax.experimental.pallas import tpu as pltpu
from jax.sharding import PartitionSpec as P

MESH = pl.DeviceIdType.MESH
F32 = jnp.float32
BF16 = jnp.bfloat16
EPSILON = 1e-06
ROWS = 8
COLS = 32
WIDTH = 512
HIDDEN = 1024
NBLOCKS = 8
PLACES = ROWS * COLS
HEADS = 16
HSZ = 32
NLAT = 3
PIECE = (0, 128, 192, 64)
ROW_AT = (0, 32, 128, 160, 192, 224, 64, 96)
MIRROR = 11


def dev(xh, xl, y, z, core):
    return (xh * 2 + core, y * 16 + xl * 8 + z)


def remote(src, dst, send, recv, target):
    return pltpu.make_async_remote_copy(
        src_ref=src, dst_ref=dst, send_sem=send, recv_sem=recv, device_id=target, device_id_type=MESH
    )


def normed_rows(x, gain):
    average = jnp.mean(x, axis=-1, keepdims=True)
    centred = x - average
    spread = jnp.mean(centred * centred, axis=-1, keepdims=True)
    return centred * lax.rsqrt(spread + EPSILON) * gain


def gelu(x):
    return 0.5 * x * (1.0 + lax.erf(x * (2.0**-0.5)))


def kernel(
    pixels, embed_weight, level_code, depth, gain, up, up_bias, down, down_bias,
    fold_gain, latents, memory_weight, output_weight,
    out,
    embw, codes, taps, gains, up_shift, down_shift, fold_scale, lats,
    pix, pack, pack_f, upw, downw, memw, outw, feat, top, bottom, padded, taps8, conv8, conv, hidden, gath, cellw, fold_in,
    pix_send, pix_recv, small_send, small_recv, own_load, sib_send, sib_recv,
    bnd_send, bnd_recv, fwd_send, fwd_recv, sibf_send, sibf_recv,
    halo_send, halo_recv, fin_send, fin_recv, misc, load_sem, move_send, move_recv,
):
    loads = [
        pltpu.make_async_copy(source, target, load_sem.at[n])
        for n, (source, target) in enumerate(
            (
                (depth, taps), (gain, gains), (up_bias, up_shift), (down_bias, down_shift),
                (embed_weight, embw), (level_code, codes), (fold_gain, fold_scale), (latents, lats),
            )
        )
    ]
    for load in loads:
        load.start()
    seg = lax.axis_index("segment")
    lat = lax.axis_index("lat")
    xh, core = seg // 2, seg % 2
    y, xl, z = lat // 16, (lat // 8) % 2, lat % 8
    early, late = xh == 0, xh == 1
    level, bend = z % 4, (y + xh) % 2
    chip = 2 * y + (xl + bend) % 2
    band = 2 * chip + core
    has_up, has_down = band > 0, band < 15

    def of_band(n):
        return dev(xh, (n // 2 + n // 4 + xh) % 2, n // 4, z, n % 2)

    sibling = dev(xh, xl, y, z, 1 - core)
    partner = dev(1 - xh, 1 - xl, y, z, core)
    crossed = dev(1 - xh, 1 - xl, y, z, 1 - core)
    odd = 2 * (y % 2)
    flipped = jnp.where((xl + xh) % 2 == 0, y + 1 - odd, (y + 3 + odd) % 4)
    ring = [
        dev(xh, xl, y, (z + 1) % 8, core),
        dev(xh, xl, y, (z + 7) % 8, core),
        dev(xh, xl, flipped, z, core),
    ]
    others = [sibling, partner, crossed]
    above = of_band(jnp.maximum(band - 1, 0))
    below = of_band(jnp.minimum(band + 1, 15))
    goes = [dev(xh, (xl + bend) % 2, y, core * 4 + l, z // 4) for l in range(4)]
    comes = [dev(xh, chip % 2, y, core * 4 + k, z // 4) for k in range(4)]

    def is_me(target):
        return (target[0] == seg) & (target[1] == lat)

    def not_me(target):
        return (target[0] != seg) | (target[1] != lat)

    barrier = pltpu.get_barrier_semaphore()

    def greet(target):
        pl.semaphore_signal(barrier, inc=1, device_id=target, device_id_type=MESH)

    for target in ring + others:
        greet(target)
    expected = jnp.int32(6)
    for target in goes + comes:
        pl.when(not_me(target))(functools.partial(greet, target))
        expected = expected + not_me(target).astype(jnp.int32)
    pl.when(has_up)(functools.partial(greet, above))
    pl.when(has_down)(functools.partial(greet, below))
    expected = expected + has_up.astype(jnp.int32) + has_down.astype(jnp.int32)

    my_slot = lat % 4

    def micro(image):
        return core + 2 * image

    def pix_copy(image, l):
        at = 4 * image + my_slot
        return remote(
            pixels.at[micro(image), l], pix.at[at], pix_send.at[4 * image + l], pix_recv.at[at], goes[l]
        )

    def pix_local(image, l):
        at = 4 * image + my_slot
        return pltpu.make_async_copy(pixels.at[micro(image), l], pix.at[at], pix_recv.at[at])

    def pix_wait(image, k):
        at = 4 * image + k
        remote(pixels.at[0, 0], pix.at[at], pix_send.at[0], pix_recv.at[at], comes[k]).wait_recv()

    quarter = (z + 2 * (y % 2)) % 4
    mine = 2 * seg
    far = 2 * ((1 - xh) * 2 + core)
    far_sib = 2 * ((1 - xh) * 2 + (1 - core))
    sib_first = 2 * (xh * 2 + (1 - core))

    def store(ud):
        return (upw, downw)[ud]

    def given(ud):
        return (up, down)[ud]

    def span(ud, q):
        rows = (128, 256)[ud]
        return pl.ds(pl.multiple_of(q * rows, rows), rows)

    def own_copy(i, ud):
        return pltpu.make_async_copy(given(ud).at[0, i], store(ud).at[mine + i], own_load.at[i, ud])

    def sib_copy(i, ud):
        return remote(given(ud).at[0, i], store(ud).at[mine + i], sib_send.at[i, ud], sib_recv.at[i, ud], sibling)

    def sib_arrives(i, ud):
        remote(given(ud).at[0, i], store(ud).at[sib_first + i], sib_send.at[i, ud], sib_recv.at[i, ud], sibling).wait_recv()

    def bnd_copy(i, ud):
        return remote(
            given(ud).at[0, i, span(ud, quarter)],
            store(ud).at[mine + i, span(ud, quarter)],
            bnd_send.at[i, ud], bnd_recv.at[i, ud], partner,
        )

    def far_part(i, ud, q):
        return store(ud).at[far + i, span(ud, q)]

    def bnd_arrives(i, ud):
        part = far_part(i, ud, quarter)
        remote(part, part, bnd_send.at[i, ud], bnd_recv.at[i, ud], partner).wait_recv()

    def fwd_copy(i, ud, r):
        part = far_part(i, ud, quarter)
        return remote(part, part, fwd_send.at[i, ud, r], fwd_recv.at[i, ud, r], ring[r])

    def fwd_arrives(i, ud, r):
        part = far_part(i, ud, (quarter + (3, 1, 2)[r]) % 4)
        remote(part, part, fwd_send.at[i, ud, r], fwd_recv.at[i, ud, r], ring[r]).wait_recv()

    def sibf_copy(i, ud):
        whole = store(ud).at[far + i]
        return remote(whole, whole, sibf_send.at[i, ud], sibf_recv.at[i, ud], sibling)

    def sibf_arrives(i, ud):
        whole = store(ud).at[far_sib + i]
        remote(whole, whole, sibf_send.at[i, ud], sibf_recv.at[i, ud], sibling).wait_recv()

    def forward(i, ud):
        bnd_arrives(i, ud)
        for r in range(3):
            fwd_copy(i, ud, r).start()

    def hand_over(i, ud):
        for r in range(3):
            fwd_arrives(i, ud, r)
        sibf_copy(i, ud).start()

    def by_core(first, second):
        return jnp.where(early, jnp.where(core == 0, first, second), -9)

    def when(step, part):
        return 3 * step + part

    pt_fwd = {
        (0, 0): by_core(when(1, 0), when(1, 0)), (0, 1): by_core(when(3, 0), when(3, 0)),
        (1, 0): by_core(when(5, 0), when(5, 0)), (1, 1): by_core(when(7, 0), when(7, 0)),
    }
    pt_hand = {
        (0, 0): by_core(when(4, 0), when(4, 0)), (0, 1): by_core(when(6, 0), when(6, 0)),
        (1, 0): by_core(when(8, 0), when(8, 2)), (1, 1): by_core(when(9, 0), when(9, 2)),
    }
    pt_sib = {
        (0, 0): by_core(-1, -1), (0, 1): by_core(-1, -1),
        (1, 0): by_core(when(0, 1), when(0, 1)), (1, 1): by_core(when(0, 1), when(0, 1)),
    }
    KINDS = [(0, 0), (0, 1), (1, 0), (1, 1)]

    def service(point):
        for i, ud in KINDS:
            pl.when(pt_sib[i, ud] == point)(lambda i=i, ud=ud: sib_copy(i, ud).start())
        for i, ud in KINDS:
            pl.when(pt_fwd[i, ud] == point)(functools.partial(forward, i, ud))
        for i, ud in KINDS:
            pl.when(pt_hand[i, ud] == point)(functools.partial(hand_over, i, ud))

    for i, ud in KINDS:
        own_copy(i, ud).start()
    load_mem = pltpu.make_async_copy(memory_weight, memw, misc.at[0])
    load_out = pltpu.make_async_copy(output_weight, outw, misc.at[1])
    load_mem.start()
    load_out.start()

    for load in loads:
        load.wait()
    for i in range(2):
        pack_f[0:25] = taps[0, :, i, :].astype(F32)
        pack_f[25:26] = gains[0, i : i + 1, :].astype(F32)
        pack_f[26:27] = up_shift[0, i : i + 1, :WIDTH].astype(F32)
        pack_f[27:28] = up_shift[0, i : i + 1, WIDTH:].astype(F32)
        pack_f[28:29] = down_shift[0, i : i + 1, :].astype(F32)
        pack_f[29:32] = jnp.zeros((3, WIDTH), F32)
        pack[mine + i] = pack_f[...].astype(BF16)

    def small_copy(k):
        part = pack.at[pl.ds(mine, 2)]
        return remote(part, part, small_send.at[k], small_recv.at[k], others[k])

    def small_from(k):
        return (xh * 2 + (1 - core), (1 - xh) * 2 + core, (1 - xh) * 2 + (1 - core))[k]

    def small_arrives(k):
        part = pack.at[pl.ds(2 * small_from(k), 2)]
        remote(part, part, small_send.at[k], small_recv.at[k], others[k]).wait_recv()

    grid5 = padded.reshape(2, 8, COLS + 4, 8, 128)
    for image in range(2):
        grid5[image, :, 0:2] = jnp.zeros((8, 2, 8, 128), F32)
        grid5[image, :, COLS + 2 :] = jnp.zeros((8, 2, 8, 128), F32)

    def place(image, padded_row, values):
        for flip in range(2):
            p = MIRROR - padded_row if flip else padded_row
            if p < 8:
                for c in range(0, COLS, 8):
                    for g in range(4):
                        start = (p * (COLS + 4) + 2 + c) * 8 + flip * 4 + g
                        padded[image, pl.ds(start, 8, stride=8), :] = values[c : c + 8, g * 128 : g * 128 + 128]

    def equal(a, b):
        return jnp.where(a == b, 1.0, 0.0).astype(BF16)

    rho = lax.broadcasted_iota(jnp.int32, (128, 128), 0)
    lon = lax.broadcasted_iota(jnp.int32, (128, 128), 1)
    pick = equal(lon, 4 * (rho % 32) + rho // 32)
    row = lax.broadcasted_iota(jnp.int32, (40, 80), 0)
    col = lax.broadcasted_iota(jnp.int32, (40, 80), 1)
    source_col = ((row // 8) * 4 + row % 4) * 4
    half = (row // 4) % 2
    @pl.when(early)
    def _():
        for r2 in range(2):
            for j in range(4):
                choose = equal(jnp.where(half == r2, source_col + j, -1), col)
                part = jnp.dot(choose, embw[...], preferred_element_type=F32)
                cellw[4 * r2 + j] = part.astype(BF16)

    for image in range(2):
        @pl.when(jnp.logical_not(has_up))
        def _():
            for r in range(2):
                place(image, r, jnp.zeros((COLS, WIDTH), F32))

        @pl.when(jnp.logical_not(has_down))
        def _():
            for r in range(2):
                place(image, ROWS + 2 + r, jnp.zeros((COLS, WIDTH), F32))

    pl.semaphore_wait(barrier, expected)

    @pl.when(early)
    def _():
        for image in (1, 0):
            for l in range(4):
                pl.when(not_me(goes[l]))(lambda: pix_copy(image, l).start())
                pl.when(is_me(goes[l]))(lambda: pix_local(image, l).start())

    small_copy(0).start()
    service(-1)

    def embed(image):
        for k in range(4):
            pix_wait(image, k)
        for k in range(4):
            cells = pix[4 * image + k].astype(F32).reshape(40, 128).astype(BF16)
            picked = lax.dot_general(pick, cells, (((1,), (1,)), ((), ())), preferred_element_type=F32)
            for j in range(4):
                gath[j, k * 32 : (k + 1) * 32, :] = picked[j * 32 : (j + 1) * 32, :]
        level_row = lax.broadcasted_iota(jnp.int32, (4, WIDTH), 0)
        code = jnp.sum(jnp.where(level_row == level, codes[...].astype(F32), 0.0), axis=0, keepdims=True)
        for r2 in range(2):
            total = jnp.zeros((128, WIDTH), F32)
            for j in range(4):
                total = total + jnp.dot(gath[j].astype(BF16), cellw[4 * r2 + j], preferred_element_type=F32)
            total = (total + code).astype(BF16)
            for k in range(4):
                piece = total[k * 32 : (k + 1) * 32, :]
                start = PIECE[k] + r2 * 32
                feat[2 * image, start : start + 32, :] = piece
                place(image, 2 + 2 * k + r2, piece.astype(F32))

    def halo_up(image, h, slot):
        at = NBLOCKS * image + h
        source = feat.at[2 * image + slot, pl.ds(0, 64)]
        return remote(source, bottom.at[at], halo_send.at[0, at], halo_recv.at[0, at], above)

    def halo_down(image, h, slot):
        at = NBLOCKS * image + h
        source = feat.at[2 * image + slot, pl.ds(64, 64)]
        return remote(source, top.at[at], halo_send.at[1, at], halo_recv.at[1, at], below)

    def send_halos(image, h, slot):
        pl.when(has_up)(lambda: halo_up(image, h, slot).start())
        pl.when(has_down)(lambda: halo_down(image, h, slot).start())

    def halos_sent(image, h, slot):
        pl.when(has_up)(lambda: halo_up(image, h, slot).wait_send())
        pl.when(has_down)(lambda: halo_down(image, h, slot).wait_send())

    def move_copy(part):
        rows = pl.ds(128 * part, 128)
        return remote(feat.at[2, rows], feat.at[0, rows], move_send.at[part], move_recv.at[part], partner)

    def move_arrives(part):
        move_copy(part).wait_recv()
        rows = (0, 1, 6, 7, 2, 3, 4, 5)[4 * part : 4 * part + 4]
        for n, r in enumerate(rows):
            start = ROW_AT[r]
            place(0, 2 + r, feat[0, start : start + 32, :].astype(F32))

    @pl.when(early)
    def _():
        for image in (1, 0):
            embed(image)
            send_halos(image, 0, 0)

    @pl.when(late)
    def _():
        for i, ud in KINDS:
            sib_copy(i, ud).start()
        bnd_copy(0, 0).start()
        bnd_copy(0, 1).start()
        bnd_copy(0, 0).wait_send()
        bnd_copy(1, 0).start()
        bnd_copy(0, 1).wait_send()
        bnd_copy(1, 1).start()
        for k in (1, 2):
            small_copy(k).start()
        bnd_copy(1, 0).wait_send()
        bnd_copy(1, 1).wait_send()
        move_arrives(0)
        send_halos(0, 4, 0)
        move_arrives(1)

    def conv_rows(image, first, lines, drain):
        def columns(step, _):
            base = step * 8
            sums = [[None] * 8 for _ in range(2)]
            at = [[pl.ds(pl.multiple_of(((first + r) * COLS + q) * 8 + base * 8, 8), 8) for q in range(8)] for r in range(2)]
            if lines[0] < 2:
                sums = [[conv8[at[r][q], :] for q in range(8)] for r in range(2)]
            for p in lines:
                for c in range(12):
                    value = padded[image, pl.ds(pl.multiple_of((p * (COLS + 4) + c) * 8 + base * 8, 8), 8), :]
                    for r in range(2):
                        i = p - first - r
                        for j in range(5):
                            if 0 <= i < 5 and 0 <= c - j < 8:
                                term = value * taps8[8 * (5 * i + j) : 8 * (5 * i + j) + 8, :]
                                old = sums[r][c - j]
                                sums[r][c - j] = term if old is None else old + term
            for r in range(2):
                for q in range(8):
                    conv8[at[r][q], :] = sums[r][q]
            return 0

        lax.fori_loop(0, COLS // 8, columns, 0)
        for r in (first, first + 1, 7 - first, 6 - first) if drain else ():
            flip = r > 3
            line = 7 - r if flip else r
            for c in range(0, COLS, 8):
                for g in range(4):
                    start = (line * COLS + c) * 8 + flip * 4 + g
                    at = ROW_AT[r] + c
                    conv[at : at + 8, g * 128 : g * 128 + 128] = conv8[pl.ds(start, 8, stride=8), :]

    def fin_copy(k):
        source = feat.at[0, pl.ds(PIECE[k], 64)]
        return remote(source, fold_in.at[level], fin_send.at[k], fin_recv.at[level], comes[k])

    def fin_local(k):
        source = feat.at[0, pl.ds(PIECE[k], 64)]
        return pltpu.make_async_copy(source, fold_in.at[level], fin_recv.at[level])

    def finish(k):
        pl.when(not_me(comes[k]))(lambda: fin_copy(k).start())
        pl.when(is_me(comes[k]))(lambda: fin_local(k).start())

    def block(step, _):
        both = early & (step < 8)
        image = jnp.where(both, 1 - step % 2, 0)
        b = jnp.where(both, step // 2, jnp.where(early, step - 4, step + 4))
        first_use = late | (image == 1) | (b >= 4)
        slot = b % 2
        other = 1 - slot
        section, i = b // 2, b % 2
        final = jnp.where(image == 1, 3, NBLOCKS - 1)
        service(3 * step)
        for k in range(3):
            pl.when(first_use & (i == 0) & (section == small_from(k)))(functools.partial(small_arrives, k))
        pack_f[...] = pack[b].astype(F32)
        for n in range(5):
            for g in range(4):
                five = pack_f[5 * n : 5 * n + 5, g * 128 : g * 128 + 128]
                taps8[pl.ds(40 * n + g, 5, stride=8), :] = five
                taps8[pl.ds(40 * (4 - n) + 4 + g, 5, stride=8), :] = five
        conv_rows(image, 2, range(2, 8), True)
        conv_rows(image, 0, range(2, 6), False)
        service(3 * step + 1)

        def settle(test, arrives):
            for n in range(2):
                for ud in range(2):
                    pl.when(test & first_use & (i == n))(functools.partial(arrives, n, ud))

        near = section // 2 == xh
        same = section % 2 == core
        settle(near & same, lambda n, ud: own_copy(n, ud).wait())
        settle(near & jnp.logical_not(same), sib_arrives)
        settle(jnp.logical_not(near) & jnp.logical_not(same), sibf_arrives)

        @pl.when(has_up)
        def _():
            halo_down(image, b, slot).wait_recv()
            for r in range(2):
                place(image, r, top[NBLOCKS * image + b, r * 32 : r * 32 + 32, :].astype(F32))

        @pl.when(has_down)
        def _():
            halo_up(image, b, slot).wait_recv()
            for r in range(2):
                place(image, ROWS + 2 + r, bottom[NBLOCKS * image + b, r * 32 : r * 32 + 32, :].astype(F32))

        conv_rows(image, 0, range(2), True)

        def pointwise(first, count):
            part_rows = slice(first, first + count)
            normed = normed_rows(conv[part_rows, :], pack_f[25:26, :]).astype(BF16)
            for n in range(2):
                at = pl.ds(n * WIDTH, WIDTH)
                raised = jnp.dot(normed, upw[b, :, at], preferred_element_type=F32)
                hidden[0:count, at] = gelu(raised + pack_f[26 + n : 27 + n, :]).astype(BF16)
            branch = jnp.dot(hidden[0:count, :], downw[b], preferred_element_type=F32)
            old = feat[2 * image + slot, part_rows, :].astype(F32)
            new = (old + (branch + pack_f[28:29, :])).astype(BF16)
            feat[2 * image + other, part_rows, :] = new
            wide = new.astype(F32)
            for r in range(ROWS):
                if first <= ROW_AT[r] < first + count:
                    place(image, 2 + r, wide[ROW_AT[r] - first : ROW_AT[r] - first + 32, :])

        @pl.when(b > jnp.where(late, 4, 0))
        def _():
            halos_sent(image, b - 1, other)

        whole = early & (step < 6)
        pl.when(whole)(lambda: pointwise(0, PLACES))
        pl.when(jnp.logical_not(whole))(lambda: pointwise(0, PLACES // 2))

        @pl.when(b < final)
        def _():
            send_halos(image, b + 1, other)

        @pl.when((b == final) & (image == 0))
        def _():
            finish(0)
            finish(3)

        pl.when((b == final) & (image == 1))(lambda: move_copy(0).start())
        service(3 * step + 2)
        pl.when(jnp.logical_not(whole))(lambda: pointwise(PLACES // 2, PLACES // 2))
        pl.when((b == final) & (image == 1))(lambda: move_copy(1).start())
        return 0

    lax.fori_loop(0, jnp.where(early, 12, 4), block, 0)

    finish(1)
    finish(2)

    small_copy(0).wait_send()
    for i, ud in KINDS:
        sib_copy(i, ud).wait_send()
    halos_sent(0, NBLOCKS - 1, 1)

    @pl.when(early)
    def _():
        for image in range(2):
            for l in range(4):
                pl.when(not_me(goes[l]))(lambda: pix_copy(image, l).wait_send())
        for i, ud in KINDS:
            sibf_copy(i, ud).wait_send()
            for r in range(3):
                fwd_copy(i, ud, r).wait_send()
        halos_sent(1, 3, 1)
        for part in range(2):
            move_copy(part).wait_send()

    @pl.when(late)
    def _():
        for k in (1, 2):
            small_copy(k).wait_send()

    load_mem.wait()
    load_out.wait()

    lane = lax.broadcasted_iota(jnp.int32, (8, 128), 1)
    query = lax.broadcasted_iota(jnp.int32, (8, 128), 0)
    heads_of = equal(jnp.where(lane < HEADS * NLAT, lane // HEADS, -1), query)
    lat_f = jnp.concatenate([lats[...].astype(F32), jnp.zeros((5, WIDTH), F32)], axis=0)
    spread = jnp.dot(lat_f.T.astype(BF16), heads_of, preferred_element_type=F32)
    d_row = lax.broadcasted_iota(jnp.int32, (WIDTH, 128), 0)
    d_lane = lax.broadcasted_iota(jnp.int32, (WIDTH, 128), 1)
    queries = jnp.where(d_row // HSZ == d_lane % HEADS, spread, 0.0).astype(BF16)
    e_row = lax.broadcasted_iota(jnp.int32, (128, WIDTH), 0)
    e_lane = lax.broadcasted_iota(jnp.int32, (128, WIDTH), 1)

    for l in range(4):
        remote(feat.at[0, pl.ds(0, 64)], fold_in.at[l], fin_send.at[0], fin_recv.at[l], goes[l]).wait_recv()

    memory = normed_rows(
        fold_in[...].astype(F32).reshape(PLACES, WIDTH), fold_scale[...].astype(F32)
    ).astype(BF16)
    keys = jnp.dot(memory, memw[:, :WIDTH], preferred_element_type=F32).astype(BF16)
    values = jnp.dot(memory, memw[:, WIDTH:], preferred_element_type=F32).astype(BF16).astype(F32)
    raised = jnp.exp(jnp.dot(keys, queries, preferred_element_type=F32) * HSZ ** (-0.5))
    raised = raised.reshape(4, 64, 128)
    share = (raised / jnp.sum(raised, axis=0, keepdims=True)).astype(BF16).reshape(PLACES, 128)
    for q in range(NLAT):
        widen = equal(e_row, q * HEADS + e_lane // HSZ)
        wide = jnp.dot(share, widen, preferred_element_type=F32)
        mixed = jnp.sum((wide * values).reshape(4, 64, WIDTH), axis=0).astype(BF16)
        folded = jnp.dot(mixed, outw[...], preferred_element_type=F32) + lat_f[q : q + 1, :]
        folded = folded.astype(BF16)
        for r in range(2):
            out[0, r, q] = folded[r * 32 : (r + 1) * 32, :]

    for k in range(4):
        pl.when(not_me(comes[k]))(lambda k=k: fin_copy(k).wait_send())


def on_device(
    pixels, embed_weight, level_code, depth_kernel, norm_gain, up_weight, up_bias,
    down_weight, down_bias, fold_gain, latents, memory_weight, output_weight,
):
    vmem = pl.BlockSpec(memory_space=pltpu.VMEM)
    hbm = pl.BlockSpec(memory_space=pl.ANY)
    dma = pltpu.SemaphoreType.DMA
    result = pl.pallas_call(
        kernel,
        out_shape=jax.ShapeDtypeStruct((1, 2, NLAT, COLS, WIDTH), BF16),
        in_specs=[hbm] * 13,
        out_specs=vmem,
        scratch_shapes=[
            pltpu.VMEM((80, WIDTH), BF16),
            pltpu.VMEM((4, WIDTH), BF16),
            pltpu.VMEM((1, 25, 2, WIDTH), BF16),
            pltpu.VMEM((1, 2, WIDTH), BF16),
            pltpu.VMEM((1, 2, HIDDEN), BF16),
            pltpu.VMEM((1, 2, WIDTH), BF16),
            pltpu.VMEM((WIDTH,), BF16),
            pltpu.VMEM((NLAT, WIDTH), BF16),
            pltpu.VMEM((8, 5, 8, 128), BF16),
            pltpu.VMEM((NBLOCKS, 32, WIDTH), BF16),
            pltpu.VMEM((32, WIDTH), F32),
            pltpu.VMEM((NBLOCKS, WIDTH, HIDDEN), BF16),
            pltpu.VMEM((NBLOCKS, HIDDEN, WIDTH), BF16),
            pltpu.VMEM((WIDTH, 2 * WIDTH), BF16),
            pltpu.VMEM((WIDTH, WIDTH), BF16),
            pltpu.VMEM((4, PLACES, WIDTH), BF16),
            pltpu.VMEM((2 * NBLOCKS, 64, WIDTH), BF16),
            pltpu.VMEM((2 * NBLOCKS, 64, WIDTH), BF16),
            pltpu.VMEM((2, 8 * (COLS + 4) * 8, 128), F32),
            pltpu.VMEM((200, 128), F32),
            pltpu.VMEM((4 * COLS * 8, 128), F32),
            pltpu.VMEM((PLACES, WIDTH), F32),
            pltpu.VMEM((PLACES, HIDDEN), BF16),
            pltpu.VMEM((4, 128, 40), F32),
            pltpu.VMEM((8, 40, WIDTH), BF16),
            pltpu.VMEM((4, 64, WIDTH), BF16),
            dma((8,)), dma((8,)), dma((3,)), dma((3,)), dma((2, 2)), dma((2, 2)), dma((2, 2)),
            dma((2, 2)), dma((2, 2)), dma((2, 2, 3)), dma((2, 2, 3)), dma((2, 2)), dma((2, 2)),
            dma((2, 2 * NBLOCKS)), dma((2, 2 * NBLOCKS)), dma((4,)), dma((4,)), dma((2,)), dma((8,)),
            dma((2,)), dma((2,)),
        ],
        compiler_params=pltpu.CompilerParams(
            collective_id=0, has_side_effects=True, vmem_limit_bytes=62 * 1024 * 1024
        ),
    )(
        pixels, embed_weight, level_code, jnp.transpose(depth_kernel, (0, 2, 1, 3)),
        norm_gain, up_weight, up_bias, down_weight, down_bias, fold_gain, latents,
        memory_weight, output_weight,
    )
    return jnp.transpose(result, (0, 1, 3, 2, 4))


def solution(mesh):
    return jax.shard_map(
        on_device,
        mesh=mesh,
        in_specs=(
            P(None, None, None, "lat", None),
            P(),
            P(),
            P("segment", None, None, None),
            P("segment", None, None),
            P("segment", None, None, None),
            P("segment", None, None),
            P("segment", None, None, None),
            P("segment", None, None),
            P(),
            P(),
            P(),
            P(),
        ),
        out_specs=P("segment", "lat", None, None, None),
        check_vma=False,
    )
```

```python
import functools

import jax
import jax.numpy as jnp
from jax import lax
from jax.experimental import pallas as pl
from jax.experimental.pallas import tpu as pltpu
from jax.sharding import PartitionSpec as P

MESH = pl.DeviceIdType.MESH
F32 = jnp.float32
BF16 = jnp.bfloat16
EPSILON = 1e-06
ROWS = 8
COLS = 32
WIDTH = 512
HIDDEN = 1024
NBLOCKS = 8
PLACES = ROWS * COLS
HEADS = 16
HSZ = 32
NLAT = 3
PIECE = (0, 128, 192, 64)
ROW_AT = (0, 32, 128, 160, 192, 224, 64, 96)
MIRROR = 11


def dev(xh, xl, y, z, core):
    return (xh * 2 + core, y * 16 + xl * 8 + z)


def remote(src, dst, send, recv, target):
    return pltpu.make_async_remote_copy(
        src_ref=src, dst_ref=dst, send_sem=send, recv_sem=recv, device_id=target, device_id_type=MESH
    )


def normed_rows(x, gain):
    average = jnp.mean(x, axis=-1, keepdims=True)
    centred = x - average
    spread = jnp.mean(centred * centred, axis=-1, keepdims=True)
    return centred * lax.rsqrt(spread + EPSILON) * gain


def gelu(x):
    return 0.5 * x * (1.0 + lax.erf(x * (2.0**-0.5)))


def kernel(
    pixels, embed_weight, level_code, depth, gain, up, up_bias, down, down_bias,
    fold_gain, latents, memory_weight, output_weight,
    out,
    embw, codes, taps, gains, up_shift, down_shift, fold_scale, lats,
    pix, pack, pack_f, upw, downw, memw, outw, feat, top, bottom, padded, taps8, conv8, conv, hidden, gath, cellw, fold_in,
    pix_send, pix_recv, small_send, small_recv, own_load, sib_send, sib_recv,
    bnd_send, bnd_recv, fwd_send, fwd_recv, sibf_send, sibf_recv,
    halo_send, halo_recv, fin_send, fin_recv, misc, load_sem, move_send, move_recv,
):
    loads = [
        pltpu.make_async_copy(source, target, load_sem.at[n])
        for n, (source, target) in enumerate(
            (
                (depth, taps), (gain, gains), (up_bias, up_shift), (down_bias, down_shift),
                (embed_weight, embw), (level_code, codes), (fold_gain, fold_scale), (latents, lats),
            )
        )
    ]
    for load in loads:
        load.start()
    seg = lax.axis_index("segment")
    lat = lax.axis_index("lat")
    xh, core = seg // 2, seg % 2
    y, xl, z = lat // 16, (lat // 8) % 2, lat % 8
    early, late = xh == 0, xh == 1
    level, bend = z % 4, (y + xh) % 2
    chip = 2 * y + (xl + bend) % 2
    band = 2 * chip + core
    has_up, has_down = band > 0, band < 15

    def of_band(n):
        return dev(xh, (n // 2 + n // 4 + xh) % 2, n // 4, z, n % 2)

    sibling = dev(xh, xl, y, z, 1 - core)
    partner = dev(1 - xh, 1 - xl, y, z, core)
    crossed = dev(1 - xh, 1 - xl, y, z, 1 - core)
    odd = 2 * (y % 2)
    flipped = jnp.where((xl + xh) % 2 == 0, y + 1 - odd, (y + 3 + odd) % 4)
    ring = [
        dev(xh, xl, y, (z + 1) % 8, core),
        dev(xh, xl, y, (z + 7) % 8, core),
        dev(xh, xl, flipped, z, core),
    ]
    others = [sibling, partner, crossed]
    above = of_band(jnp.maximum(band - 1, 0))
    below = of_band(jnp.minimum(band + 1, 15))
    goes = [dev(xh, (xl + bend) % 2, y, core * 4 + l, z // 4) for l in range(4)]
    comes = [dev(xh, chip % 2, y, core * 4 + k, z // 4) for k in range(4)]

    def is_me(target):
        return (target[0] == seg) & (target[1] == lat)

    def not_me(target):
        return (target[0] != seg) | (target[1] != lat)

    barrier = pltpu.get_barrier_semaphore()

    def greet(target):
        pl.semaphore_signal(barrier, inc=1, device_id=target, device_id_type=MESH)

    for target in ring + others:
        greet(target)
    expected = jnp.int32(6)
    for target in goes + comes:
        pl.when(not_me(target))(functools.partial(greet, target))
        expected = expected + not_me(target).astype(jnp.int32)
    pl.when(has_up)(functools.partial(greet, above))
    pl.when(has_down)(functools.partial(greet, below))
    expected = expected + has_up.astype(jnp.int32) + has_down.astype(jnp.int32)

    my_slot = lat % 4

    def micro(image):
        return core + 2 * image

    def pix_copy(image, l):
        at = 4 * image + my_slot
        return remote(
            pixels.at[micro(image), l], pix.at[at], pix_send.at[4 * image + l], pix_recv.at[at], goes[l]
        )

    def pix_local(image, l):
        at = 4 * image + my_slot
        return pltpu.make_async_copy(pixels.at[micro(image), l], pix.at[at], pix_recv.at[at])

    def pix_wait(image, k):
        at = 4 * image + k
        remote(pixels.at[0, 0], pix.at[at], pix_send.at[0], pix_recv.at[at], comes[k]).wait_recv()

    quarter = (z + 2 * (y % 2)) % 4
    mine = 2 * seg
    far = 2 * ((1 - xh) * 2 + core)
    far_sib = 2 * ((1 - xh) * 2 + (1 - core))
    sib_first = 2 * (xh * 2 + (1 - core))

    def store(ud):
        return (upw, downw)[ud]

    def given(ud):
        return (up, down)[ud]

    def span(ud, q):
        rows = (128, 256)[ud]
        return pl.ds(pl.multiple_of(q * rows, rows), rows)

    def own_copy(i, ud):
        return pltpu.make_async_copy(given(ud).at[0, i], store(ud).at[mine + i], own_load.at[i, ud])

    def sib_copy(i, ud):
        return remote(given(ud).at[0, i], store(ud).at[mine + i], sib_send.at[i, ud], sib_recv.at[i, ud], sibling)

    def sib_arrives(i, ud):
        remote(given(ud).at[0, i], store(ud).at[sib_first + i], sib_send.at[i, ud], sib_recv.at[i, ud], sibling).wait_recv()

    def bnd_copy(i, ud):
        return remote(
            given(ud).at[0, i, span(ud, quarter)],
            store(ud).at[mine + i, span(ud, quarter)],
            bnd_send.at[i, ud], bnd_recv.at[i, ud], partner,
        )

    def far_part(i, ud, q):
        return store(ud).at[far + i, span(ud, q)]

    def bnd_arrives(i, ud):
        part = far_part(i, ud, quarter)
        remote(part, part, bnd_send.at[i, ud], bnd_recv.at[i, ud], partner).wait_recv()

    def fwd_copy(i, ud, r):
        part = far_part(i, ud, quarter)
        return remote(part, part, fwd_send.at[i, ud, r], fwd_recv.at[i, ud, r], ring[r])

    def fwd_arrives(i, ud, r):
        part = far_part(i, ud, (quarter + (3, 1, 2)[r]) % 4)
        remote(part, part, fwd_send.at[i, ud, r], fwd_recv.at[i, ud, r], ring[r]).wait_recv()

    def sibf_copy(i, ud):
        whole = store(ud).at[far + i]
        return remote(whole, whole, sibf_send.at[i, ud], sibf_recv.at[i, ud], sibling)

    def sibf_arrives(i, ud):
        whole = store(ud).at[far_sib + i]
        remote(whole, whole, sibf_send.at[i, ud], sibf_recv.at[i, ud], sibling).wait_recv()

    def forward(i, ud):
        bnd_arrives(i, ud)
        for r in range(2):
            fwd_copy(i, ud, r).start()

    def hand_over(i, ud):
        for r in range(3):
            fwd_arrives(i, ud, r)
        sibf_copy(i, ud).start()

    def by_core(first, second):
        return jnp.where(early, jnp.where(core == 0, first, second), -9)

    def when(step, part):
        return 3 * step + part

    pt_fwd = {
        (0, 0): by_core(when(1, 0), when(1, 0)), (0, 1): by_core(when(3, 0), when(3, 0)),
        (1, 0): by_core(when(5, 0), when(5, 0)), (1, 1): by_core(when(7, 0), when(7, 0)),
    }
    pt_hand = {
        (0, 0): by_core(when(4, 0), when(4, 0)), (0, 1): by_core(when(6, 0), when(6, 0)),
        (1, 0): by_core(when(8, 0), when(8, 2)), (1, 1): by_core(when(9, 0), when(9, 2)),
    }
    pt_sib = {
        (0, 0): by_core(-1, -1), (0, 1): by_core(-1, -1),
        (1, 0): by_core(when(0, 1), when(0, 1)), (1, 1): by_core(when(0, 1), when(0, 1)),
    }
    KINDS = [(0, 0), (0, 1), (1, 0), (1, 1)]

    def service(point):
        for i, ud in KINDS:
            pl.when(pt_sib[i, ud] == point)(lambda i=i, ud=ud: sib_copy(i, ud).start())
        for i, ud in KINDS:
            pl.when(pt_fwd[i, ud] == point)(functools.partial(forward, i, ud))
            pl.when(pt_fwd[i, ud] + 3 == point)(lambda i=i, ud=ud: fwd_copy(i, ud, 2).start())
        for i, ud in KINDS:
            pl.when(pt_hand[i, ud] == point)(functools.partial(hand_over, i, ud))

    for i, ud in KINDS:
        own_copy(i, ud).start()
    load_mem = pltpu.make_async_copy(memory_weight, memw, misc.at[0])
    load_out = pltpu.make_async_copy(output_weight, outw, misc.at[1])
    load_mem.start()
    load_out.start()

    for load in loads:
        load.wait()
    for i in range(2):
        pack_f[0:25] = taps[0, :, i, :].astype(F32)
        pack_f[25:26] = gains[0, i : i + 1, :].astype(F32)
        pack_f[26:27] = up_shift[0, i : i + 1, :WIDTH].astype(F32)
        pack_f[27:28] = up_shift[0, i : i + 1, WIDTH:].astype(F32)
        pack_f[28:29] = down_shift[0, i : i + 1, :].astype(F32)
        pack_f[29:32] = jnp.zeros((3, WIDTH), F32)
        pack[mine + i] = pack_f[...].astype(BF16)

    def small_copy(k):
        part = pack.at[pl.ds(mine, 2)]
        return remote(part, part, small_send.at[k], small_recv.at[k], others[k])

    def small_from(k):
        return (xh * 2 + (1 - core), (1 - xh) * 2 + core, (1 - xh) * 2 + (1 - core))[k]

    def small_arrives(k):
        part = pack.at[pl.ds(2 * small_from(k), 2)]
        remote(part, part, small_send.at[k], small_recv.at[k], others[k]).wait_recv()

    grid5 = padded.reshape(2, 8, COLS + 4, 8, 128)
    for image in range(2):
        grid5[image, :, 0:2] = jnp.zeros((8, 2, 8, 128), F32)
        grid5[image, :, COLS + 2 :] = jnp.zeros((8, 2, 8, 128), F32)

    def place(image, padded_row, values):
        for flip in range(2):
            p = MIRROR - padded_row if flip else padded_row
            if p < 8:
                for c in range(0, COLS, 8):
                    for g in range(4):
                        start = (p * (COLS + 4) + 2 + c) * 8 + flip * 4 + g
                        padded[image, pl.ds(start, 8, stride=8), :] = values[c : c + 8, g * 128 : g * 128 + 128]

    def equal(a, b):
        return jnp.where(a == b, 1.0, 0.0).astype(BF16)

    rho = lax.broadcasted_iota(jnp.int32, (128, 128), 0)
    lon = lax.broadcasted_iota(jnp.int32, (128, 128), 1)
    pick = equal(lon, 4 * (rho % 32) + rho // 32)
    row = lax.broadcasted_iota(jnp.int32, (40, 80), 0)
    col = lax.broadcasted_iota(jnp.int32, (40, 80), 1)
    source_col = ((row // 8) * 4 + row % 4) * 4
    half = (row // 4) % 2
    @pl.when(early)
    def _():
        for r2 in range(2):
            for j in range(4):
                choose = equal(jnp.where(half == r2, source_col + j, -1), col)
                part = jnp.dot(choose, embw[...], preferred_element_type=F32)
                cellw[4 * r2 + j] = part.astype(BF16)

    for image in range(2):
        @pl.when(jnp.logical_not(has_up))
        def _():
            for r in range(2):
                place(image, r, jnp.zeros((COLS, WIDTH), F32))

        @pl.when(jnp.logical_not(has_down))
        def _():
            for r in range(2):
                place(image, ROWS + 2 + r, jnp.zeros((COLS, WIDTH), F32))

    pl.semaphore_wait(barrier, expected)

    @pl.when(early)
    def _():
        for image in (1, 0):
            for l in range(4):
                pl.when(not_me(goes[l]))(lambda: pix_copy(image, l).start())
                pl.when(is_me(goes[l]))(lambda: pix_local(image, l).start())

    small_copy(0).start()
    service(-1)

    def embed(image):
        for k in range(4):
            pix_wait(image, k)
        for k in range(4):
            cells = pix[4 * image + k].astype(F32).reshape(40, 128).astype(BF16)
            picked = lax.dot_general(pick, cells, (((1,), (1,)), ((), ())), preferred_element_type=F32)
            for j in range(4):
                gath[j, k * 32 : (k + 1) * 32, :] = picked[j * 32 : (j + 1) * 32, :]
        level_row = lax.broadcasted_iota(jnp.int32, (4, WIDTH), 0)
        code = jnp.sum(jnp.where(level_row == level, codes[...].astype(F32), 0.0), axis=0, keepdims=True)
        for r2 in range(2):
            total = jnp.zeros((128, WIDTH), F32)
            for j in range(4):
                total = total + jnp.dot(gath[j].astype(BF16), cellw[4 * r2 + j], preferred_element_type=F32)
            total = (total + code).astype(BF16)
            for k in range(4):
                piece = total[k * 32 : (k + 1) * 32, :]
                start = PIECE[k] + r2 * 32
                feat[2 * image, start : start + 32, :] = piece
                place(image, 2 + 2 * k + r2, piece.astype(F32))

    def halo_up(image, h, slot):
        at = NBLOCKS * image + h
        source = feat.at[2 * image + slot, pl.ds(0, 64)]
        return remote(source, bottom.at[at], halo_send.at[0, at], halo_recv.at[0, at], above)

    def halo_down(image, h, slot):
        at = NBLOCKS * image + h
        source = feat.at[2 * image + slot, pl.ds(64, 64)]
        return remote(source, top.at[at], halo_send.at[1, at], halo_recv.at[1, at], below)

    def send_halos(image, h, slot):
        pl.when(has_up)(lambda: halo_up(image, h, slot).start())
        pl.when(has_down)(lambda: halo_down(image, h, slot).start())

    def halos_sent(image, h, slot):
        pl.when(has_up)(lambda: halo_up(image, h, slot).wait_send())
        pl.when(has_down)(lambda: halo_down(image, h, slot).wait_send())

    def move_copy(part):
        rows = pl.ds(128 * part, 128)
        return remote(feat.at[2, rows], feat.at[0, rows], move_send.at[part], move_recv.at[part], partner)

    def move_arrives(part):
        move_copy(part).wait_recv()
        rows = (0, 1, 6, 7, 2, 3, 4, 5)[4 * part : 4 * part + 4]
        for n, r in enumerate(rows):
            start = ROW_AT[r]
            place(0, 2 + r, feat[0, start : start + 32, :].astype(F32))

    @pl.when(early)
    def _():
        for image in (1, 0):
            embed(image)
            send_halos(image, 0, 0)

    @pl.when(late)
    def _():
        for i, ud in KINDS:
            sib_copy(i, ud).start()
        bnd_copy(0, 0).start()
        bnd_copy(0, 1).start()
        bnd_copy(0, 0).wait_send()
        bnd_copy(1, 0).start()
        bnd_copy(0, 1).wait_send()
        bnd_copy(1, 1).start()
        for k in (1, 2):
            small_copy(k).start()
        bnd_copy(1, 0).wait_send()
        bnd_copy(1, 1).wait_send()
        move_arrives(0)
        send_halos(0, 4, 0)
        move_arrives(1)

    def conv_rows(image, first, lines, drain):
        def columns(step, _):
            base = step * 8
            sums = [[None] * 8 for _ in range(2)]
            at = [[pl.ds(pl.multiple_of(((first + r) * COLS + q) * 8 + base * 8, 8), 8) for q in range(8)] for r in range(2)]
            if lines[0] < 2:
                sums = [[conv8[at[r][q], :] for q in range(8)] for r in range(2)]
            for p in lines:
                for c in range(12):
                    value = padded[image, pl.ds(pl.multiple_of((p * (COLS + 4) + c) * 8 + base * 8, 8), 8), :]
                    for r in range(2):
                        i = p - first - r
                        for j in range(5):
                            if 0 <= i < 5 and 0 <= c - j < 8:
                                term = value * taps8[8 * (5 * i + j) : 8 * (5 * i + j) + 8, :]
                                old = sums[r][c - j]
                                sums[r][c - j] = term if old is None else old + term
            for r in range(2):
                for q in range(8):
                    conv8[at[r][q], :] = sums[r][q]
            return 0

        lax.fori_loop(0, COLS // 8, columns, 0)
        for r in (first, first + 1, 7 - first, 6 - first) if drain else ():
            flip = r > 3
            line = 7 - r if flip else r
            for c in range(0, COLS, 8):
                for g in range(4):
                    start = (line * COLS + c) * 8 + flip * 4 + g
                    at = ROW_AT[r] + c
                    conv[at : at + 8, g * 128 : g * 128 + 128] = conv8[pl.ds(start, 8, stride=8), :]

    def fin_copy(k):
        source = feat.at[0, pl.ds(PIECE[k], 64)]
        return remote(source, fold_in.at[level], fin_send.at[k], fin_recv.at[level], comes[k])

    def fin_local(k):
        source = feat.at[0, pl.ds(PIECE[k], 64)]
        return pltpu.make_async_copy(source, fold_in.at[level], fin_recv.at[level])

    def finish(k):
        pl.when(not_me(comes[k]))(lambda: fin_copy(k).start())
        pl.when(is_me(comes[k]))(lambda: fin_local(k).start())

    def block(step, _):
        both = early & (step < 8)
        image = jnp.where(both, 1 - step % 2, 0)
        b = jnp.where(both, step // 2, jnp.where(early, step - 4, step + 4))
        first_use = late | (image == 1) | (b >= 4)
        slot = b % 2
        other = 1 - slot
        section, i = b // 2, b % 2
        final = jnp.where(image == 1, 3, NBLOCKS - 1)
        service(3 * step)
        for k in range(3):
            pl.when(first_use & (i == 0) & (section == small_from(k)))(functools.partial(small_arrives, k))
        pack_f[...] = pack[b].astype(F32)
        for n in range(5):
            for g in range(4):
                five = pack_f[5 * n : 5 * n + 5, g * 128 : g * 128 + 128]
                taps8[pl.ds(40 * n + g, 5, stride=8), :] = five
                taps8[pl.ds(40 * (4 - n) + 4 + g, 5, stride=8), :] = five
        conv_rows(image, 2, range(2, 8), True)
        conv_rows(image, 0, range(2, 6), False)
        service(3 * step + 1)

        def settle(test, arrives):
            for n in range(2):
                for ud in range(2):
                    pl.when(test & first_use & (i == n))(functools.partial(arrives, n, ud))

        near = section // 2 == xh
        same = section % 2 == core
        settle(near & same, lambda n, ud: own_copy(n, ud).wait())
        settle(near & jnp.logical_not(same), sib_arrives)
        settle(jnp.logical_not(near) & jnp.logical_not(same), sibf_arrives)

        @pl.when(has_up)
        def _():
            halo_down(image, b, slot).wait_recv()
            for r in range(2):
                place(image, r, top[NBLOCKS * image + b, r * 32 : r * 32 + 32, :].astype(F32))

        @pl.when(has_down)
        def _():
            halo_up(image, b, slot).wait_recv()
            for r in range(2):
                place(image, ROWS + 2 + r, bottom[NBLOCKS * image + b, r * 32 : r * 32 + 32, :].astype(F32))

        conv_rows(image, 0, range(2), True)

        def pointwise(first, count):
            part_rows = slice(first, first + count)
            normed = normed_rows(conv[part_rows, :], pack_f[25:26, :]).astype(BF16)
            for n in range(2):
                at = pl.ds(n * WIDTH, WIDTH)
                raised = jnp.dot(normed, upw[b, :, at], preferred_element_type=F32)
                hidden[0:count, at] = gelu(raised + pack_f[26 + n : 27 + n, :]).astype(BF16)
            branch = jnp.dot(hidden[0:count, :], downw[b], preferred_element_type=F32)
            old = feat[2 * image + slot, part_rows, :].astype(F32)
            new = (old + (branch + pack_f[28:29, :])).astype(BF16)
            feat[2 * image + other, part_rows, :] = new
            wide = new.astype(F32)
            for r in range(ROWS):
                if first <= ROW_AT[r] < first + count:
                    place(image, 2 + r, wide[ROW_AT[r] - first : ROW_AT[r] - first + 32, :])

        @pl.when(b > jnp.where(late, 4, 0))
        def _():
            halos_sent(image, b - 1, other)

        whole = early & (step < 6)
        pl.when(whole)(lambda: pointwise(0, PLACES))
        pl.when(jnp.logical_not(whole))(lambda: pointwise(0, PLACES // 2))

        @pl.when(b < final)
        def _():
            send_halos(image, b + 1, other)

        @pl.when((b == final) & (image == 0))
        def _():
            finish(0)
            finish(3)

        pl.when((b == final) & (image == 1))(lambda: move_copy(0).start())
        service(3 * step + 2)
        pl.when(jnp.logical_not(whole))(lambda: pointwise(PLACES // 2, PLACES // 2))
        pl.when((b == final) & (image == 1))(lambda: move_copy(1).start())
        return 0

    lax.fori_loop(0, jnp.where(early, 12, 4), block, 0)

    finish(1)
    finish(2)

    small_copy(0).wait_send()
    for i, ud in KINDS:
        sib_copy(i, ud).wait_send()
    halos_sent(0, NBLOCKS - 1, 1)

    @pl.when(early)
    def _():
        for image in range(2):
            for l in range(4):
                pl.when(not_me(goes[l]))(lambda: pix_copy(image, l).wait_send())
        for i, ud in KINDS:
            sibf_copy(i, ud).wait_send()
            for r in range(3):
                fwd_copy(i, ud, r).wait_send()
        halos_sent(1, 3, 1)
        for part in range(2):
            move_copy(part).wait_send()

    @pl.when(late)
    def _():
        for k in (1, 2):
            small_copy(k).wait_send()

    load_mem.wait()
    load_out.wait()

    lane = lax.broadcasted_iota(jnp.int32, (8, 128), 1)
    query = lax.broadcasted_iota(jnp.int32, (8, 128), 0)
    heads_of = equal(jnp.where(lane < HEADS * NLAT, lane // HEADS, -1), query)
    lat_f = jnp.concatenate([lats[...].astype(F32), jnp.zeros((5, WIDTH), F32)], axis=0)
    spread = jnp.dot(lat_f.T.astype(BF16), heads_of, preferred_element_type=F32)
    d_row = lax.broadcasted_iota(jnp.int32, (WIDTH, 128), 0)
    d_lane = lax.broadcasted_iota(jnp.int32, (WIDTH, 128), 1)
    queries = jnp.where(d_row // HSZ == d_lane % HEADS, spread, 0.0).astype(BF16)
    e_row = lax.broadcasted_iota(jnp.int32, (128, WIDTH), 0)
    e_lane = lax.broadcasted_iota(jnp.int32, (128, WIDTH), 1)

    for l in range(4):
        remote(feat.at[0, pl.ds(0, 64)], fold_in.at[l], fin_send.at[0], fin_recv.at[l], goes[l]).wait_recv()

    memory = normed_rows(
        fold_in[...].astype(F32).reshape(PLACES, WIDTH), fold_scale[...].astype(F32)
    ).astype(BF16)
    keys = jnp.dot(memory, memw[:, :WIDTH], preferred_element_type=F32).astype(BF16)
    values = jnp.dot(memory, memw[:, WIDTH:], preferred_element_type=F32).astype(BF16).astype(F32)
    raised = jnp.exp(jnp.dot(keys, queries, preferred_element_type=F32) * HSZ ** (-0.5))
    raised = raised.reshape(4, 64, 128)
    share = (raised / jnp.sum(raised, axis=0, keepdims=True)).astype(BF16).reshape(PLACES, 128)
    for q in range(NLAT):
        widen = equal(e_row, q * HEADS + e_lane // HSZ)
        wide = jnp.dot(share, widen, preferred_element_type=F32)
        mixed = jnp.sum((wide * values).reshape(4, 64, WIDTH), axis=0).astype(BF16)
        folded = jnp.dot(mixed, outw[...], preferred_element_type=F32) + lat_f[q : q + 1, :]
        folded = folded.astype(BF16)
        for r in range(2):
            out[0, r, q] = folded[r * 32 : (r + 1) * 32, :]

    for k in range(4):
        pl.when(not_me(comes[k]))(lambda k=k: fin_copy(k).wait_send())


def on_device(
    pixels, embed_weight, level_code, depth_kernel, norm_gain, up_weight, up_bias,
    down_weight, down_bias, fold_gain, latents, memory_weight, output_weight,
):
    vmem = pl.BlockSpec(memory_space=pltpu.VMEM)
    hbm = pl.BlockSpec(memory_space=pl.ANY)
    dma = pltpu.SemaphoreType.DMA
    result = pl.pallas_call(
        kernel,
        out_shape=jax.ShapeDtypeStruct((1, 2, NLAT, COLS, WIDTH), BF16),
        in_specs=[hbm] * 13,
        out_specs=vmem,
        scratch_shapes=[
            pltpu.VMEM((80, WIDTH), BF16),
            pltpu.VMEM((4, WIDTH), BF16),
            pltpu.VMEM((1, 25, 2, WIDTH), BF16),
            pltpu.VMEM((1, 2, WIDTH), BF16),
            pltpu.VMEM((1, 2, HIDDEN), BF16),
            pltpu.VMEM((1, 2, WIDTH), BF16),
            pltpu.VMEM((WIDTH,), BF16),
            pltpu.VMEM((NLAT, WIDTH), BF16),
            pltpu.VMEM((8, 5, 8, 128), BF16),
            pltpu.VMEM((NBLOCKS, 32, WIDTH), BF16),
            pltpu.VMEM((32, WIDTH), F32),
            pltpu.VMEM((NBLOCKS, WIDTH, HIDDEN), BF16),
            pltpu.VMEM((NBLOCKS, HIDDEN, WIDTH), BF16),
            pltpu.VMEM((WIDTH, 2 * WIDTH), BF16),
            pltpu.VMEM((WIDTH, WIDTH), BF16),
            pltpu.VMEM((4, PLACES, WIDTH), BF16),
            pltpu.VMEM((2 * NBLOCKS, 64, WIDTH), BF16),
            pltpu.VMEM((2 * NBLOCKS, 64, WIDTH), BF16),
            pltpu.VMEM((2, 8 * (COLS + 4) * 8, 128), F32),
            pltpu.VMEM((200, 128), F32),
            pltpu.VMEM((4 * COLS * 8, 128), F32),
            pltpu.VMEM((PLACES, WIDTH), F32),
            pltpu.VMEM((PLACES, HIDDEN), BF16),
            pltpu.VMEM((4, 128, 40), F32),
            pltpu.VMEM((8, 40, WIDTH), BF16),
            pltpu.VMEM((4, 64, WIDTH), BF16),
            dma((8,)), dma((8,)), dma((3,)), dma((3,)), dma((2, 2)), dma((2, 2)), dma((2, 2)),
            dma((2, 2)), dma((2, 2)), dma((2, 2, 3)), dma((2, 2, 3)), dma((2, 2)), dma((2, 2)),
            dma((2, 2 * NBLOCKS)), dma((2, 2 * NBLOCKS)), dma((4,)), dma((4,)), dma((2,)), dma((8,)),
            dma((2,)), dma((2,)),
        ],
        compiler_params=pltpu.CompilerParams(
            collective_id=0, has_side_effects=True, vmem_limit_bytes=62 * 1024 * 1024
        ),
    )(
        pixels, embed_weight, level_code, jnp.transpose(depth_kernel, (0, 2, 1, 3)),
        norm_gain, up_weight, up_bias, down_weight, down_bias, fold_gain, latents,
        memory_weight, output_weight,
    )
    return jnp.transpose(result, (0, 1, 3, 2, 4))


def solution(mesh):
    return jax.shard_map(
        on_device,
        mesh=mesh,
        in_specs=(
            P(None, None, None, "lat", None),
            P(),
            P(),
            P("segment", None, None, None),
            P("segment", None, None),
            P("segment", None, None, None),
            P("segment", None, None),
            P("segment", None, None, None),
            P("segment", None, None),
            P(),
            P(),
            P(),
            P(),
        ),
        out_specs=P("segment", "lat", None, None, None),
        check_vma=False,
    )
```
